32 devices in a mesh: dp: 8 (over y, x, core), seq: 4 (over z).
Axes of the slice: x: 2, y: 2, z: 4, core: 2. Of those that a mesh axis runs over, the one named last changes fastest.
Arguments:
- tokens: bfloat16 [8192, 1536], P(('dp', 'seq')), may hold values from -6 to 6
- context: bfloat16 [8, 2, 128, 768], P('dp'), may hold values from -6 to 6
- item_lengths: int32 [8, 2], P('dp'), may hold values from 0 to 1024, as said below
- gain_self: bfloat16 [1536], replicated, may hold values from 0.25 to 1.75
- gain_cross: bfloat16 [1536], replicated, may hold values from 0.25 to 1.75
- gain_feed: bfloat16 [1536], replicated, may hold values from 0.25 to 1.75
- self_query: bfloat16 [1536, 1536], P(('dp', 'seq')), may hold values from -0.15625 to 0.15625
- self_key: bfloat16 [1536, 1536], P(('dp', 'seq')), may hold values from -0.15625 to 0.15625
- self_value: bfloat16 [1536, 1536], P(('dp', 'seq')), may hold values from -0.15625 to 0.15625
- self_out: bfloat16 [1536, 1536], P(('dp', 'seq')), may hold values from -3 to 3
- cross_query: bfloat16 [1536, 1536], P(('dp', 'seq')), may hold values from -0.15625 to 0.15625
- cross_key: bfloat16 [768, 1536], P(('dp', 'seq')), may hold values from -0.21875 to 0.21875
- cross_value: bfloat16 [768, 1536], P(('dp', 'seq')), may hold values from -0.21875 to 0.21875
- cross_out: bfloat16 [1536, 1536], P(('dp', 'seq')), may hold values from -1 to 1
- feed_gate: bfloat16 [6144, 1536], P(('dp', 'seq')), may hold values from -0.15625 to 0.15625
- feed_up: bfloat16 [6144, 1536], P(('dp', 'seq')), may hold values from -0.15625 to 0.15625
- feed_down: bfloat16 [6144, 1536], P(('dp', 'seq')), may hold values from -0.078125 to 0.078125
- cotangent: bfloat16 [8192, 1536], P(('dp', 'seq')), may hold values from -6 to 6
Outputs:
- output: bfloat16 [8192, 1536], P(('dp', 'seq'))
- grad_tokens: bfloat16 [8192, 1536], P(('dp', 'seq'))
- grad_gain_self: float32 [1536], P(('dp', 'seq'))
- grad_gain_cross: float32 [1536], P(('dp', 'seq'))
- grad_gain_feed: float32 [1536], P(('dp', 'seq'))
- grad_self_query: float32 [1536, 1536], P(('dp', 'seq'))
- grad_self_key: float32 [1536, 1536], P(('dp', 'seq'))
- grad_self_value: float32 [1536, 1536], P(('dp', 'seq'))
- grad_self_out: float32 [1536, 1536], P(('dp', 'seq'))
- grad_cross_query: float32 [1536, 1536], P(('dp', 'seq'))
- grad_cross_key: float32 [768, 1536], P(('dp', 'seq'))
- grad_cross_value: float32 [768, 1536], P(('dp', 'seq'))
- grad_cross_out: float32 [1536, 1536], P(('dp', 'seq'))
- grad_feed_gate: float32 [6144, 1536], P(('dp', 'seq'))
- grad_feed_up: float32 [6144, 1536], P(('dp', 'seq'))
- grad_feed_down: float32 [6144, 1536], P(('dp', 'seq'))
The draws below stay inside these ranges and needn't reach their ends.
Inputs may be any that keep to these rules, and one draw needn't show every extreme that they name: Each sequence holds either one item (item_lengths[g, 1] = 0) followed by fewer than 256 padding rows, or two items, the first of 448 to 576 rows, the second filling the rest but for fewer than 256 padding rows. Some sequence is one item of all 1024 rows.
All inputs are finite; a program needn't handle non-finite values.
Results may differ from the reference program's by a relative error of at most 0.024.
Values may be sent and summed in bfloat16 or wider, within the bound.
No kernel may reach another device: no remote copies, remote signals or barrier semaphores. Data moves between devices by JAX's collectives and lax.ppermute only.
A program may use at most 448 MiB of HBM per device.

```python
import jax
import jax.numpy as jnp
from jax import lax

D = 1536
HEADS = 24
HDIM = 64
ROT = 32
FF = 6144
CTX_DIM = 768
CTX = 128
LEN = 1024
ROWS_DEV = 256
GROUPS = 8
TOKENS = 8192
BLOCK = 512


def draw_item_lengths(key, part):
    key = jax.random.fold_in(key, 11)
    tail_key, shift_key, pick_key, kind_key = jax.random.split(key, 4)
    group_ids = jnp.arange(GROUPS, dtype=jnp.int32)
    tail_rows = jax.random.randint(tail_key, (GROUPS,), 0, ROWS_DEV)
    chosen = jax.random.randint(pick_key, (), 0, GROUPS)
    paired = jax.random.randint(kind_key, (GROUPS,), 0, 2)
    spread = max(1, LEN // 16)
    shift = jax.random.randint(shift_key, (GROUPS,), -spread, spread + 1)
    single = jnp.logical_or(paired == 0, group_ids == chosen)
    tail_rows = jnp.where(group_ids == chosen, 0, tail_rows)
    half_first = LEN // 2 + shift
    first = jnp.where(single, LEN - tail_rows, half_first)
    second = jnp.where(single, 0, LEN - half_first - tail_rows)
    return jnp.stack([first, second], axis=1).astype(jnp.int32)


def strengthened(values, own_key, source, target, parts, factor):
    owner, partner = [(jnp.arange(values.shape[dim]) // (values.shape[dim] // parts)).reshape([-1 if axis == dim else 1 for axis in range(values.ndim)]) for dim in (source, target)]
    chosen = jax.random.permutation(own_key, parts)[partner]
    strong = (owner == chosen) | (owner == (partner + parts // 2) % parts)
    return jnp.where(strong, factor * values, values)


def level_of(key, shape, pieces, smallest, high):
    def one(dim, blocks):
        heights = jax.random.uniform(jax.random.fold_in(jax.random.fold_in(key, 6), dim), (blocks,), jnp.float32, smallest / len(pieces), high / len(pieces))
        return jnp.repeat(jnp.exp(heights), shape[dim] // blocks).reshape((-1,) + (1,) * (len(shape) - dim - 1))

    gain = one(*pieces[0])
    for cut in pieces[1:]:
        gain = gain * one(*cut)
    return gain


def normal_values(stream_key, dims, scale, limit, cuts=(), kind=jnp.bfloat16):
    array = scale * jax.random.normal(stream_key, dims, jnp.float32)
    if cuts:
        array = array * level_of(stream_key, dims, cuts, -0.22, 0.18)
    return jnp.clip(array, -limit, limit).astype(kind)


def heavy_noise(own_key, dims, width, reach, pieces, heavy, held_as=jnp.bfloat16):
    entries = width * jax.random.normal(own_key, dims, jnp.float32)
    if pieces:
        entries = entries * level_of(own_key, dims, pieces, -0.22, 0.18)
    return jnp.clip(strengthened(entries, jax.random.fold_in(own_key, 3), *heavy), -reach, reach).astype(held_as)


def setup_inputs(seed: int = 0) -> dict:
    key_of = jax.random.split(jax.random.key(seed), 19)
    return {
        "tokens": heavy_noise(key_of[0], (TOKENS, D), 1.0, 6.0, ((0, 32),), (0, 1, 32, 2.75)),
        "context": normal_values(key_of[1], (GROUPS, 2, CTX, CTX_DIM), 1.0, 6.0, ((0, 8),)),
        "item_lengths": draw_item_lengths(jax.random.fold_in(key_of[18], 71), 0),
        "gain_self": jnp.clip(1.0 + 0.15 * jax.random.normal(key_of[3], (D,), jnp.float32), 0.25, 1.75).astype(jnp.bfloat16),
        "gain_cross": jnp.clip(1.0 + 0.15 * jax.random.normal(key_of[4], (D,), jnp.float32), 0.25, 1.75).astype(jnp.bfloat16),
        "gain_feed": jnp.clip(1.0 + 0.15 * jax.random.normal(key_of[5], (D,), jnp.float32), 0.25, 1.75).astype(jnp.bfloat16),
        "self_query": normal_values(key_of[6], (D, D), D ** -0.5, 0.15625, ((0, 32),)),
        "self_key": normal_values(key_of[7], (D, D), D ** -0.5, 0.15625, ((0, 32),)),
        "self_value": normal_values(key_of[8], (D, D), D ** -0.5, 0.15625, ((0, 32),)),
        "self_out": normal_values(key_of[9], (D, D), (max(1, 3 * D // LEN)) ** -0.5, 3.0, ((0, 32),)),
        "cross_query": normal_values(key_of[10], (D, D), D ** -0.5, 0.15625, ((0, 32),)),
        "cross_key": normal_values(key_of[11], (CTX_DIM, D), CTX_DIM ** -0.5, 0.21875, ((0, 32),)),
        "cross_value": normal_values(key_of[12], (CTX_DIM, D), CTX_DIM ** -0.5, 0.21875, ((0, 32),)),
        "cross_out": normal_values(key_of[13], (D, D), (max(1, 3 * D // CTX)) ** -0.5, 1.0, ((0, 32),)),
        "feed_gate": normal_values(key_of[14], (FF, D), D ** -0.5, 0.15625, ((0, 32),)),
        "feed_up": normal_values(key_of[15], (FF, D), D ** -0.5, 0.15625, ((0, 32),)),
        "feed_down": normal_values(key_of[16], (FF, D), FF ** -0.5, 0.078125, ((0, 32),)),
        "cotangent": normal_values(key_of[17], (TOKENS, D), 1.0, 6.0, ((0, 32),)),
    }


EPSILON = 1e-05
NEG_FILL = -1e+30
HIGHEST = lax.Precision.HIGHEST

@jax.custom_vjp
def low(v):
    return lax.optimization_barrier(v.astype(jnp.bfloat16)).astype(jnp.float32)

@jax.custom_vjp
def low_back(v):
    return v

def low_keep(v):
    return (low(v), None)

def low_pass(kept, grad):
    return (grad,)

def back_keep(v):
    return (v, None)

def back_low(kept, grad):
    return (low(grad),)
low.defvjp(low_keep, low_pass)
low_back.defvjp(back_keep, back_low)

def layer_norm(values, gain_vector):
    average = lax.optimization_barrier(jnp.mean(values, axis=-1, keepdims=True))
    centered = values - average
    variance = lax.optimization_barrier(jnp.mean(centered * centered, axis=-1, keepdims=True))
    return centered * lax.rsqrt(variance + EPSILON) * gain_vector

def product(left, right):
    return jnp.dot(left, right, precision=HIGHEST)

def layout(lengths, length):
    row_ids = jnp.arange(length, dtype=jnp.int32)
    first_end = lengths[0].astype(jnp.int32)
    second_end = (lengths[0] + lengths[1]).astype(jnp.int32)
    segment = jnp.where(row_ids < first_end, 0, jnp.where(row_ids < second_end, 1, 2)).astype(jnp.int32)
    seg_start = jnp.where(segment == 0, 0, jnp.where(segment == 1, first_end, second_end)).astype(jnp.int32)
    return (segment, row_ids - seg_start)

def rotary_tables(position):
    half_rot = ROT // 2
    frequency = 10000.0 ** (-jnp.arange(half_rot, dtype=jnp.float32) / half_rot)
    angles = position.astype(jnp.float32)[:, None] * frequency[None, :]
    return (jnp.cos(angles), jnp.sin(angles))

def rotate(values, cosine, sine_table):
    half_rot = ROT // 2
    first_half = values[..., :half_rot]
    second_half = values[..., half_rot:ROT]
    remainder = values[..., ROT:]
    cos_heads = cosine[:, None, :]
    sin_heads = sine_table[:, None, :]
    return jnp.concatenate([first_half * cos_heads - second_half * sin_heads, second_half * cos_heads + first_half * sin_heads, remainder], axis=-1)

def softmax_rows(scores):
    highest = lax.optimization_barrier(jnp.max(scores, axis=-1, keepdims=True))
    raised = jnp.exp(scores - highest)
    return raised / lax.optimization_barrier(jnp.sum(raised, axis=-1, keepdims=True))

def self_attention(queries, key_rows, value_rows, segment):
    scaling = HDIM ** (-0.5)
    block_count = LEN // BLOCK
    query_blocks = queries.reshape(block_count, BLOCK, HEADS, HDIM)
    segment_blocks = segment.reshape(block_count, BLOCK)

    def attend(inputs):
        query_block, query_segment = inputs
        scores = jnp.einsum('qhd,khd->hqk', query_block, key_rows, precision=HIGHEST) * scaling
        scores = jnp.where(query_segment[None, :, None] == segment[None, None, :], scores, NEG_FILL)
        chance = softmax_rows(low_back(scores))
        return jnp.einsum('hqk,khd->qhd', low(chance), value_rows, precision=HIGHEST)
    result = lax.map(jax.checkpoint(attend), (query_blocks, segment_blocks))
    return result.reshape(LEN, HEADS * HDIM)

def cross_attention(queries, key_rows, value_rows, item_index):
    scaling = HDIM ** (-0.5)
    key_item = jnp.arange(2 * CTX, dtype=jnp.int32) // CTX
    scores = jnp.einsum('qhd,khd->hqk', queries, key_rows, precision=HIGHEST) * scaling
    scores = jnp.where(item_index[None, :, None] == key_item[None, None, :], scores, NEG_FILL)
    chance = softmax_rows(low_back(scores))
    return jnp.einsum('hqk,khd->qhd', low(chance), value_rows, precision=HIGHEST).reshape(LEN, D)

def forward(token_values, weights, memory_group, segment, position):
    gain_self, gain_cross, gain_feed, self_query, self_key, self_value, self_out, cross_query, cross_key, cross_value, cross_out, feed_gate, feed_up, feed_down = weights
    cosine, sine_table = rotary_tables(position)
    norm_one = low(layer_norm(token_values, gain_self))
    queries = low(rotate(low_back(product(norm_one, self_query)).reshape(LEN, HEADS, HDIM), cosine, sine_table))
    key_rows = low(rotate(low_back(product(norm_one, self_key)).reshape(LEN, HEADS, HDIM), cosine, sine_table))
    value_rows = low(low_back(product(norm_one, self_value))).reshape(LEN, HEADS, HDIM)
    attended = low(low_back(self_attention(queries, key_rows, value_rows, segment)))
    first_sum = token_values + low_back(product(attended, self_out))
    norm_two = low(layer_norm(first_sum, gain_cross))
    cross_queries = low(low_back(product(norm_two, cross_query))).reshape(LEN, HEADS, HDIM)
    memory = memory_group.reshape(2 * CTX, CTX_DIM)
    memory_keys = low(product(memory, cross_key)).reshape(2 * CTX, HEADS, HDIM)
    memory_values = low(product(memory, cross_value)).reshape(2 * CTX, HEADS, HDIM)
    item_index = jnp.where(segment == 1, 1, 0).astype(jnp.int32)
    cross_mixed = low(low_back(cross_attention(cross_queries, memory_keys, memory_values, item_index)))
    second_sum = first_sum + low_back(product(cross_mixed, cross_out))
    norm_three = low(layer_norm(second_sum, gain_feed))
    gate_proj = low_back(product(norm_three, feed_gate.T))
    up_proj = low_back(product(norm_three, feed_up.T))
    activation = low(jax.nn.silu(gate_proj) * up_proj)
    return second_sum + low_back(product(activation, feed_down))

def reference(tokens, context, item_lengths, gain_self, gain_cross, gain_feed, self_query, self_key, self_value, self_out, cross_query, cross_key, cross_value, cross_out, feed_gate, feed_up, feed_down, cotangent):
    params = tuple((weight_array.astype(jnp.float32) for weight_array in (gain_self, gain_cross, gain_feed, self_query, self_key, self_value, self_out, cross_query, cross_key, cross_value, cross_out, feed_gate, feed_up, feed_down)))
    token_groups = tokens.astype(jnp.float32).reshape(GROUPS, LEN, D)
    cot_groups = cotangent.astype(jnp.float32).reshape(GROUPS, LEN, D)
    context_values = context.astype(jnp.float32)

    def one_group(running, inputs):
        group_tokens, group_context, lengths, group_cot = inputs
        segment, position = layout(lengths, LEN)
        valid_rows = (segment < 2).astype(jnp.float32)[:, None]

        def apply_layer(token_values, weight_values):
            return forward(token_values, weight_values, group_context, segment, position)
        result, pullback = jax.vjp(apply_layer, group_tokens, params)
        grad_input, grad_params = pullback(group_cot * valid_rows)
        running = tuple((total_now + increment for total_now, increment in zip(running, grad_params)))
        return (running, (result.astype(jnp.bfloat16), grad_input.astype(jnp.bfloat16)))
    initial = tuple((jnp.zeros(weight_array.shape, jnp.float32) for weight_array in params))
    totals, (outputs, grads_in) = lax.scan(one_group, initial, (token_groups, context_values, item_lengths, cot_groups))
    return (outputs.reshape(TOKENS, D), grads_in.reshape(TOKENS, D), totals[0], totals[1], totals[2], totals[3], totals[4], totals[5], totals[6], totals[7], totals[8], totals[9], totals[10], totals[11], totals[12], totals[13])
```

```python
import jax
import jax.numpy as jnp
from jax import lax
from jax.experimental import pallas as pl
from jax.experimental.pallas import tpu as pltpu
from jax.sharding import PartitionSpec as P

HEADS = 24
HDIM = 64
ROT = 32


EPSILON = 1e-05
NEG_FILL = -1e30
HIGHEST = lax.Precision.HIGHEST


def layer_norm(values, gain_vector):
    average = jnp.mean(values, axis=-1, keepdims=True)
    centered = values - average
    variance = jnp.mean(centered * centered, axis=-1, keepdims=True)
    return centered * lax.rsqrt(variance + EPSILON) * gain_vector


def layout(lengths, row_ids):
    first_end = lengths[0]
    second_end = lengths[0] + lengths[1]
    segment = jnp.where(row_ids < first_end, 0, jnp.where(row_ids < second_end, 1, 2)).astype(
        jnp.int32
    )
    seg_start = jnp.where(segment == 0, 0, jnp.where(segment == 1, first_end, second_end))
    return (segment, row_ids - seg_start)


def rotary_tables(position):
    half_rot = ROT // 2
    frequency = 10000.0 ** (-jnp.arange(half_rot, dtype=jnp.float32) / half_rot)
    angles = position.astype(jnp.float32)[:, None] * frequency[None, :]
    return (jnp.cos(angles), jnp.sin(angles))


def rotate(values, cosine, sine_table):
    half_rot = ROT // 2
    first_half = values[..., :half_rot]
    second_half = values[..., half_rot:ROT]
    remainder = values[..., ROT:]
    cos_heads = cosine[:, None, :]
    sin_heads = sine_table[:, None, :]
    return jnp.concatenate(
        [
            first_half * cos_heads - second_half * sin_heads,
            second_half * cos_heads + first_half * sin_heads,
            remainder,
        ],
        axis=-1,
    )


def matmul(left, right):
    return jnp.dot(left, right, preferred_element_type=jnp.float32)


def contract_rows(left, right):
    return lax.dot_general(
        left, right, (((0,), (0,)), ((), ())), preferred_element_type=jnp.float32
    )


def contract_cols(left, right):
    return lax.dot_general(
        left, right, (((1,), (1,)), ((), ())), preferred_element_type=jnp.float32
    )


def softmax_rows(scores):
    highest = jnp.max(scores, axis=-1, keepdims=True)
    raised = jnp.exp(scores - highest)
    denominator = jnp.sum(raised, axis=-1, keepdims=True)
    return (raised / denominator, highest + jnp.log(denominator))


def gate_backward(gate_proj, up_proj, grad_activation):
    unused, pullback = jax.vjp(
        lambda gate_in, up_in: jax.nn.silu(gate_in) * up_in, gate_proj, up_proj
    )
    grad_gate, grad_up = pullback(grad_activation)
    return (grad_gate.astype(jnp.bfloat16), grad_up.astype(jnp.bfloat16))


def heads_forward(queries, key_rows, value_rows, segment, block_rows):
    length, heads_dev, head_dim = queries.shape
    scaling = head_dim ** (-0.5)

    def attend(block_index):
        first_row = block_index * block_rows
        query_block = lax.dynamic_slice_in_dim(queries, first_row, block_rows, 0)
        query_segment = lax.dynamic_slice_in_dim(segment, first_row, block_rows, 0)
        scores = (
            jnp.einsum("qhd,khd->hqk", query_block, key_rows, preferred_element_type=jnp.float32)
            * scaling
        )
        scores = jnp.where(query_segment[None, :, None] == segment[None, None, :], scores, NEG_FILL)
        chance, log_total = softmax_rows(scores)
        attended = jnp.einsum(
            "hqk,khd->qhd",
            chance.astype(jnp.bfloat16),
            value_rows,
            preferred_element_type=jnp.float32,
        )
        return (attended, log_total[..., 0])

    attended, log_total = lax.map(attend, jnp.arange(length // block_rows))
    return (attended.reshape(length, heads_dev * head_dim), log_total)


def heads_backward(queries, key_rows, value_rows, grad_out, log_total, segment, block_rows):
    length, heads_dev, head_dim = queries.shape
    scaling = head_dim ** (-0.5)

    def backward_block(carried, block_index):
        grad_keys, grad_values = carried
        first_row = block_index * block_rows
        query_block = lax.dynamic_slice_in_dim(queries, first_row, block_rows, 0)
        grad_block = lax.dynamic_slice_in_dim(grad_out, first_row, block_rows, 0)
        query_segment = lax.dynamic_slice_in_dim(segment, first_row, block_rows, 0)
        scores = (
            jnp.einsum("qhd,khd->hqk", query_block, key_rows, preferred_element_type=jnp.float32)
            * scaling
        )
        scores = jnp.where(query_segment[None, :, None] == segment[None, None, :], scores, NEG_FILL)
        chance = jnp.exp(scores - log_total[block_index][:, :, None])
        grad_chance = jnp.einsum(
            "qhd,khd->hqk", grad_block, value_rows, preferred_element_type=jnp.float32
        )
        row_inner = jnp.sum(chance * grad_chance, axis=-1, keepdims=True)
        grad_scores = (chance * (grad_chance - row_inner)).astype(jnp.bfloat16)
        grad_query = (
            jnp.einsum("hqk,khd->qhd", grad_scores, key_rows, preferred_element_type=jnp.float32)
            * scaling
        )
        grad_keys = (
            grad_keys
            + jnp.einsum(
                "hqk,qhd->khd", grad_scores, query_block, preferred_element_type=jnp.float32
            )
            * scaling
        )
        grad_values = grad_values + jnp.einsum(
            "hqk,qhd->khd",
            chance.astype(jnp.bfloat16),
            grad_block,
            preferred_element_type=jnp.float32,
        )
        return ((grad_keys, grad_values), grad_query)

    initial = jnp.zeros((length, heads_dev, head_dim), jnp.float32)
    (grad_keys, grad_values), grad_query = lax.scan(
        backward_block, (initial, initial), jnp.arange(length // block_rows)
    )
    return (grad_query.reshape(length, heads_dev, head_dim), grad_keys, grad_values)


def swap_core(values):
    return lax.ppermute(values, "dp", [(d, d ^ 1) for d in range(lax.axis_size("dp"))])


def swap_x(values):
    return lax.ppermute(values, "dp", [(d, d ^ 2) for d in range(lax.axis_size("dp"))])


def shift_y(values, step):
    size = lax.axis_size("dp")
    return lax.ppermute(values, "dp", [(d, (d + 4 * step) % size) for d in range(size)])


def shift_seq(values, step):
    size = lax.axis_size("seq")
    return lax.ppermute(values, "seq", [(s, (s + step) % size) for s in range(size)])


def gather_seq(values):
    pieces = [values]
    for _ in range(lax.axis_size("seq") - 1):
        pieces.append(shift_seq(pieces[-1], 1))
    return pieces


def reduce_seq(blocks):
    total = blocks[-1]
    for block in blocks[-2::-1]:
        total = add_low(shift_seq(total, -1), block)
    return total


def add_wide(left, right):
    return left.astype(jnp.float32) + right.astype(jnp.float32)


def add_low(left, right):
    return add_wide(left, right).astype(jnp.bfloat16)


def gather_dp(first, second):
    y_size = lax.axis_size("dp") // 4
    held = {(0, 0, 0, 0): first, (1, 0, 0, 0): second}
    held[0, 0, 0, 1] = swap_x(first)
    for y in range(1, y_size):
        for x in range(2):
            held[0, 0, y, x] = shift_y(held[0, 0, y - 1, x], 1)
    for y in range(1, y_size):
        held[1, 0, y, 0] = shift_y(held[1, 0, y - 1, 0], 1)
    for y in range(y_size):
        held[1, 0, y, 1] = swap_x(held[1, 0, y, 0])
    for half, core, y, x in list(held):
        held[half, 1, y, x] = swap_core(held[half, 0, y, x])
    return held


def pick(values, index, axis):
    if isinstance(index, int):
        return lax.index_in_dim(values, index, axis, keepdims=False)
    return lax.dynamic_index_in_dim(values, index, axis, keepdims=False)


def reduce_dp(first, second, y_place, x_place):
    y_size = first.shape[0]
    total = pick(first, y_place(y_size - 1), 0)
    for y in range(y_size - 2, -1, -1):
        total = add_low(shift_y(total, -1), pick(first, y_place(y), 0))
    first_sum = add_wide(pick(total, x_place(0), 0), swap_x(pick(total, x_place(1), 0)))
    rows = add_low(pick(second, x_place(0), 1), swap_x(pick(second, x_place(1), 1)))
    total = pick(rows, y_place(y_size - 1), 0)
    for y in range(y_size - 2, -1, -1):
        total = add_wide(shift_y(total.astype(jnp.bfloat16), -1), pick(rows, y_place(y), 0))
    return first_sum, total


def assemble(pieces, out_shapes, copies):
    count = len(pieces)

    def body(*refs):
        sources, targets = refs[:count], refs[count : count + len(out_shapes)]
        held, loaded, stored = (
            refs[count + len(out_shapes) : -2],
            refs[-2],
            refs[-1],
        )
        dp_place, seq_place = lax.axis_index("dp"), lax.axis_index("seq")
        loads = [
            pltpu.make_async_copy(sources[n], held[n], loaded.at[n]) for n in range(count)
        ]
        for load in loads:
            load.start()
        stores = []
        for n in range(count):
            loads[n].wait()
            for number, (piece, source, out, target) in enumerate(copies):
                if piece == n:
                    stores.append(
                        pltpu.make_async_copy(
                            held[n].at[source],
                            targets[out].at[target(dp_place, seq_place)],
                            stored.at[number],
                        )
                    )
                    stores[-1].start()
        for store in stores:
            store.wait()

    moved = sum(2 * p.size * p.dtype.itemsize for p in pieces)
    return pl.pallas_call(
        body,
        out_shape=[jax.ShapeDtypeStruct(s, jnp.bfloat16) for s in out_shapes],
        in_specs=[pl.BlockSpec(memory_space=pl.ANY)] * len(pieces),
        out_specs=[pl.BlockSpec(memory_space=pl.ANY)] * len(out_shapes),
        scratch_shapes=[pltpu.VMEM(p.shape, p.dtype) for p in pieces]
        + [pltpu.SemaphoreType.DMA((count,)), pltpu.SemaphoreType.DMA((len(copies),))],
        compiler_params=pltpu.CompilerParams(vmem_limit_bytes=32 << 20),
        cost_estimate=pl.CostEstimate(flops=0, bytes_accessed=moved, transcendentals=0),
    )(*pieces)


def dp_block(core, y, x, dp_place):
    size = lax.axis_size("dp")
    return ((dp_place + size - 4 * y) % size) ^ (core + 2 * x)


def local(
    tokens,
    context,
    item_lengths,
    gain_self,
    gain_cross,
    gain_feed,
    self_query,
    self_key,
    self_value,
    self_out,
    cross_query,
    cross_key,
    cross_value,
    cross_out,
    feed_gate,
    feed_up,
    feed_down,
    cotangent,
):
    rows_dev, width = tokens.shape
    dp_size, seq_size = lax.axis_size("dp"), lax.axis_size("seq")
    dp_place, seq_place = lax.axis_index("dp"), lax.axis_index("seq")
    y_size = dp_size // 4
    y_own, x_own, core_own = dp_place // 4, (dp_place // 2) % 2, dp_place % 2
    length = rows_dev * seq_size
    heads_dev = HEADS // seq_size
    head_width = heads_dev * HDIM
    block_rows = min(512, length)
    scaling = HDIM ** (-0.5)
    part_rows = self_query.shape[0]
    row_ids = jnp.concatenate(
        [
            (seq_place + seq_size - k) % seq_size * rows_dev + jnp.arange(rows_dev, dtype=jnp.int32)
            for k in range(seq_size)
        ]
    )
    segment, position = layout(item_lengths[0], row_ids)
    row_segment = segment[:rows_dev]
    cosine, sine_table = rotary_tables(position)

    def seq_order(values):
        blocks = values.reshape((seq_size, -1) + values.shape[1:])
        return jnp.concatenate(
            [pick(blocks, (seq_place + seq_size - k) % seq_size, 0) for k in range(seq_size)]
        )

    qkv_parts = jnp.stack([self_query, self_key, self_value]).reshape(
        3, part_rows, seq_size, head_width
    )
    qkv_parts = lax.all_to_all(
        qkv_parts.transpose(2, 1, 0, 3), "seq", split_axis=0, concat_axis=0, tiled=True
    ).reshape(seq_size * part_rows, 3 * head_width)
    half_rows = seq_size * part_rows // 2
    held = gather_dp(qkv_parts[:half_rows], qkv_parts[half_rows:])
    places = list(held)
    qkv_cols = assemble(
        [held[p] for p in places],
        [(dp_size, 2, half_rows, 3 * head_width)],
        [
            (n, (), 0, lambda d, s, h=half, p=(core, y, x): (dp_block(*p, d), h))
            for n, (half, core, y, x) in enumerate(places)
        ],
    )[0].reshape(width, 3 * head_width)

    feed_parts = jnp.stack([feed_gate, feed_up, feed_down])
    half_units = feed_parts.shape[1] // 2
    held = gather_dp(feed_parts[:, :half_units], feed_parts[:, half_units:])
    places = [
        (half, core, y, x)
        for core in range(2)
        for half in range(2)
        for y in range(y_size)
        for x in range(2)
    ]
    unit_gate_up = jnp.concatenate(
        [held[p][0] for p in places] + [held[p][1] for p in places], axis=0
    )
    unit_down = jnp.concatenate([held[p][2] for p in places], axis=0)
    units = unit_down.shape[0]

    part_groups = (
        jnp.stack([self_out, cross_query]),
        jnp.stack([cross_out, jnp.concatenate([cross_key, cross_value])]),
    )
    held = gather_dp(*(jnp.stack(gather_seq(group)) for group in part_groups))
    whole = []
    for group in range(2):
        places = [p for p in held if p[0] == group]
        whole += assemble(
            [held[p] for p in places],
            [(dp_size, seq_size, part_rows, width)] * 2,
            [
                (
                    n,
                    (k, weight),
                    weight,
                    lambda d, s, p=p[1:], k=k: (dp_block(*p, d), (s + seq_size - k) % seq_size),
                )
                for n, p in enumerate(places)
                for k in range(seq_size)
                for weight in range(2)
            ],
        )
    full_out, full_cross_query, full_cross_out = (w.reshape(width, width) for w in whole[:3])
    full_cross_kv = whole[3].reshape(dp_size * seq_size, 2, part_rows // 2, width)
    full_cross_key = full_cross_kv[:, 0].reshape(-1, width)
    full_cross_value = full_cross_kv[:, 1].reshape(-1, width)

    token_values = tokens.astype(jnp.float32)
    norm_one, norm_one_back = jax.vjp(layer_norm, token_values, gain_self.astype(jnp.float32))
    norm_one = norm_one.astype(jnp.bfloat16)
    head_shape = (length, heads_dev, HDIM)
    all_norm_one = jnp.concatenate(gather_seq(norm_one))
    projected = matmul(all_norm_one, qkv_cols)
    head_queries = rotate(projected[:, :head_width].reshape(head_shape), cosine, sine_table)
    head_queries = head_queries.astype(jnp.bfloat16)
    head_keys = rotate(
        projected[:, head_width : 2 * head_width].reshape(head_shape), cosine, sine_table
    ).astype(jnp.bfloat16)
    head_values = projected[:, 2 * head_width :].astype(jnp.bfloat16).reshape(head_shape)
    head_attended, log_total = heads_forward(
        head_queries, head_keys, head_values, segment, block_rows
    )
    attended = lax.all_to_all(
        seq_order(head_attended.astype(jnp.bfloat16)), "seq", split_axis=0, concat_axis=1, tiled=True
    )
    first_sum = token_values + matmul(attended, full_out)
    norm_two, norm_two_back = jax.vjp(layer_norm, first_sum, gain_cross.astype(jnp.float32))
    norm_two = norm_two.astype(jnp.bfloat16)
    cross_queries = matmul(norm_two, full_cross_query).astype(jnp.bfloat16)
    memory = context[0].reshape(-1, context.shape[3])
    memory_rows = memory.shape[0]
    memory_keys = matmul(memory, full_cross_key).astype(jnp.bfloat16)
    memory_values = matmul(memory, full_cross_value).astype(jnp.bfloat16)
    item_index = jnp.where(row_segment == 1, 1, 0).astype(jnp.int32)
    key_item = jnp.arange(memory_rows, dtype=jnp.int32) // (memory_rows // 2)
    cross_mask = item_index[None, :, None] == key_item[None, None, :]
    query_heads = cross_queries.reshape(rows_dev, HEADS, HDIM)
    memory_key_heads = memory_keys.reshape(memory_rows, HEADS, HDIM)
    memory_value_heads = memory_values.reshape(memory_rows, HEADS, HDIM)
    cross_scores = (
        jnp.einsum(
            "qhd,khd->hqk", query_heads, memory_key_heads, preferred_element_type=jnp.float32
        )
        * scaling
    )
    cross_scores = jnp.where(cross_mask, cross_scores, NEG_FILL)
    cross_chance = softmax_rows(cross_scores)[0]
    cross_mixed = jnp.einsum(
        "hqk,khd->qhd",
        cross_chance.astype(jnp.bfloat16),
        memory_value_heads,
        preferred_element_type=jnp.float32,
    )
    cross_mixed = cross_mixed.reshape(rows_dev, width).astype(jnp.bfloat16)
    second_sum = first_sum + matmul(cross_mixed, full_cross_out)
    norm_three, norm_three_back = jax.vjp(layer_norm, second_sum, gain_feed.astype(jnp.float32))
    norm_three = norm_three.astype(jnp.bfloat16)
    valid_rows = (row_segment < 2).astype(jnp.float32)[:, None]
    grad_output = cotangent.astype(jnp.float32) * valid_rows
    grad_output_low = grad_output.astype(jnp.bfloat16)
    all_norm = jnp.concatenate(gather_seq(norm_three))
    all_grad = jnp.concatenate(gather_seq(grad_output_low))
    gate_up = contract_cols(all_norm, unit_gate_up)
    gate_proj, up_proj = gate_up[:, :units], gate_up[:, units:]
    activation = (jax.nn.silu(gate_proj) * up_proj).astype(jnp.bfloat16)
    feed_partial = matmul(activation, unit_down).astype(jnp.bfloat16)
    grad_activation = contract_cols(all_grad, unit_down)
    grad_gate_up = jnp.concatenate(gate_backward(gate_proj, up_proj, grad_activation), axis=1)
    norm_partial = matmul(grad_gate_up, unit_gate_up).astype(jnp.bfloat16)

    def seq_blocks(values):
        return [values[k * rows_dev : (k + 1) * rows_dev] for k in range(seq_size)]

    grad_norm_three = reduce_seq(seq_blocks(norm_partial)).astype(jnp.float32)
    feed_result = reduce_seq(seq_blocks(feed_partial)).astype(jnp.float32)
    output = (second_sum + feed_result).astype(jnp.bfloat16)

    def unit_grad(terms):
        terms = terms.astype(jnp.bfloat16).reshape(2, 2, y_size, 2, half_units, width)
        chip = add_low(terms[0], swap_core(terms[1]))
        return jnp.concatenate(reduce_dp(chip[0], chip[1], lambda y: y, lambda x: x))

    grad_feed_down = unit_grad(contract_rows(activation, all_grad))
    grad_feed_gate = unit_grad(contract_rows(grad_gate_up[:, :units], all_norm))
    grad_feed_up = unit_grad(contract_rows(grad_gate_up[:, units:], all_norm))

    def own_blocks(terms):
        terms = terms.astype(jnp.bfloat16).reshape(y_size, 2, 2, 2, -1, terms.shape[1])
        sent = swap_core(pick(terms, 1 - core_own, 2))
        chip = add_low(pick(terms, core_own, 2), sent)
        halves = reduce_dp(
            chip[:, :, 0],
            chip[:, :, 1],
            lambda y: (y_own + y_size - y) % y_size,
            lambda x: x_own if x == 0 else 1 - x_own,
        )
        return jnp.concatenate([h.astype(jnp.bfloat16) for h in halves])

    def own_rows(terms):
        blocks = own_blocks(terms).reshape(seq_size, -1, terms.shape[1])
        return jnp.sum(
            lax.all_to_all(blocks, "seq", split_axis=0, concat_axis=0, tiled=True).astype(
                jnp.float32
            ),
            axis=0,
        )

    grad_second, grad_gain_feed = norm_three_back(grad_norm_three)
    grad_second = grad_second + grad_output
    second_low = grad_second.astype(jnp.bfloat16)
    grad_cross_out = own_rows(contract_rows(cross_mixed, second_low))
    grad_mixed = (
        contract_cols(second_low, full_cross_out)
        .astype(jnp.bfloat16)
        .reshape(rows_dev, HEADS, HDIM)
    )
    grad_chance = jnp.einsum(
        "qhd,khd->hqk", grad_mixed, memory_value_heads, preferred_element_type=jnp.float32
    )
    row_inner = jnp.sum(cross_chance * grad_chance, axis=-1, keepdims=True)
    grad_scores = (cross_chance * (grad_chance - row_inner)).astype(jnp.bfloat16)
    grad_cross_queries = (
        jnp.einsum(
            "hqk,khd->qhd", grad_scores, memory_key_heads, preferred_element_type=jnp.float32
        )
        * scaling
    )
    grad_cross_queries = grad_cross_queries.reshape(rows_dev, width).astype(jnp.bfloat16)
    grad_memory_keys = (
        jnp.einsum("hqk,qhd->khd", grad_scores, query_heads, preferred_element_type=jnp.float32)
        * scaling
    ).reshape(memory_rows, width)
    grad_memory_values = jnp.einsum(
        "hqk,qhd->khd",
        cross_chance.astype(jnp.bfloat16),
        grad_mixed,
        preferred_element_type=jnp.float32,
    ).reshape(memory_rows, width)
    grad_cross_key = own_rows(contract_rows(memory, grad_memory_keys.astype(jnp.bfloat16)))
    grad_cross_value = own_rows(contract_rows(memory, grad_memory_values.astype(jnp.bfloat16)))
    grad_cross_query = own_rows(contract_rows(norm_two, grad_cross_queries))
    grad_norm_two = contract_cols(grad_cross_queries, full_cross_query)
    grad_first, grad_gain_cross = norm_two_back(grad_norm_two)
    grad_first = grad_first + grad_second
    first_low = grad_first.astype(jnp.bfloat16)
    grad_self_out = own_rows(contract_rows(attended, first_low))
    grad_attended = contract_cols(first_low, full_out).astype(jnp.bfloat16)
    head_grad = seq_order(
        lax.all_to_all(grad_attended, "seq", split_axis=1, concat_axis=0, tiled=True)
    ).reshape(head_shape)
    grad_head_queries, grad_head_keys, grad_head_values = heads_backward(
        head_queries, head_keys, head_values, head_grad, log_total, segment, block_rows
    )
    turned = jnp.concatenate(
        [
            rotate(grad_head_queries, cosine, -sine_table).reshape(length, head_width),
            rotate(grad_head_keys, cosine, -sine_table).reshape(length, head_width),
            grad_head_values.reshape(length, head_width),
        ],
        axis=1,
    ).astype(jnp.bfloat16)
    grad_norm_one = reduce_seq(
        seq_blocks(contract_cols(turned, qkv_cols).astype(jnp.bfloat16))
    ).astype(jnp.float32)
    qkv_sums = own_blocks(contract_rows(all_norm_one, turned)).reshape(
        seq_size, part_rows, 3, head_width
    )
    placed = lax.all_to_all(qkv_sums, "seq", split_axis=0, concat_axis=0, tiled=True)
    placed = placed.transpose(2, 1, 0, 3).reshape(3, part_rows, width).astype(jnp.float32)
    grad_tokens_wide, grad_gain_self = norm_one_back(grad_norm_one)
    grad_tokens = (grad_tokens_wide + grad_first).astype(jnp.bfloat16)

    def own_gain(terms):
        terms = terms.reshape(dp_size * seq_size, -1)
        return jnp.sum(
            lax.all_to_all(terms, ("dp", "seq"), split_axis=0, concat_axis=0, tiled=True), axis=0
        )

    later = own_gain(jnp.stack([grad_gain_cross, grad_gain_feed]).reshape(
        2, dp_size * seq_size, -1).transpose(1, 0, 2))
    gain_rows = later.shape[0] // 2
    return (
        output,
        grad_tokens,
        own_gain(grad_gain_self),
        later[:gain_rows],
        later[gain_rows:],
        placed[0],
        placed[1],
        placed[2],
        grad_self_out,
        grad_cross_query,
        grad_cross_key,
        grad_cross_value,
        grad_cross_out,
        grad_feed_gate,
        grad_feed_up,
        grad_feed_down,
    )


def solution(mesh):
    placed = (
        P(("dp", "seq"), None),
        P("dp", None, None, None),
        P("dp", None),
        P(),
        P(),
        P(),
        P(("dp", "seq"), None),
        P(("dp", "seq"), None),
        P(("dp", "seq"), None),
        P(("dp", "seq"), None),
        P(("dp", "seq"), None),
        P(("dp", "seq"), None),
        P(("dp", "seq"), None),
        P(("dp", "seq"), None),
        P(("dp", "seq"), None),
        P(("dp", "seq"), None),
        P(("dp", "seq"), None),
        P(("dp", "seq"), None),
    )
    return jax.shard_map(
        local,
        mesh=mesh,
        in_specs=placed,
        out_specs=(
            P(("dp", "seq"), None),
            P(("dp", "seq"), None),
            P(("dp", "seq")),
            P(("dp", "seq")),
            P(("dp", "seq")),
            P(("dp", "seq"), None),
            P(("dp", "seq"), None),
            P(("dp", "seq"), None),
            P(("dp", "seq"), None),
            P(("dp", "seq"), None),
            P(("dp", "seq"), None),
            P(("dp", "seq"), None),
            P(("dp", "seq"), None),
            P(("dp", "seq"), None),
            P(("dp", "seq"), None),
            P(("dp", "seq"), None),
        ),
        check_vma=False,
    )
```

```python
import jax
import jax.numpy as jnp
from jax import lax
from jax.experimental import pallas as pl
from jax.experimental.pallas import tpu as pltpu
from jax.sharding import PartitionSpec as P

HEADS = 24
HDIM = 64
ROT = 32


EPSILON = 1e-05
NEG_FILL = -1e30


def layer_norm(values, gain_vector):
    average = jnp.mean(values, axis=-1, keepdims=True)
    centered = values - average
    variance = jnp.mean(centered * centered, axis=-1, keepdims=True)
    return centered * lax.rsqrt(variance + EPSILON) * gain_vector


def layout(lengths, row_ids):
    first_end = lengths[0]
    second_end = lengths[0] + lengths[1]
    segment = jnp.where(row_ids < first_end, 0, jnp.where(row_ids < second_end, 1, 2)).astype(
        jnp.int32
    )
    seg_start = jnp.where(segment == 0, 0, jnp.where(segment == 1, first_end, second_end))
    return (segment, row_ids - seg_start)


def matmul(left, right):
    return jnp.dot(left, right, preferred_element_type=jnp.float32)


def contract_rows(left, right):
    return lax.dot_general(
        left, right, (((0,), (0,)), ((), ())), preferred_element_type=jnp.float32
    )


def contract_cols(left, right):
    return lax.dot_general(
        left, right, (((1,), (1,)), ((), ())), preferred_element_type=jnp.float32
    )


LANES = 128
PAIR = LANES // HDIM
LOG2E = 1.4426950408889634


def turn(values, cosine, sine_low, sine_high, sign):
    half_rot = ROT // 2
    ahead = pltpu.roll(values, LANES - half_rot, 1)
    behind = pltpu.roll(values, half_rot, 1)
    return values * cosine + sign * (behind * sine_high - ahead * sine_low)


def dot(left, right, left_dim, right_dim):
    return lax.dot_general(
        left, right, (((left_dim,), (right_dim,)), ((), ())), preferred_element_type=jnp.float32
    )


def lane_tables(position):
    half_rot = ROT // 2
    feature = jnp.arange(LANES, dtype=jnp.int32) % HDIM
    frequency = 10000.0 ** (-(feature % half_rot).astype(jnp.float32) / half_rot)
    angles = position.astype(jnp.float32)[:, None] * frequency[None, :]
    cosine = jnp.where(feature < ROT, jnp.cos(angles), 1.0)
    sine = jnp.sin(angles)
    return (
        cosine,
        jnp.where(feature < half_rot, sine, 0.0),
        jnp.where((feature >= half_rot) & (feature < ROT), sine, 0.0),
    )


def seq_distance_order(block, seq_size):
    place = lax.axis_index("seq")
    return lax.rem(place + (seq_size - block), seq_size)


def part(kind, head):
    return slice(kind * LANES + head * HDIM, kind * LANES + (head + 1) * HDIM)


def self_forward(norms, qkv_cols, tables, segment):
    seq_size, (block, width) = len(norms), norms[0].shape
    length = block * seq_size
    group = 3 * LANES
    pairs = qkv_cols.shape[1] // group
    scale = HDIM ** (-0.5) * LOG2E

    def body(*refs):
        norm_refs = refs[:seq_size]
        cols_ref, cos_ref, low_ref, high_ref, seg_col, seg_row, qkv_out, mixed_ref, total_ref = refs[
            seq_size:
        ]
        for number in range(seq_size):
            rows = slice(number * block, (number + 1) * block)
            tables = cos_ref[rows], low_ref[rows], high_ref[rows]
            projected = dot(norm_refs[number][...], cols_ref[...], 1, 0)
            for kind in range(3):
                cols = slice(kind * LANES, (kind + 1) * LANES)
                values = projected[:, cols]
                if kind < 2:
                    values = turn(values, *tables, 1.0)
                qkv_out[rows, cols] = values.astype(jnp.bfloat16)
        for number in range(seq_size):
            rows = slice(number * block, (number + 1) * block)
            same = seg_col[...] == seg_row[:, rows]
            mixed = []
            for head in range(PAIR):
                scores = dot(qkv_out[:, part(1, head)], qkv_out[rows, part(0, head)], 1, 1)
                scores = jnp.where(same, scores, NEG_FILL)
                highest = jnp.max(scores, axis=0, keepdims=True)
                raised = jnp.exp2((scores - highest) * scale)
                total = jnp.sum(raised, axis=0, keepdims=True)
                mixed.append(dot(qkv_out[:, part(2, head)], raised.astype(jnp.bfloat16), 0, 0) / total)
                total_ref[0, head : head + 1, rows] = highest * scale + jnp.log2(total)
            place = seq_distance_order(number, seq_size)
            target = pl.ds(pl.multiple_of(place * block, block), block)
            mixed_ref[target, :] = jnp.concatenate(mixed).T.astype(jnp.bfloat16)

    whole = pl.BlockSpec((length, LANES), lambda p: (0, 0))
    return pl.pallas_call(
        body,
        grid=(pairs,),
        in_specs=[pl.BlockSpec((block, width), lambda p: (0, 0))] * seq_size
        + [pl.BlockSpec((width, group), lambda p: (0, p))]
        + [whole] * 3
        + [
            pl.BlockSpec((length, 1), lambda p: (0, 0)),
            pl.BlockSpec((1, length), lambda p: (0, 0)),
        ],
        out_specs=[
            pl.BlockSpec((length, group), lambda p: (0, p)),
            pl.BlockSpec((length, LANES), lambda p: (0, p)),
            pl.BlockSpec((1, PAIR, length), lambda p: (p, 0, 0)),
        ],
        out_shape=[
            jax.ShapeDtypeStruct((length, pairs * group), jnp.bfloat16),
            jax.ShapeDtypeStruct((length, pairs * LANES), jnp.bfloat16),
            jax.ShapeDtypeStruct((pairs, PAIR, length), jnp.float32),
        ],
        compiler_params=pltpu.CompilerParams(vmem_limit_bytes=40 << 20),
        cost_estimate=pl.CostEstimate(
            flops=8 * pairs * PAIR * length * length * HDIM,
            bytes_accessed=2 * (length + group * pairs) * width,
            transcendentals=pairs * PAIR * length * length,
        ),
    )(*norms, qkv_cols, *tables, segment[:, None], segment[None, :])


def self_backward(qkv, grad_out, log_total, tables, segment, seq_size):
    length = qkv.shape[0]
    group = 3 * LANES
    pairs = qkv.shape[1] // group
    block = length // seq_size
    scaling = HDIM ** (-0.5)
    scale = scaling * LOG2E

    def body(qkv_ref, grad_ref, total_ref, *rest):
        cos_ref, low_ref, high_ref, seg_col, seg_row, out_ref, dk_sum, dv_sum = rest
        for number in range(seq_size):
            rows = slice(number * block, (number + 1) * block)
            same = seg_col[...] == seg_row[:, rows]
            place = seq_distance_order(number, seq_size)
            grads = grad_ref[pl.ds(pl.multiple_of(place * block, block), block), :]
            grad_queries = []
            for head in range(PAIR):
                cols = slice(head * HDIM, (head + 1) * HDIM)
                grad_head = grads[:, cols]
                query_head = qkv_ref[rows, part(0, head)]
                key_head = qkv_ref[:, part(1, head)]
                scores = dot(key_head, query_head, 1, 1) * scale - total_ref[
                    0, head : head + 1, rows
                ]
                chance = jnp.exp2(jnp.where(same, scores, NEG_FILL))
                grad_chance = dot(qkv_ref[:, part(2, head)], grad_head, 1, 1)
                inner = jnp.sum(chance * grad_chance, axis=0, keepdims=True)
                grad_scores = (chance * (grad_chance - inner)).astype(jnp.bfloat16)
                grad_queries.append(dot(key_head, grad_scores, 0, 0))
                grad_keys = dot(grad_scores, query_head, 1, 0)
                grad_values = dot(chance.astype(jnp.bfloat16), grad_head, 1, 0)
                if number == 0:
                    dk_sum[:, cols] = grad_keys
                    dv_sum[:, cols] = grad_values
                else:
                    dk_sum[:, cols] += grad_keys
                    dv_sum[:, cols] += grad_values
            tables = cos_ref[rows], low_ref[rows], high_ref[rows]
            turned = turn(jnp.concatenate(grad_queries).T * scaling, *tables, -1.0)
            out_ref[rows, :LANES] = turned.astype(jnp.bfloat16)
        tables = cos_ref[...], low_ref[...], high_ref[...]
        turned = turn(dk_sum[...] * scaling, *tables, -1.0)
        out_ref[:, LANES : 2 * LANES] = turned.astype(jnp.bfloat16)
        out_ref[:, 2 * LANES :] = dv_sum[...].astype(jnp.bfloat16)

    whole = pl.BlockSpec((length, LANES), lambda p: (0, 0))
    return pl.pallas_call(
        body,
        grid=(pairs,),
        in_specs=[
            pl.BlockSpec((length, group), lambda p: (0, p)),
            pl.BlockSpec((length, LANES), lambda p: (0, p)),
            pl.BlockSpec((1, PAIR, length), lambda p: (p, 0, 0)),
        ]
        + [whole] * 3
        + [
            pl.BlockSpec((length, 1), lambda p: (0, 0)),
            pl.BlockSpec((1, length), lambda p: (0, 0)),
        ],
        out_specs=pl.BlockSpec((length, group), lambda p: (0, p)),
        out_shape=jax.ShapeDtypeStruct(qkv.shape, jnp.bfloat16),
        scratch_shapes=[pltpu.VMEM((length, LANES), jnp.float32)] * 2,
        compiler_params=pltpu.CompilerParams(vmem_limit_bytes=40 << 20),
        cost_estimate=pl.CostEstimate(
            flops=20 * pairs * PAIR * length * length * HDIM,
            bytes_accessed=20 * grad_out.size,
            transcendentals=pairs * PAIR * length * length,
        ),
    )(qkv, grad_out, log_total, *tables, segment[:, None], segment[None, :])


CROSS_HEADS = 8


def cross_softmax(queries, key_rows, item_row):
    scale = HDIM ** (-0.5) * LOG2E
    scores = dot(key_rows, queries, 1, 1)
    count = key_rows.shape[0]
    key_item = (lax.broadcasted_iota(jnp.int32, (count, 1), 0) >= count // 2).astype(jnp.int32)
    scores = jnp.where(key_item == item_row, scores, NEG_FILL)
    raised = jnp.exp2((scores - jnp.max(scores, axis=0, keepdims=True)) * scale)
    return raised / jnp.sum(raised, axis=0, keepdims=True)


def cross_call(body, arrays, item_row, out_rows, flops):
    width = arrays[0].shape[1]
    lanes = CROSS_HEADS * HDIM
    blocks = [pl.BlockSpec((a.shape[0], lanes), lambda p: (0, p)) for a in arrays]
    return pl.pallas_call(
        body,
        grid=(width // lanes,),
        in_specs=blocks + [pl.BlockSpec(item_row.shape, lambda p: (0, 0))],
        out_specs=[pl.BlockSpec((rows, lanes), lambda p: (0, p)) for rows in out_rows],
        out_shape=[jax.ShapeDtypeStruct((rows, width), jnp.bfloat16) for rows in out_rows],
        compiler_params=pltpu.CompilerParams(vmem_limit_bytes=32 << 20),
        cost_estimate=pl.CostEstimate(
            flops=flops * width * arrays[0].shape[0] * arrays[1].shape[0],
            bytes_accessed=2 * sum(a.size for a in arrays),
            transcendentals=HEADS * arrays[0].shape[0] * arrays[1].shape[0],
        ),
    )(*arrays, item_row)


def cross_forward(queries, key_rows, value_rows, item_row):
    def body(q_ref, k_ref, v_ref, item_ref, mixed_ref):
        mixed = []
        for head in range(CROSS_HEADS):
            cols = slice(head * HDIM, (head + 1) * HDIM)
            chance = cross_softmax(q_ref[:, cols], k_ref[:, cols], item_ref[...])
            mixed.append(dot(v_ref[:, cols], chance.astype(jnp.bfloat16), 0, 0))
        mixed_ref[...] = jnp.concatenate(mixed).T.astype(jnp.bfloat16)

    return cross_call(
        body, (queries, key_rows, value_rows), item_row, [queries.shape[0]], 4
    )[0]


def cross_backward(queries, key_rows, value_rows, grad_mixed, item_row):
    scaling = HDIM ** (-0.5)

    def body(q_ref, k_ref, v_ref, grad_ref, item_ref, dq_ref, dk_ref, dv_ref):
        grad_queries = []
        for head in range(CROSS_HEADS):
            cols = slice(head * HDIM, (head + 1) * HDIM)
            query_head, key_head, grad_head = q_ref[:, cols], k_ref[:, cols], grad_ref[:, cols]
            chance = cross_softmax(query_head, key_head, item_ref[...])
            grad_chance = dot(v_ref[:, cols], grad_head, 1, 1)
            inner = jnp.sum(chance * grad_chance, axis=0, keepdims=True)
            grad_scores = (chance * (grad_chance - inner)).astype(jnp.bfloat16)
            grad_queries.append(dot(key_head, grad_scores, 0, 0))
            dk_ref[:, cols] = (dot(grad_scores, query_head, 1, 0) * scaling).astype(jnp.bfloat16)
            dv_ref[:, cols] = dot(chance.astype(jnp.bfloat16), grad_head, 1, 0).astype(
                jnp.bfloat16
            )
        dq_ref[...] = (jnp.concatenate(grad_queries).T * scaling).astype(jnp.bfloat16)

    rows, keys = queries.shape[0], key_rows.shape[0]
    return cross_call(
        body, (queries, key_rows, value_rows, grad_mixed), item_row, [rows, keys, keys], 10
    )


def feed_block(normed, grads, gate_up, down, number, count, held):
    rows, width = normed.shape
    units = down.shape[0]
    steps = 3
    tile = units // steps

    def body(x_ref, g_ref, gate_ref, up_ref, down_ref, *rest):
        act_ref, dgate_ref, dup_ref, out_ref, dx_ref, out_sum, dx_sum = rest[-7:]
        step = pl.program_id(0)
        values, grad_rows = x_ref[...], g_ref[...]
        gate = dot(values, gate_ref[...], 1, 1)
        up = dot(values, up_ref[...], 1, 1)
        grad_act = dot(grad_rows, down_ref[...], 1, 1)
        chance = jax.nn.sigmoid(gate)
        silu = gate * chance
        act = (silu * up).astype(jnp.bfloat16)
        grad_gate = (grad_act * up * (chance + silu * (1.0 - chance))).astype(jnp.bfloat16)
        grad_up = (grad_act * silu).astype(jnp.bfloat16)
        act_ref[...] = act
        dgate_ref[...] = grad_gate
        dup_ref[...] = grad_up
        out_part = dot(act, down_ref[...], 1, 0)
        dx_part = dot(grad_gate, gate_ref[...], 1, 0) + dot(grad_up, up_ref[...], 1, 0)

        @pl.when(step == 0)
        def _():
            out_sum[...] = out_part
            dx_sum[...] = dx_part

        @pl.when(step > 0)
        def _():
            out_sum[...] += out_part
            dx_sum[...] += dx_part

        @pl.when(step == steps - 1)
        def _():
            out_ref[...] = out_sum[...].astype(jnp.bfloat16)
            dx_ref[...] = dx_sum[...].astype(jnp.bfloat16)

    full = pl.BlockSpec((rows, width), lambda t: (0, 0))
    block = pl.BlockSpec((rows, tile), lambda t: (number, t))
    unit_shape = jax.ShapeDtypeStruct((rows * count, units), jnp.bfloat16)
    row_shape = jax.ShapeDtypeStruct((rows, width), jnp.bfloat16)
    held = [] if held is None else list(held)
    return pl.pallas_call(
        body,
        grid=(steps,),
        in_specs=[
            full,
            full,
            pl.BlockSpec((tile, width), lambda t: (t, 0)),
            pl.BlockSpec((tile, width), lambda t: (steps + t, 0)),
            pl.BlockSpec((tile, width), lambda t: (t, 0)),
        ]
        + [pl.BlockSpec(memory_space=pl.ANY)] * len(held),
        out_specs=[block] * 3 + [full] * 2,
        out_shape=[unit_shape] * 3 + [row_shape] * 2,
        scratch_shapes=[pltpu.VMEM((rows, width), jnp.float32)] * 2,
        input_output_aliases={5 + n: n for n in range(len(held))},
        compiler_params=pltpu.CompilerParams(vmem_limit_bytes=40 << 20),
        cost_estimate=pl.CostEstimate(
            flops=12 * rows * width * units,
            bytes_accessed=6 * units * width + 10 * rows * width,
            transcendentals=rows * units,
        ),
    )(normed, grads, gate_up, gate_up, down, *held)


def unit_products(units, norms, grads, core, arrived=None):
    seq_size, (block, width) = len(norms), norms[0].shape
    length, count = units[0].shape
    steps = 3
    tile = count // (2 * steps)

    def body(*refs):
        unit_refs, refs = refs[:3], refs[3:]
        norm_refs, grad_refs, refs = refs[:seq_size], refs[seq_size : 2 * seq_size], refs[2 * seq_size :]
        out_ref, all_norms, all_grads = refs[-3:]

        @pl.when(pl.program_id(0) == 0)
        def _():
            for k in range(seq_size):
                rows = slice(k * block, (k + 1) * block)
                all_norms[rows, :] = norm_refs[k][...]
                all_grads[rows, :] = grad_refs[k][...]

        for kind in range(3):
            rows = (all_grads if kind == 2 else all_norms)[...]
            total = dot(unit_refs[kind][...], rows, 0, 0)
            if arrived is not None:
                total += refs[0][kind].astype(jnp.float32)
            out_ref[kind] = total.astype(jnp.bfloat16)

    out_block = pl.BlockSpec((3, tile, width), lambda t: (0, t, 0))
    extra = [] if arrived is None else [arrived]
    return pl.pallas_call(
        body,
        grid=(steps,),
        in_specs=[pl.BlockSpec((length, tile), lambda t: (0, core * steps + t))] * 3
        + [pl.BlockSpec((block, width), lambda t: (0, 0))] * (2 * seq_size)
        + [out_block] * len(extra),
        out_specs=out_block,
        out_shape=jax.ShapeDtypeStruct((3, count // 2, width), jnp.bfloat16),
        scratch_shapes=[pltpu.VMEM((length, width), jnp.bfloat16)] * 2,
        compiler_params=pltpu.CompilerParams(vmem_limit_bytes=56 << 20),
        cost_estimate=pl.CostEstimate(
            flops=3 * length * width * count,
            bytes_accessed=4 * length * width + 6 * count * width,
            transcendentals=0,
        ),
    )(*units, *norms, *grads, *extra)


def weight_products(lefts, rights, slot=0, slots=1, held=None):
    dp_size = lax.axis_size("dp")
    y_size = dp_size // 4
    rows, height = lefts[0].shape
    columns = rights[0].shape[1]
    tile = 3 * LANES
    place_rows = height // dp_size
    half_rows = place_rows * len(rights) // 2
    per_step = tile // place_rows

    def body(*refs):
        left_refs, refs = refs[: len(lefts)], refs[len(lefts) :]
        right_refs, (own_ref, other_ref, product) = refs[: len(rights)], refs[-3:]
        dp_place = lax.axis_index("dp")
        step = pl.program_id(0)
        for number, right_ref in enumerate(right_refs):
            total = None
            for k, left_ref in enumerate(left_refs):
                term = dot(left_ref[...], right_ref[k * rows : (k + 1) * rows, :], 0, 0)
                total = term if total is None else total + term
            product[...] = total.astype(jnp.bfloat16)
            for chip in range(per_step // 2):
                chip_place = step * (per_step // 2) + chip
                y_back = lax.rem((dp_place >> 2) + y_size - (chip_place >> 1), y_size)
                x_back = ((dp_place >> 1) ^ chip_place) & 1
                for target, core in ((own_ref, dp_place & 1), (other_ref, 1 - (dp_place & 1))):
                    first_row = (2 * chip + core) * place_rows
                    for half in range(2 // len(rights)):
                        begin = pl.multiple_of(first_row + half * half_rows, 16)
                        target[0, number + half, y_back, x_back] = product[
                            pl.ds(begin, half_rows), :
                        ]

    whole = (1, 2, y_size, 2, half_rows, columns)
    out_block = pl.BlockSpec(whole, lambda t: (slot, 0, 0, 0, 0, 0))
    out_shape = jax.ShapeDtypeStruct((slots,) + whole[1:], jnp.bfloat16)
    held = [] if held is None else list(held)
    return pl.pallas_call(
        body,
        grid=(height // tile,),
        in_specs=[pl.BlockSpec((rows, tile), lambda t: (0, t))] * len(lefts)
        + [pl.BlockSpec(r.shape, lambda t: (0, 0)) for r in rights]
        + [pl.BlockSpec(memory_space=pl.ANY)] * len(held),
        out_specs=[out_block] * 2,
        out_shape=[out_shape] * 2,
        scratch_shapes=[pltpu.VMEM((tile, columns), jnp.bfloat16)],
        input_output_aliases={len(lefts) + len(rights) + n: n for n in range(len(held))},
        compiler_params=pltpu.CompilerParams(vmem_limit_bytes=40 << 20),
        cost_estimate=pl.CostEstimate(
            flops=2 * rows * len(lefts) * height * columns * len(rights),
            bytes_accessed=4 * height * columns * len(rights),
            transcendentals=0,
        ),
    )(*lefts, *rights, *held)


def swap_core(values):
    return lax.ppermute(values, "dp", [(d, d ^ 1) for d in range(lax.axis_size("dp"))])


def shift_dp(values, y, x):
    size = lax.axis_size("dp")
    return lax.ppermute(values, "dp", [(d, ((d + 4 * y) % size) ^ (2 * x)) for d in range(size)])


def shift_seq(values, step=1):
    size = lax.axis_size("seq")
    return lax.ppermute(values, "seq", [(s, (s + step) % size) for s in range(size)])


def swap_seq(values):
    return lax.all_to_all(values, "seq", split_axis=0, concat_axis=0, tiled=True)


def gather_places(values):
    size = lax.axis_size("seq")
    return swap_seq(jnp.broadcast_to(values[None], (size,) + values.shape))


def add_wide(left, right):
    return left.astype(jnp.float32) + right.astype(jnp.float32)


def add_low(left, right):
    return add_wide(left, right).astype(jnp.bfloat16)


def stage(*values):
    return lax.optimization_barrier(values)


def spread_first(first, second):
    held = {(0, 0, 0): first, (1, 0, 0): second, (0, 0, 1): shift_dp(first, 0, 1)}
    for y in range(1, lax.axis_size("dp") // 4):
        held[1, y, 0] = shift_dp(held[1, y - 1, 0], 1, 0)
    return held


def spread_second(held):
    held = dict(held)
    for half, y, x in [(h, y, 0) for h, y, _ in held if h == 1]:
        held[half, y, 1] = shift_dp(held[half, y, x], 0, 1)
    for x in range(2):
        for y in range(1, lax.axis_size("dp") // 4):
            held[0, y, x] = shift_dp(held[0, y - 1, x], 1, 0)
    return held


def with_cores(plane):
    return {(core,) + p: swap_core(v) if core else v for core in range(2) for p, v in plane.items()}


def reduce_first(own, arrived=None):
    def terms(*index):
        index = (slice(None),) + index
        values = own[index].astype(jnp.float32)
        return values if arrived is None else values + arrived[index].astype(jnp.float32)

    y_size = own.shape[2]
    total = terms(0, y_size - 1).astype(jnp.bfloat16)
    for y in range(y_size - 2, -1, -1):
        total = (shift_dp(total, -1, 0).astype(jnp.float32) + terms(0, y)).astype(jnp.bfloat16)
    sent = shift_dp(terms(1, slice(None), 1).astype(jnp.bfloat16), 0, 1).astype(jnp.float32)
    return total, (sent + terms(1, slice(None), 0)).astype(jnp.bfloat16)


def reduce_second(first, second):
    first = add_wide(first[:, 0], shift_dp(first[:, 1], 0, 1))
    total = second[:, -1]
    for y in range(second.shape[1] - 2, -1, -1):
        total = add_wide(shift_dp(total.astype(jnp.bfloat16), -1, 0), second[:, y])
    return first, total


def dp_block(core, y, x, dp_place):
    size = lax.axis_size("dp")
    return lax.rem(dp_place + (size - 4 * y), size) ^ (core + 2 * x)


def assemble(pieces, out_shapes, copies):
    count = len(pieces)

    def body(*refs):
        sources, targets = refs[:count], refs[count : count + len(out_shapes)]
        held, loaded, stored = refs[count + len(out_shapes) : -2], refs[-2], refs[-1]
        dp_place = lax.axis_index("dp")
        loads = [pltpu.make_async_copy(sources[n], held[n], loaded.at[n]) for n in range(count)]
        for load in loads:
            load.start()
        stores = []
        for n in range(count):
            loads[n].wait()
            for number, (piece, source, out, target) in enumerate(copies):
                if piece == n:
                    stores.append(
                        pltpu.make_async_copy(
                            held[n].at[source],
                            targets[out].at[target(dp_place)],
                            stored.at[number],
                        )
                    )
                    stores[-1].start()
        for store in stores:
            store.wait()

    moved = sum(2 * p.size * p.dtype.itemsize for p in pieces)
    return pl.pallas_call(
        body,
        out_shape=[jax.ShapeDtypeStruct(s, jnp.bfloat16) for s in out_shapes],
        in_specs=[pl.BlockSpec(memory_space=pl.ANY)] * count,
        out_specs=[pl.BlockSpec(memory_space=pl.ANY)] * len(out_shapes),
        scratch_shapes=[pltpu.VMEM(p.shape, p.dtype) for p in pieces]
        + [pltpu.SemaphoreType.DMA((count,)), pltpu.SemaphoreType.DMA((len(copies),))],
        compiler_params=pltpu.CompilerParams(vmem_limit_bytes=32 << 20),
        cost_estimate=pl.CostEstimate(flops=0, bytes_accessed=moved, transcendentals=0),
    )(*pieces)


def in_place(plane):
    held = with_cores(plane)
    places = list(held)
    return assemble(
        [held[p] for p in places],
        [(lax.axis_size("dp"), 2) + held[places[0]].shape],
        [
            (n, (), 0, lambda d, p=p: (dp_block(p[0], p[2], p[3], d), p[1]))
            for n, p in enumerate(places)
        ],
    )[0]


def halves(values):
    middle = values.shape[0] // 2
    return values[:middle], values[middle:]


def local(
    tokens,
    context,
    item_lengths,
    gain_self,
    gain_cross,
    gain_feed,
    self_query,
    self_key,
    self_value,
    self_out,
    cross_query,
    cross_key,
    cross_value,
    cross_out,
    feed_gate,
    feed_up,
    feed_down,
    cotangent,
):
    rows_dev, width = tokens.shape
    dp_size, seq_size = lax.axis_size("dp"), lax.axis_size("seq")
    seq_place = lax.axis_index("seq")
    y_size = dp_size // 4
    head_width = HEADS // seq_size * HDIM
    pairs = -(-head_width // LANES)
    part_rows = self_query.shape[0]

    def whole_rows(rows):
        return lax.all_gather(rows, "dp", axis=0, tiled=False).reshape(width, width)

    qkv_parts = jnp.stack([self_query, self_key, self_value]).reshape(
        3, part_rows, seq_size, head_width
    )
    qkv_parts = jnp.pad(qkv_parts, ((0, 0),) * 3 + ((0, pairs * LANES - head_width),))
    qkv_parts = qkv_parts.reshape(3, part_rows, seq_size, pairs, LANES).transpose(2, 1, 3, 0, 4)
    qkv_rows = swap_seq(qkv_parts.reshape(seq_size, part_rows, pairs * 3 * LANES))
    full_cross_kv = lax.all_gather(
        jnp.stack([cross_key, cross_value]), ("dp", "seq"), axis=0, tiled=False
    )
    token_values = tokens.astype(jnp.float32)
    norm_one, norm_one_back = jax.vjp(layer_norm, token_values, gain_self.astype(jnp.float32))
    norm_one = norm_one.astype(jnp.bfloat16)
    norms_one = [norm_one, shift_seq(norm_one)]
    feed_parts = jnp.stack([feed_gate, feed_up, feed_down])
    half_units = feed_parts.shape[1] // 2
    feed_held = spread_first(feed_parts[:, :half_units], feed_parts[:, half_units:])
    row_ids = jnp.concatenate(
        [
            lax.rem(seq_place + (seq_size - k), seq_size) * rows_dev
            + jnp.arange(rows_dev, dtype=jnp.int32)
            for k in range(seq_size)
        ]
    )
    segment, position = layout(item_lengths[0], row_ids)
    row_segment = segment[:rows_dev]
    tables = lane_tables(position)
    valid_rows = (row_segment < 2).astype(jnp.float32)[:, None]
    grad_output_low = (cotangent.astype(jnp.float32) * valid_rows).astype(jnp.bfloat16)
    qkv_rows, norms_one[1], feed_held, tables, grad_output_low, self_out, cross_query, cross_out = (
        stage(
            qkv_rows,
            norms_one[1],
            feed_held,
            tables,
            grad_output_low,
            self_out,
            cross_query,
            cross_out,
        )
    )

    qkv_plane = spread_second(spread_first(*halves(qkv_rows)))
    norms_one.append(shift_seq(norms_one[-1]))
    out_rows = gather_places(self_out)
    qkv_plane, norms_one, out_rows, feed_held, cross_query, cross_out = stage(
        qkv_plane, norms_one, out_rows, feed_held, cross_query, cross_out
    )
    full_out = whole_rows(out_rows)

    for _ in range(seq_size - 3):
        norms_one.append(shift_seq(norms_one[-1]))
    cross_query_rows = gather_places(cross_query)
    for y in range(1, y_size):
        feed_held[0, y, 0] = shift_dp(feed_held[0, y - 1, 0], 1, 0)
    feed_held[1, 0, 1] = shift_dp(feed_held[1, 0, 0], 0, 1)
    qkv_cols = in_place(qkv_plane).reshape(width, pairs * 3 * LANES)
    norms_one, cross_query_rows, qkv_cols, feed_held, cross_out = stage(
        norms_one, cross_query_rows, qkv_cols, feed_held, cross_out
    )
    full_cross_query = whole_rows(cross_query_rows)

    cross_out_rows = gather_places(cross_out)
    for y in range(1, y_size):
        feed_held[0, y, 1] = shift_dp(feed_held[0, y - 1, 1], 1, 0)
        feed_held[1, y, 1] = shift_dp(feed_held[1, y, 0], 0, 1)
    qkv, head_attended, log_total = self_forward(norms_one, qkv_cols, tables, segment)
    cross_out_rows, feed_held, head_attended = stage(cross_out_rows, feed_held, head_attended)
    full_cross_out = whole_rows(cross_out_rows)

    attended = swap_seq(head_attended[:, :head_width].reshape(seq_size, rows_dev, head_width))
    feed_cores = with_cores(feed_held)
    places = [
        (core, half, y, x)
        for core in range(2)
        for half in range(2)
        for y in range(y_size)
        for x in range(2)
    ]
    unit_gate_up = jnp.concatenate(
        [feed_cores[p][kind] for kind in range(2) for p in places], axis=0
    )
    unit_down = jnp.concatenate([feed_cores[p][2] for p in places], axis=0)
    attended, unit_gate_up, unit_down, grad_output_low = stage(
        attended, unit_gate_up, unit_down, grad_output_low
    )

    all_grads = [grad_output_low, shift_seq(grad_output_low)]
    attended = jnp.concatenate([attended[s] for s in range(seq_size)], axis=1)
    first_sum = token_values + matmul(attended, full_out)
    norm_two, norm_two_back = jax.vjp(layer_norm, first_sum, gain_cross.astype(jnp.float32))
    norm_two = norm_two.astype(jnp.bfloat16)
    cross_queries = matmul(norm_two, full_cross_query).astype(jnp.bfloat16)
    all_grads, cross_queries = stage(all_grads, cross_queries)

    all_grads.append(shift_seq(all_grads[-1]))
    memory = context[0].reshape(-1, context.shape[3])
    full_cross_key = full_cross_kv[:, 0].reshape(-1, width)
    full_cross_value = full_cross_kv[:, 1].reshape(-1, width)
    memory_keys = matmul(memory, full_cross_key).astype(jnp.bfloat16)
    memory_values = matmul(memory, full_cross_value).astype(jnp.bfloat16)
    item_row = (row_segment == 1).astype(jnp.int32)[None, :]
    cross_mixed = cross_forward(cross_queries, memory_keys, memory_values, item_row)
    second_sum = first_sum + matmul(cross_mixed, full_cross_out)
    norm_three, norm_three_back = jax.vjp(layer_norm, second_sum, gain_feed.astype(jnp.float32))
    norm_three = norm_three.astype(jnp.bfloat16)
    all_grads, norm_three = stage(all_grads, norm_three)

    norms = [norm_three, shift_seq(norm_three)]
    for _ in range(seq_size - 3):
        all_grads.append(shift_seq(all_grads[-1]))
    norms, all_grads = stage(norms, all_grads)

    held, feed_out, feed_dx, moving, feed_moving = None, {}, {}, None, None

    def run_block(k, held):
        *held, feed_out[k], feed_dx[k] = feed_block(
            norms[k], all_grads[k], unit_gate_up, unit_down, k, seq_size, held
        )
        return held

    for k in range(1, seq_size):
        if k + 1 < seq_size:
            norms.append(shift_seq(norms[-1]))
        arrived = None if k == 1 else shift_seq(moving)
        held = run_block(k, held)
        if k == seq_size - 1:
            feed_moving = shift_seq(feed_out[1])
            held = run_block(0, held)
            activation, grad_gate, grad_up = held
            held = (grad_gate, grad_up, activation)
            other_units = unit_products(held, norms, all_grads, 1)
            arrived, feed_moving, held, other_units, feed_out, feed_dx = stage(
                arrived, feed_moving, held, other_units, feed_out, feed_dx
            )
        else:
            norms, arrived, held, feed_out, feed_dx = stage(norms, arrived, held, feed_out, feed_dx)
        moving = feed_dx[k] if k == 1 else add_low(arrived, feed_dx[k])
    arrived = shift_seq(moving)
    other_units = swap_core(other_units)
    arrived, other_units = stage(arrived, other_units)
    grad_norm_three = add_wide(arrived, feed_dx[0])

    def seq_blocks(first, second):
        blocks = jnp.concatenate([first.astype(jnp.bfloat16), second.astype(jnp.bfloat16)])
        return blocks.reshape(seq_size, part_rows, blocks.shape[1])

    if seq_size > 2:
        feed_moving = shift_seq(add_low(feed_moving, feed_out[2]))
    grad_output = cotangent.astype(jnp.float32) * valid_rows
    grad_second, grad_gain_feed = norm_three_back(grad_norm_three)
    grad_second = grad_second + grad_output
    second_low = grad_second.astype(jnp.bfloat16)
    grad_mixed = contract_cols(second_low, full_cross_out).astype(jnp.bfloat16)
    cross_out_own, cross_out_other = weight_products([cross_mixed], [second_low])
    cross_out_other = swap_core(cross_out_other)
    grad_cross_queries, grad_memory_keys, grad_memory_values = cross_backward(
        cross_queries, memory_keys, memory_values, grad_mixed, item_row
    )
    grad_norm_two = contract_cols(grad_cross_queries, full_cross_query)
    grad_first, grad_gain_cross = norm_two_back(grad_norm_two)
    grad_first = grad_first + grad_second
    first_low = grad_first.astype(jnp.bfloat16)
    grad_attended = contract_cols(first_low, full_out).astype(jnp.bfloat16)
    grad_attended = jnp.stack(
        [grad_attended[:, s * head_width : (s + 1) * head_width] for s in range(seq_size)]
    )
    feed_moving, cross_out_own, cross_out_other, grad_attended, first_low, grad_cross_queries = (
        stage(
            feed_moving,
            cross_out_own,
            cross_out_other,
            grad_attended,
            first_low,
            grad_cross_queries,
        )
    )

    head_grad = swap_seq(grad_attended).reshape(rows_dev * seq_size, head_width)
    head_grad = jnp.pad(head_grad, ((0, 0), (0, pairs * LANES - head_width)))
    for k in range(3, seq_size):
        feed_moving = shift_seq(add_low(feed_moving, feed_out[k]))
    cross_out_firsts = reduce_first(cross_out_own, cross_out_other)
    products = weight_products([norm_two], [grad_cross_queries], 0, 3)
    products = weight_products([attended], [first_low], 1, 3, products)
    weight_own, weight_other = weight_products(
        [memory], [grad_memory_keys, grad_memory_values], 2, 3, products
    )
    weight_other = swap_core(weight_other)
    head_grad, feed_moving, cross_out_firsts, weight_own, weight_other = stage(
        head_grad, feed_moving, cross_out_firsts, weight_own, weight_other
    )

    output = (second_sum + add_wide(feed_moving, feed_out[0])).astype(jnp.bfloat16)
    weight_firsts = reduce_first(weight_own, weight_other)
    turned = self_backward(qkv, head_grad, log_total, tables, segment, seq_size)
    norm_terms = contract_cols(turned, qkv_cols).astype(jnp.bfloat16)
    norm_terms = [norm_terms[k * rows_dev : (k + 1) * rows_dev] for k in range(seq_size)]
    weight_firsts, norm_terms, turned, cross_out_firsts = stage(
        weight_firsts, norm_terms, turned, cross_out_firsts
    )

    moving = shift_seq(norm_terms[1])
    cross_out_second = reduce_second(*cross_out_firsts)
    weight_seconds = reduce_second(*weight_firsts)
    own_units = unit_products(held, norms, all_grads, 0, other_units)
    qkv_own, qkv_other = weight_products(norms_one, [turned])
    moving, cross_out_second, weight_seconds, own_units, qkv_own, qkv_other = stage(
        moving, cross_out_second, weight_seconds, own_units, qkv_own, qkv_other
    )

    unit_firsts = reduce_first(own_units.reshape(3, 2, y_size, 2, half_units, width))
    placed = swap_seq(
        jnp.stack(
            [
                seq_blocks(*(s[0] for s in cross_out_second)),
                seq_blocks(*(s[0] for s in weight_seconds)),
            ],
            axis=1,
        )
    )
    if seq_size > 2:
        moving = shift_seq(add_low(moving, norm_terms[2]))
    qkv_other = swap_core(qkv_other)
    moving, placed, unit_firsts, qkv_other, weight_seconds = stage(
        moving, placed, unit_firsts, qkv_other, weight_seconds
    )

    for k in range(3, seq_size):
        moving = shift_seq(add_low(moving, norm_terms[k]))
    qkv_firsts = reduce_first(qkv_own, qkv_other)
    unit_grads = jnp.concatenate(reduce_second(*unit_firsts), axis=1)
    kv_blocks = jnp.stack(
        [s[2].astype(jnp.bfloat16).reshape(seq_size, -1, width) for s in weight_seconds], axis=1
    )
    later = swap_seq(
        jnp.stack(
            [
                seq_blocks(*(s[1] for s in weight_seconds)),
                kv_blocks.reshape(seq_size, part_rows, width),
            ],
            axis=1,
        )
    )
    moving, later, unit_grads, qkv_firsts = stage(moving, later, unit_grads, qkv_firsts)

    qkv_placed = swap_seq(seq_blocks(*(s[0] for s in reduce_second(*qkv_firsts))))
    grad_norm_one = add_wide(moving, norm_terms[0])
    grad_tokens_wide, grad_gain_self = norm_one_back(grad_norm_one)
    grad_tokens = (grad_tokens_wide + grad_first).astype(jnp.bfloat16)
    gains = jnp.stack([grad_gain_self, grad_gain_cross, grad_gain_feed])
    gains = gains.reshape(-1, dp_size * seq_size, part_rows).transpose(1, 0, 2)
    gains = jnp.sum(
        lax.all_to_all(gains, ("dp", "seq"), split_axis=0, concat_axis=0, tiled=True), axis=0
    )
    grad_cross_out, grad_cross_query, grad_cross_kv, grad_self_out = (
        jnp.sum(p[:, n].astype(jnp.float32), axis=0)
        for p, n in ((placed, 0), (placed, 1), (later, 1), (later, 0))
    )
    kv_rows = part_rows // 2
    grad_qkv = (
        qkv_placed
        .reshape(seq_size, part_rows, pairs, 3, LANES)
        .transpose(3, 1, 0, 2, 4)
        .reshape(3, part_rows, seq_size, pairs * LANES)[..., :head_width]
        .reshape(3, part_rows, width)
        .astype(jnp.float32)
    )
    return (
        output,
        grad_tokens,
        gains[0],
        gains[1],
        gains[2],
        grad_qkv[0],
        grad_qkv[1],
        grad_qkv[2],
        grad_self_out,
        grad_cross_query,
        grad_cross_kv[:kv_rows],
        grad_cross_kv[kv_rows:],
        grad_cross_out,
        unit_grads[0],
        unit_grads[1],
        unit_grads[2],
    )


def solution(mesh):
    placed = (
        P(("dp", "seq"), None),
        P("dp", None, None, None),
        P("dp", None),
        P(),
        P(),
        P(),
        P(("dp", "seq"), None),
        P(("dp", "seq"), None),
        P(("dp", "seq"), None),
        P(("dp", "seq"), None),
        P(("dp", "seq"), None),
        P(("dp", "seq"), None),
        P(("dp", "seq"), None),
        P(("dp", "seq"), None),
        P(("dp", "seq"), None),
        P(("dp", "seq"), None),
        P(("dp", "seq"), None),
        P(("dp", "seq"), None),
    )
    return jax.shard_map(
        local,
        mesh=mesh,
        in_specs=placed,
        out_specs=(
            P(("dp", "seq"), None),
            P(("dp", "seq"), None),
            P(("dp", "seq")),
            P(("dp", "seq")),
            P(("dp", "seq")),
            P(("dp", "seq"), None),
            P(("dp", "seq"), None),
            P(("dp", "seq"), None),
            P(("dp", "seq"), None),
            P(("dp", "seq"), None),
            P(("dp", "seq"), None),
            P(("dp", "seq"), None),
            P(("dp", "seq"), None),
            P(("dp", "seq"), None),
            P(("dp", "seq"), None),
            P(("dp", "seq"), None),
        ),
        check_vma=False,
    )
```

```python
import jax
import jax.numpy as jnp
from jax import lax
from jax.experimental import pallas as pl
from jax.experimental.pallas import tpu as pltpu
from jax.sharding import PartitionSpec as P

HEADS = 24
HDIM = 64
ROT = 32


EPSILON = 1e-05
NEG_FILL = -1e30


def layer_norm(values, gain_vector):
    average = jnp.mean(values, axis=-1, keepdims=True)
    centered = values - average
    variance = jnp.mean(centered * centered, axis=-1, keepdims=True)
    return centered * lax.rsqrt(variance + EPSILON) * gain_vector


def layout(lengths, row_ids):
    first_end = lengths[0]
    second_end = lengths[0] + lengths[1]
    segment = jnp.where(row_ids < first_end, 0, jnp.where(row_ids < second_end, 1, 2)).astype(
        jnp.int32
    )
    seg_start = jnp.where(segment == 0, 0, jnp.where(segment == 1, first_end, second_end))
    return (segment, row_ids - seg_start)


def matmul(left, right):
    return jnp.dot(left, right, preferred_element_type=jnp.float32)


def contract_rows(left, right):
    return lax.dot_general(
        left, right, (((0,), (0,)), ((), ())), preferred_element_type=jnp.float32
    )


def contract_cols(left, right):
    return lax.dot_general(
        left, right, (((1,), (1,)), ((), ())), preferred_element_type=jnp.float32
    )


LANES = 128
PAIR = LANES // HDIM
LOG2E = 1.4426950408889634


def taking(microseconds):
    return pl.CostEstimate(
        flops=0, bytes_accessed=int(3e6 * microseconds), transcendentals=0
    )


def turn(values, cosine, sine_low, sine_high, sign):
    half_rot = ROT // 2
    ahead = pltpu.roll(values, LANES - half_rot, 1)
    behind = pltpu.roll(values, half_rot, 1)
    return values * cosine + sign * (behind * sine_high - ahead * sine_low)


def dot(left, right, left_dim, right_dim):
    return lax.dot_general(
        left, right, (((left_dim,), (right_dim,)), ((), ())), preferred_element_type=jnp.float32
    )


def lane_tables(position):
    half_rot = ROT // 2
    feature = jnp.arange(LANES, dtype=jnp.int32) % HDIM
    frequency = 10000.0 ** (-(feature % half_rot).astype(jnp.float32) / half_rot)
    angles = position.astype(jnp.float32)[:, None] * frequency[None, :]
    cosine = jnp.where(feature < ROT, jnp.cos(angles), 1.0)
    sine = jnp.sin(angles)
    return (
        cosine,
        jnp.where(feature < half_rot, sine, 0.0),
        jnp.where((feature >= half_rot) & (feature < ROT), sine, 0.0),
    )


def seq_distance_order(block, seq_size):
    place = lax.axis_index("seq")
    return lax.rem(place + (seq_size - block), seq_size)


def part(kind, head):
    return slice(kind * LANES + head * HDIM, kind * LANES + (head + 1) * HDIM)


def self_forward(norms, qkv_cols, tables, segment):
    seq_size, (block, width) = len(norms), norms[0].shape
    length = block * seq_size
    group = 3 * LANES
    pairs = qkv_cols.shape[1] // group
    scale = HDIM ** (-0.5) * LOG2E

    def body(*refs):
        norm_refs = refs[:seq_size]
        cols_ref, cos_ref, low_ref, high_ref, seg_col, seg_row, qkv_out, mixed_ref, total_ref = refs[
            seq_size:
        ]
        for number in range(seq_size):
            rows = slice(number * block, (number + 1) * block)
            tables = cos_ref[rows], low_ref[rows], high_ref[rows]
            projected = dot(norm_refs[number][...], cols_ref[...], 1, 0)
            for kind in range(3):
                cols = slice(kind * LANES, (kind + 1) * LANES)
                values = projected[:, cols]
                if kind < 2:
                    values = turn(values, *tables, 1.0)
                qkv_out[rows, cols] = values.astype(jnp.bfloat16)
        for number in range(seq_size):
            rows = slice(number * block, (number + 1) * block)
            same = seg_col[...] == seg_row[:, rows]
            mixed = []
            for head in range(PAIR):
                scores = dot(qkv_out[:, part(1, head)], qkv_out[rows, part(0, head)], 1, 1)
                scores = jnp.where(same, scores, NEG_FILL)
                highest = jnp.max(scores, axis=0, keepdims=True)
                raised = jnp.exp2((scores - highest) * scale)
                total = jnp.sum(raised, axis=0, keepdims=True)
                mixed.append(dot(qkv_out[:, part(2, head)], raised.astype(jnp.bfloat16), 0, 0) / total)
                total_ref[0, head : head + 1, rows] = highest * scale + jnp.log2(total)
            place = seq_distance_order(number, seq_size)
            target = pl.ds(pl.multiple_of(place * block, block), block)
            mixed_ref[target, :] = jnp.concatenate(mixed).T.astype(jnp.bfloat16)

    whole = pl.BlockSpec((length, LANES), lambda p: (0, 0))
    return pl.pallas_call(
        body,
        grid=(pairs,),
        in_specs=[pl.BlockSpec((block, width), lambda p: (0, 0))] * seq_size
        + [pl.BlockSpec((width, group), lambda p: (0, p))]
        + [whole] * 3
        + [
            pl.BlockSpec((length, 1), lambda p: (0, 0)),
            pl.BlockSpec((1, length), lambda p: (0, 0)),
        ],
        out_specs=[
            pl.BlockSpec((length, group), lambda p: (0, p)),
            pl.BlockSpec((length, LANES), lambda p: (0, p)),
            pl.BlockSpec((1, PAIR, length), lambda p: (p, 0, 0)),
        ],
        out_shape=[
            jax.ShapeDtypeStruct((length, pairs * group), jnp.bfloat16),
            jax.ShapeDtypeStruct((length, pairs * LANES), jnp.bfloat16),
            jax.ShapeDtypeStruct((pairs, PAIR, length), jnp.float32),
        ],
        compiler_params=pltpu.CompilerParams(vmem_limit_bytes=40 << 20),
        cost_estimate=taking(8),
    )(*norms, qkv_cols, *tables, segment[:, None], segment[None, :])


def self_backward(qkv, grad_out, log_total, tables, segment, seq_size):
    length = qkv.shape[0]
    group = 3 * LANES
    pairs = qkv.shape[1] // group
    block = length // seq_size
    scaling = HDIM ** (-0.5)
    scale = scaling * LOG2E

    def body(qkv_ref, grad_ref, total_ref, *rest):
        cos_ref, low_ref, high_ref, seg_col, seg_row, out_ref, dk_sum, dv_sum = rest
        for number in range(seq_size):
            rows = slice(number * block, (number + 1) * block)
            same = seg_col[...] == seg_row[:, rows]
            place = seq_distance_order(number, seq_size)
            grads = grad_ref[pl.ds(pl.multiple_of(place * block, block), block), :]
            grad_queries = []
            for head in range(PAIR):
                cols = slice(head * HDIM, (head + 1) * HDIM)
                grad_head = grads[:, cols]
                query_head = qkv_ref[rows, part(0, head)]
                key_head = qkv_ref[:, part(1, head)]
                scores = dot(key_head, query_head, 1, 1) * scale - total_ref[
                    0, head : head + 1, rows
                ]
                chance = jnp.exp2(jnp.where(same, scores, NEG_FILL))
                grad_chance = dot(qkv_ref[:, part(2, head)], grad_head, 1, 1)
                inner = jnp.sum(chance * grad_chance, axis=0, keepdims=True)
                grad_scores = (chance * (grad_chance - inner)).astype(jnp.bfloat16)
                grad_queries.append(dot(key_head, grad_scores, 0, 0))
                grad_keys = dot(grad_scores, query_head, 1, 0)
                grad_values = dot(chance.astype(jnp.bfloat16), grad_head, 1, 0)
                if number == 0:
                    dk_sum[:, cols] = grad_keys
                    dv_sum[:, cols] = grad_values
                else:
                    dk_sum[:, cols] += grad_keys
                    dv_sum[:, cols] += grad_values
            tables = cos_ref[rows], low_ref[rows], high_ref[rows]
            turned = turn(jnp.concatenate(grad_queries).T * scaling, *tables, -1.0)
            out_ref[rows, :LANES] = turned.astype(jnp.bfloat16)
        tables = cos_ref[...], low_ref[...], high_ref[...]
        turned = turn(dk_sum[...] * scaling, *tables, -1.0)
        out_ref[:, LANES : 2 * LANES] = turned.astype(jnp.bfloat16)
        out_ref[:, 2 * LANES :] = dv_sum[...].astype(jnp.bfloat16)

    whole = pl.BlockSpec((length, LANES), lambda p: (0, 0))
    return pl.pallas_call(
        body,
        grid=(pairs,),
        in_specs=[
            pl.BlockSpec((length, group), lambda p: (0, p)),
            pl.BlockSpec((length, LANES), lambda p: (0, p)),
            pl.BlockSpec((1, PAIR, length), lambda p: (p, 0, 0)),
        ]
        + [whole] * 3
        + [
            pl.BlockSpec((length, 1), lambda p: (0, 0)),
            pl.BlockSpec((1, length), lambda p: (0, 0)),
        ],
        out_specs=pl.BlockSpec((length, group), lambda p: (0, p)),
        out_shape=jax.ShapeDtypeStruct(qkv.shape, jnp.bfloat16),
        scratch_shapes=[pltpu.VMEM((length, LANES), jnp.float32)] * 2,
        compiler_params=pltpu.CompilerParams(vmem_limit_bytes=40 << 20),
        cost_estimate=taking(9),
    )(qkv, grad_out, log_total, *tables, segment[:, None], segment[None, :])


CROSS_HEADS = 8


def cross_softmax(queries, key_rows, item_row):
    scale = HDIM ** (-0.5) * LOG2E
    scores = dot(key_rows, queries, 1, 1)
    count = key_rows.shape[0]
    key_item = (lax.broadcasted_iota(jnp.int32, (count, 1), 0) >= count // 2).astype(jnp.int32)
    scores = jnp.where(key_item == item_row, scores, NEG_FILL)
    raised = jnp.exp2((scores - jnp.max(scores, axis=0, keepdims=True)) * scale)
    return raised / jnp.sum(raised, axis=0, keepdims=True)


def cross_call(body, arrays, item_row, out_rows, flops):
    width = arrays[0].shape[1]
    lanes = CROSS_HEADS * HDIM
    blocks = [pl.BlockSpec((a.shape[0], lanes), lambda p: (0, p)) for a in arrays]
    return pl.pallas_call(
        body,
        grid=(width // lanes,),
        in_specs=blocks + [pl.BlockSpec(item_row.shape, lambda p: (0, 0))],
        out_specs=[pl.BlockSpec((rows, lanes), lambda p: (0, p)) for rows in out_rows],
        out_shape=[jax.ShapeDtypeStruct((rows, width), jnp.bfloat16) for rows in out_rows],
        compiler_params=pltpu.CompilerParams(vmem_limit_bytes=32 << 20),
        cost_estimate=taking(4),
    )(*arrays, item_row)


def cross_forward(queries, key_rows, value_rows, item_row):
    def body(q_ref, k_ref, v_ref, item_ref, mixed_ref):
        mixed = []
        for head in range(CROSS_HEADS):
            cols = slice(head * HDIM, (head + 1) * HDIM)
            chance = cross_softmax(q_ref[:, cols], k_ref[:, cols], item_ref[...])
            mixed.append(dot(v_ref[:, cols], chance.astype(jnp.bfloat16), 0, 0))
        mixed_ref[...] = jnp.concatenate(mixed).T.astype(jnp.bfloat16)

    return cross_call(
        body, (queries, key_rows, value_rows), item_row, [queries.shape[0]], 4
    )[0]


def cross_backward(queries, key_rows, value_rows, grad_mixed, item_row):
    scaling = HDIM ** (-0.5)

    def body(q_ref, k_ref, v_ref, grad_ref, item_ref, dq_ref, dk_ref, dv_ref):
        grad_queries = []
        for head in range(CROSS_HEADS):
            cols = slice(head * HDIM, (head + 1) * HDIM)
            query_head, key_head, grad_head = q_ref[:, cols], k_ref[:, cols], grad_ref[:, cols]
            chance = cross_softmax(query_head, key_head, item_ref[...])
            grad_chance = dot(v_ref[:, cols], grad_head, 1, 1)
            inner = jnp.sum(chance * grad_chance, axis=0, keepdims=True)
            grad_scores = (chance * (grad_chance - inner)).astype(jnp.bfloat16)
            grad_queries.append(dot(key_head, grad_scores, 0, 0))
            dk_ref[:, cols] = (dot(grad_scores, query_head, 1, 0) * scaling).astype(jnp.bfloat16)
            dv_ref[:, cols] = dot(chance.astype(jnp.bfloat16), grad_head, 1, 0).astype(
                jnp.bfloat16
            )
        dq_ref[...] = (jnp.concatenate(grad_queries).T * scaling).astype(jnp.bfloat16)

    rows, keys = queries.shape[0], key_rows.shape[0]
    return cross_call(
        body, (queries, key_rows, value_rows, grad_mixed), item_row, [rows, keys, keys], 10
    )


def feed_block(normed, grads, gate_up, down, number, count, held):
    rows, width = normed.shape
    units = down.shape[0]
    steps = 3
    tile = units // steps

    def body(x_ref, g_ref, gate_ref, up_ref, down_ref, *rest):
        act_ref, dgate_ref, dup_ref, out_ref, dx_ref, out_sum, dx_sum = rest[-7:]
        step = pl.program_id(0)
        values, grad_rows = x_ref[...], g_ref[...]
        gate = dot(values, gate_ref[...], 1, 1)
        up = dot(values, up_ref[...], 1, 1)
        grad_act = dot(grad_rows, down_ref[...], 1, 1)
        chance = jax.nn.sigmoid(gate)
        silu = gate * chance
        act = (silu * up).astype(jnp.bfloat16)
        grad_gate = (grad_act * up * (chance + silu * (1.0 - chance))).astype(jnp.bfloat16)
        grad_up = (grad_act * silu).astype(jnp.bfloat16)
        act_ref[...] = act
        dgate_ref[...] = grad_gate
        dup_ref[...] = grad_up
        out_part = dot(act, down_ref[...], 1, 0)
        dx_part = dot(grad_gate, gate_ref[...], 1, 0) + dot(grad_up, up_ref[...], 1, 0)

        @pl.when(step == 0)
        def _():
            out_sum[...] = out_part
            dx_sum[...] = dx_part

        @pl.when(step > 0)
        def _():
            out_sum[...] += out_part
            dx_sum[...] += dx_part

        @pl.when(step == steps - 1)
        def _():
            out_ref[...] = out_sum[...].astype(jnp.bfloat16)
            dx_ref[...] = dx_sum[...].astype(jnp.bfloat16)

    full = pl.BlockSpec((rows, width), lambda t: (0, 0))
    block = pl.BlockSpec((rows, tile), lambda t: (number, t))
    unit_shape = jax.ShapeDtypeStruct((rows * count, units), jnp.bfloat16)
    row_shape = jax.ShapeDtypeStruct((rows, width), jnp.bfloat16)
    held = [] if held is None else list(held)
    return pl.pallas_call(
        body,
        grid=(steps,),
        in_specs=[
            full,
            full,
            pl.BlockSpec((tile, width), lambda t: (t, 0)),
            pl.BlockSpec((tile, width), lambda t: (steps + t, 0)),
            pl.BlockSpec((tile, width), lambda t: (t, 0)),
        ]
        + [pl.BlockSpec(memory_space=pl.ANY)] * len(held),
        out_specs=[block] * 3 + [full] * 2,
        out_shape=[unit_shape] * 3 + [row_shape] * 2,
        scratch_shapes=[pltpu.VMEM((rows, width), jnp.float32)] * 2,
        input_output_aliases={5 + n: n for n in range(len(held))},
        compiler_params=pltpu.CompilerParams(vmem_limit_bytes=40 << 20),
        cost_estimate=taking(4),
    )(normed, grads, gate_up, gate_up, down, *held)


def unit_products(units, norms, grads, core, arrived=None):
    seq_size, (block, width) = len(norms), norms[0].shape
    length, count = units[0].shape
    steps = 3
    tile = count // (2 * steps)

    def body(*refs):
        unit_refs, refs = refs[:3], refs[3:]
        norm_refs, grad_refs, refs = refs[:seq_size], refs[seq_size : 2 * seq_size], refs[2 * seq_size :]
        out_ref, all_norms, all_grads = refs[-3:]

        @pl.when(pl.program_id(0) == 0)
        def _():
            for k in range(seq_size):
                rows = slice(k * block, (k + 1) * block)
                all_norms[rows, :] = norm_refs[k][...]
                all_grads[rows, :] = grad_refs[k][...]

        for kind in range(3):
            rows = (all_grads if kind == 2 else all_norms)[...]
            total = dot(unit_refs[kind][...], rows, 0, 0)
            if arrived is not None:
                total += refs[0][kind].astype(jnp.float32)
            out_ref[kind] = total.astype(jnp.bfloat16)

    out_block = pl.BlockSpec((3, tile, width), lambda t: (0, t, 0))
    extra = [] if arrived is None else [arrived]
    return pl.pallas_call(
        body,
        grid=(steps,),
        in_specs=[pl.BlockSpec((length, tile), lambda t: (0, core * steps + t))] * 3
        + [pl.BlockSpec((block, width), lambda t: (0, 0))] * (2 * seq_size)
        + [out_block] * len(extra),
        out_specs=out_block,
        out_shape=jax.ShapeDtypeStruct((3, count // 2, width), jnp.bfloat16),
        scratch_shapes=[pltpu.VMEM((length, width), jnp.bfloat16)] * 2,
        compiler_params=pltpu.CompilerParams(vmem_limit_bytes=56 << 20),
        cost_estimate=taking(5),
    )(*units, *norms, *grads, *extra)


def weight_products(lefts, rights, slot=0, slots=1, held=None):
    dp_size = lax.axis_size("dp")
    y_size = dp_size // 4
    rows, height = lefts[0].shape
    columns = rights[0].shape[1]
    tile = 3 * LANES
    place_rows = height // dp_size
    half_rows = place_rows * len(rights) // 2
    per_step = tile // place_rows

    def body(*refs):
        left_refs, refs = refs[: len(lefts)], refs[len(lefts) :]
        right_refs, (own_ref, other_ref, product) = refs[: len(rights)], refs[-3:]
        dp_place = lax.axis_index("dp")
        step = pl.program_id(0)
        for number, right_ref in enumerate(right_refs):
            total = None
            for k, left_ref in enumerate(left_refs):
                term = dot(left_ref[...], right_ref[k * rows : (k + 1) * rows, :], 0, 0)
                total = term if total is None else total + term
            product[...] = total.astype(jnp.bfloat16)
            for chip in range(per_step // 2):
                chip_place = step * (per_step // 2) + chip
                y_back = lax.rem((dp_place >> 2) + y_size - (chip_place >> 1), y_size)
                x_back = ((dp_place >> 1) ^ chip_place) & 1
                for target, core in ((own_ref, dp_place & 1), (other_ref, 1 - (dp_place & 1))):
                    first_row = (2 * chip + core) * place_rows
                    for half in range(2 // len(rights)):
                        begin = pl.multiple_of(first_row + half * half_rows, 16)
                        target[0, number + half, y_back, x_back] = product[
                            pl.ds(begin, half_rows), :
                        ]

    whole = (1, 2, y_size, 2, half_rows, columns)
    out_block = pl.BlockSpec(whole, lambda t: (slot, 0, 0, 0, 0, 0))
    out_shape = jax.ShapeDtypeStruct((slots,) + whole[1:], jnp.bfloat16)
    held = [] if held is None else list(held)
    return pl.pallas_call(
        body,
        grid=(height // tile,),
        in_specs=[pl.BlockSpec((rows, tile), lambda t: (0, t))] * len(lefts)
        + [pl.BlockSpec(r.shape, lambda t: (0, 0)) for r in rights]
        + [pl.BlockSpec(memory_space=pl.ANY)] * len(held),
        out_specs=[out_block] * 2,
        out_shape=[out_shape] * 2,
        scratch_shapes=[pltpu.VMEM((tile, columns), jnp.bfloat16)],
        input_output_aliases={len(lefts) + len(rights) + n: n for n in range(len(held))},
        compiler_params=pltpu.CompilerParams(vmem_limit_bytes=40 << 20),
        cost_estimate=taking(1.5),
    )(*lefts, *rights, *held)


def swap_core(values):
    return lax.ppermute(values, "dp", [(d, d ^ 1) for d in range(lax.axis_size("dp"))])


def shift_dp(values, y, x):
    size = lax.axis_size("dp")
    return lax.ppermute(values, "dp", [(d, ((d + 4 * y) % size) ^ (2 * x)) for d in range(size)])


def shift_seq(values, step=1):
    size = lax.axis_size("seq")
    return lax.ppermute(values, "seq", [(s, (s + step) % size) for s in range(size)])


def gather_rest(pieces):
    last = shift_seq(pieces[0], -1)
    pieces = list(pieces)
    for _ in range(lax.axis_size("seq") - 3):
        pieces.append(shift_seq(pieces[-1]))
    return pieces + [last]


def swap_seq(values):
    return lax.all_to_all(values, "seq", split_axis=0, concat_axis=0, tiled=True)


def gather_places(values):
    size = lax.axis_size("seq")
    return swap_seq(jnp.broadcast_to(values[None], (size,) + values.shape))


def add_wide(left, right):
    return left.astype(jnp.float32) + right.astype(jnp.float32)


def add_low(left, right):
    return add_wide(left, right).astype(jnp.bfloat16)


def stage(*values):
    return lax.optimization_barrier(values)


def spread_first(first, second):
    held = {(0, 0, 0): first, (1, 0, 0): second, (0, 0, 1): shift_dp(first, 0, 1)}
    for y in range(1, lax.axis_size("dp") // 4):
        held[1, y, 0] = shift_dp(held[1, y - 1, 0], 1, 0)
    return held


def spread_second(held):
    held = dict(held)
    for half, y, x in [(h, y, 0) for h, y, _ in held if h == 1]:
        held[half, y, 1] = shift_dp(held[half, y, x], 0, 1)
    for x in range(2):
        for y in range(1, lax.axis_size("dp") // 4):
            held[0, y, x] = shift_dp(held[0, y - 1, x], 1, 0)
    return held


def with_cores(plane):
    return {(core,) + p: swap_core(v) if core else v for core in range(2) for p, v in plane.items()}


def low(values):
    return values.astype(jnp.bfloat16)


def terms(own, arrived, *index):
    index = (slice(None),) + index
    values = own[index].astype(jnp.float32)
    return values if arrived is None else values + arrived[index].astype(jnp.float32)


def pack_first(own, arrived=None):
    y_size = own.shape[2]
    total = low(terms(own, arrived, 0, y_size - 1))
    for y in range(y_size - 2, 0, -1):
        total = low(shift_dp(total, -1, 0).astype(jnp.float32) + terms(own, arrived, 0, y))
    return total, low(terms(own, arrived, 1, slice(None), 1))


def send_first(packed):
    return shift_dp(packed[0], -1, 0), shift_dp(packed[1], 0, 1)


def add_first(came, own, arrived=None):
    return (
        low(came[0].astype(jnp.float32) + terms(own, arrived, 0, 0)),
        low(came[1].astype(jnp.float32) + terms(own, arrived, 1, slice(None), 0)),
    )


def pack_second(first, second):
    total = second[:, -1]
    for y in range(second.shape[1] - 2, 0, -1):
        total = add_low(shift_dp(total, -1, 0), second[:, y])
    return first[:, 1], total


def send_second(packed):
    return shift_dp(packed[0], 0, 1), shift_dp(packed[1], -1, 0)


def add_second(came, first, second):
    return add_wide(first[:, 0], came[0]), add_wide(second[:, 0], came[1])


def assemble(pieces, out_shapes, copies):
    count = len(pieces)

    def body(*refs):
        sources, targets = refs[:count], refs[count : count + len(out_shapes)]
        held, loaded, stored = refs[count + len(out_shapes) : -2], refs[-2], refs[-1]
        loads = [pltpu.make_async_copy(sources[n], held[n], loaded.at[n]) for n in range(count)]
        for load in loads:
            load.start()
        stores = []
        for n in range(count):
            loads[n].wait()
            for number, (piece, source, out, target) in enumerate(copies):
                if piece == n:
                    stores.append(
                        pltpu.make_async_copy(
                            held[n].at[source],
                            targets[out].at[target],
                            stored.at[number],
                        )
                    )
                    stores[-1].start()
        for store in stores:
            store.wait()

    return pl.pallas_call(
        body,
        out_shape=[jax.ShapeDtypeStruct(s, jnp.bfloat16) for s in out_shapes],
        in_specs=[pl.BlockSpec(memory_space=pl.ANY)] * count,
        out_specs=[pl.BlockSpec(memory_space=pl.ANY)] * len(out_shapes),
        scratch_shapes=[pltpu.VMEM(p.shape, p.dtype) for p in pieces]
        + [pltpu.SemaphoreType.DMA((count,)), pltpu.SemaphoreType.DMA((len(copies),))],
        compiler_params=pltpu.CompilerParams(vmem_limit_bytes=32 << 20),
        cost_estimate=taking(2),
    )(*pieces)


def local(
    tokens,
    context,
    item_lengths,
    gain_self,
    gain_cross,
    gain_feed,
    self_query,
    self_key,
    self_value,
    self_out,
    cross_query,
    cross_key,
    cross_value,
    cross_out,
    feed_gate,
    feed_up,
    feed_down,
    cotangent,
):
    rows_dev, width = tokens.shape
    dp_size, seq_size = lax.axis_size("dp"), lax.axis_size("seq")
    seq_place = lax.axis_index("seq")
    y_size = dp_size // 4
    head_width = HEADS // seq_size * HDIM
    pairs = -(-head_width // LANES)
    part_rows = self_query.shape[0]

    def whole_rows(rows):
        return lax.all_gather(rows, "dp", axis=0, tiled=False).reshape(-1, rows.shape[-1])

    qkv_parts = jnp.stack([self_query, self_key, self_value]).reshape(
        3, part_rows, seq_size, head_width
    )
    qkv_parts = jnp.pad(qkv_parts, ((0, 0),) * 3 + ((0, pairs * LANES - head_width),))
    qkv_parts = qkv_parts.reshape(3, part_rows, seq_size, pairs, LANES).transpose(2, 1, 3, 0, 4)
    qkv_parts = qkv_parts.reshape(seq_size, part_rows, pairs * 3 * LANES)
    qkv_parts = jnp.concatenate(
        [qkv_parts]
        + [jnp.broadcast_to(self_out[None], (seq_size,) + self_out.shape)],
        axis=2,
    )
    qkv_parts, tokens, feed_gate, feed_up, feed_down, cotangent, item_lengths = stage(
        qkv_parts, tokens, feed_gate, feed_up, feed_down, cotangent, item_lengths
    )
    early_rows = swap_seq(qkv_parts)
    token_values = tokens.astype(jnp.float32)
    norm_one, norm_one_back = jax.vjp(layer_norm, token_values, gain_self.astype(jnp.float32))
    norm_one = norm_one.astype(jnp.bfloat16)
    norms_one = [norm_one, shift_seq(norm_one)]
    feed_parts = jnp.stack([feed_gate, feed_up, feed_down])
    half_units = feed_parts.shape[1] // 2
    feed_held = spread_first(feed_parts[:, :half_units], feed_parts[:, half_units:])
    for y in range(1, y_size):
        feed_held[0, y, 0] = shift_dp(feed_held[0, y - 1, 0], 1, 0)
    feed_held[1, 0, 1] = shift_dp(feed_held[1, 0, 0], 0, 1)
    row_ids = jnp.concatenate(
        [
            lax.rem(seq_place + (seq_size - k), seq_size) * rows_dev
            + jnp.arange(rows_dev, dtype=jnp.int32)
            for k in range(seq_size)
        ]
    )
    segment, position = layout(item_lengths[0], row_ids)
    row_segment = segment[:rows_dev]
    tables = lane_tables(position)
    valid_rows = (row_segment < 2).astype(jnp.float32)[:, None]
    grad_output_low = (cotangent.astype(jnp.float32) * valid_rows).astype(jnp.bfloat16)
    cross_kv = jnp.concatenate([cross_key, cross_value])
    early_rows, norms_one[1], feed_held, tables, grad_output_low, cross_query = stage(
        early_rows, norms_one[1], feed_held, tables, grad_output_low, cross_query
    )
    qkv_cols = whole_rows(early_rows[:, :, :-width])
    full_out = whole_rows(early_rows[:, :, -width:])

    norms_one = gather_rest(norms_one)
    query_rows = gather_places(cross_query)
    for y in range(1, y_size):
        feed_held[0, y, 1] = shift_dp(feed_held[0, y - 1, 1], 1, 0)
        feed_held[1, y, 1] = shift_dp(feed_held[1, y, 0], 0, 1)
    norms_one, qkv_cols, feed_held, cross_kv, cross_out, query_rows = stage(
        norms_one, qkv_cols, feed_held, cross_kv, cross_out, query_rows
    )
    full_cross_query = whole_rows(query_rows)

    cross_rows = gather_places(jnp.stack([cross_kv, cross_out]))
    qkv, head_attended, log_total = self_forward(norms_one, qkv_cols, tables, segment)
    cross_rows, feed_held, head_attended, grad_output_low = stage(
        cross_rows, feed_held, head_attended, grad_output_low
    )
    full_cross_kv = whole_rows(cross_rows[:, 0]).reshape(dp_size * seq_size, 2, -1, width)
    full_cross_out = whole_rows(cross_rows[:, 1])

    attended = swap_seq(head_attended[:, :head_width].reshape(seq_size, rows_dev, head_width))
    all_grads = [grad_output_low, shift_seq(grad_output_low)]
    feed_cores = with_cores(feed_held)
    places = [
        (core, half, y, x)
        for core in range(2)
        for half in range(2)
        for y in range(y_size)
        for x in range(2)
    ]
    unit_gate_up, unit_down = assemble(
        [feed_cores[p] for p in places],
        [(2, len(places), half_units, width), (1, len(places), half_units, width)],
        [
            (n, (kind,), kind // 2, (kind % 2, n))
            for n in range(len(places))
            for kind in range(3)
        ],
    )
    unit_gate_up, unit_down = unit_gate_up.reshape(-1, width), unit_down.reshape(-1, width)
    attended, unit_gate_up, unit_down, all_grads = stage(
        attended, unit_gate_up, unit_down, all_grads
    )

    last_grad = shift_seq(all_grads[0], -1)
    attended = jnp.concatenate([attended[s] for s in range(seq_size)], axis=1)
    first_sum = token_values + matmul(attended, full_out)
    norm_two, norm_two_back = jax.vjp(layer_norm, first_sum, gain_cross.astype(jnp.float32))
    norm_two = norm_two.astype(jnp.bfloat16)
    cross_queries = matmul(norm_two, full_cross_query).astype(jnp.bfloat16)
    all_grads, last_grad, cross_queries = stage(all_grads, last_grad, cross_queries)

    for _ in range(seq_size - 3):
        all_grads.append(shift_seq(all_grads[-1]))
    all_grads.append(last_grad)
    memory = context[0].reshape(-1, context.shape[3])
    full_cross_key = full_cross_kv[:, 0].reshape(-1, width)
    full_cross_value = full_cross_kv[:, 1].reshape(-1, width)
    memory_keys = matmul(memory, full_cross_key).astype(jnp.bfloat16)
    memory_values = matmul(memory, full_cross_value).astype(jnp.bfloat16)
    item_row = (row_segment == 1).astype(jnp.int32)[None, :]
    cross_mixed = cross_forward(cross_queries, memory_keys, memory_values, item_row)
    second_sum = first_sum + matmul(cross_mixed, full_cross_out)
    norm_three, norm_three_back = jax.vjp(layer_norm, second_sum, gain_feed.astype(jnp.float32))
    norm_three = norm_three.astype(jnp.bfloat16)
    all_grads, norm_three = stage(all_grads, norm_three)

    norms = [norm_three, shift_seq(norm_three)]
    norms, all_grads = stage(norms, all_grads)

    held, feed_out, feed_dx, moving, feed_moving = None, {}, {}, None, None

    def run_block(k, held):
        *held, feed_out[k], feed_dx[k] = feed_block(
            norms[k], all_grads[k], unit_gate_up, unit_down, k, seq_size, held
        )
        return held

    for k in range(1, seq_size):
        if k + 1 < seq_size:
            norms.append(shift_seq(norms[-1]))
        arrived = None if k == 1 else shift_seq(moving)
        held = run_block(k, held)
        if k == seq_size - 1:
            feed_moving = shift_seq(feed_out[1])
            held = run_block(0, held)
            activation, grad_gate, grad_up = held
            held = (grad_gate, grad_up, activation)
            arrived, feed_moving, held, feed_out, feed_dx = stage(
                arrived, feed_moving, held, feed_out, feed_dx
            )
        else:
            norms, arrived, held, feed_out, feed_dx = stage(norms, arrived, held, feed_out, feed_dx)
        moving = feed_dx[k] if k == 1 else add_low(arrived, feed_dx[k])
    arrived = shift_seq(moving)
    other_units = unit_products(held, norms, all_grads, 1)
    arrived, other_units = stage(arrived, other_units)
    other_units = swap_core(other_units)
    grad_norm_three = add_wide(arrived, feed_dx[0])

    def seq_blocks(first, second):
        blocks = jnp.concatenate([first.astype(jnp.bfloat16), second.astype(jnp.bfloat16)])
        return blocks.reshape(seq_size, part_rows, blocks.shape[1])

    if seq_size > 2:
        feed_moving = shift_seq(add_low(feed_moving, feed_out[2]))
    grad_output = cotangent.astype(jnp.float32) * valid_rows
    grad_second, grad_gain_feed = norm_three_back(grad_norm_three)
    grad_second = grad_second + grad_output
    second_low = grad_second.astype(jnp.bfloat16)
    grad_mixed = contract_cols(second_low, full_cross_out).astype(jnp.bfloat16)
    cross_out_own, cross_out_other = weight_products([cross_mixed], [second_low])
    cross_out_other = swap_core(cross_out_other)
    grad_cross_queries, grad_memory_keys, grad_memory_values = cross_backward(
        cross_queries, memory_keys, memory_values, grad_mixed, item_row
    )
    grad_norm_two = contract_cols(grad_cross_queries, full_cross_query)
    grad_first, grad_gain_cross = norm_two_back(grad_norm_two)
    grad_first = grad_first + grad_second
    first_low = grad_first.astype(jnp.bfloat16)
    grad_attended = contract_cols(first_low, full_out).astype(jnp.bfloat16)
    grad_attended = jnp.stack(
        [grad_attended[:, s * head_width : (s + 1) * head_width] for s in range(seq_size)]
    )
    products = weight_products([norm_two], [grad_cross_queries], 0, 3)
    products = weight_products([attended], [first_low], 1, 3, products)
    weight_own, weight_other = weight_products(
        [memory], [grad_memory_keys, grad_memory_values], 2, 3, products
    )
    cross_out_packed = pack_first(cross_out_own, cross_out_other)
    feed_moving, cross_out_packed, grad_attended, weight_other, other_units = stage(
        feed_moving, cross_out_packed, grad_attended, weight_other, other_units
    )

    head_grad = swap_seq(grad_attended)
    cross_out_came = send_first(cross_out_packed)
    weight_other = swap_core(weight_other)
    own_units = unit_products(held, norms, all_grads, 0, other_units)
    head_grad, cross_out_came, weight_other, own_units = stage(
        head_grad, cross_out_came, weight_other, own_units
    )

    weight_packed = pack_first(weight_own, weight_other)
    cross_out_firsts = add_first(cross_out_came, cross_out_own, cross_out_other)
    head_grad = head_grad.reshape(rows_dev * seq_size, head_width)
    head_grad = jnp.pad(head_grad, ((0, 0), (0, pairs * LANES - head_width)))
    for k in range(3, seq_size):
        feed_moving = add_low(feed_moving, feed_out[k])
        if k + 1 < seq_size:
            feed_moving = shift_seq(feed_moving)
    head_grad, weight_packed, feed_moving, cross_out_firsts = stage(
        head_grad, weight_packed, feed_moving, cross_out_firsts
    )
    if seq_size > 3:
        feed_moving = shift_seq(feed_moving)
    weight_came = send_first(weight_packed)
    turned = self_backward(qkv, head_grad, log_total, tables, segment, seq_size)
    weight_came, turned, feed_moving, cross_out_firsts = stage(
        weight_came, turned, feed_moving, cross_out_firsts
    )

    norm_terms = low(contract_cols(turned, qkv_cols))
    norm_terms = [norm_terms[k * rows_dev : (k + 1) * rows_dev] for k in range(seq_size)]
    weight_firsts = add_first(weight_came, weight_own, weight_other)
    cross_out_packed = pack_second(*cross_out_firsts)
    weight_packed = pack_second(*weight_firsts)
    norm_terms, cross_out_packed, weight_packed, turned, own_units, feed_moving = stage(
        norm_terms, cross_out_packed, weight_packed, turned, own_units, feed_moving
    )
    moving = shift_seq(norm_terms[1])
    cross_out_came = send_second(cross_out_packed)
    weight_came = send_second(weight_packed)
    qkv_own, qkv_other = weight_products(norms_one, [turned])
    moving, cross_out_came, weight_came, qkv_own, qkv_other = stage(
        moving, cross_out_came, weight_came, qkv_own, qkv_other
    )

    qkv_other = swap_core(qkv_other)
    if seq_size > 2:
        moving = shift_seq(add_low(moving, norm_terms[2]))
    own_units = own_units.reshape(3, 2, y_size, 2, half_units, width)
    unit_came = send_first(pack_first(own_units))
    output = low(second_sum + add_wide(feed_moving, feed_out[0]))
    cross_out_second = add_second(cross_out_came, *cross_out_firsts)
    weight_seconds = add_second(weight_came, *weight_firsts)
    placed = swap_seq(
        jnp.stack(
            [
                seq_blocks(*(s[0] for s in cross_out_second)),
                seq_blocks(*(s[0] for s in weight_seconds)),
            ],
            axis=1,
        )
    )
    kv_blocks = jnp.stack(
        [low(s[2]).reshape(seq_size, -1, width) for s in weight_seconds], axis=1
    )
    qkv_came = send_first(pack_first(qkv_own, qkv_other))
    qkv_firsts = add_first(qkv_came, qkv_own, qkv_other)
    qkv_seconds = add_second(send_second(pack_second(*qkv_firsts)), *qkv_firsts)
    later = jnp.concatenate(
        [
            seq_blocks(*(s[1] for s in weight_seconds)),
            kv_blocks.reshape(seq_size, part_rows, width),
            seq_blocks(*(s[0] for s in qkv_seconds)),
        ],
        axis=2,
    )
    moving, placed, unit_came, later = stage(moving, placed, unit_came, later)

    for k in range(3, seq_size):
        moving = shift_seq(add_low(moving, norm_terms[k]))
    later = swap_seq(later)
    unit_firsts = add_first(unit_came, own_units)
    unit_came = send_second(pack_second(*unit_firsts))
    moving, later, unit_came = stage(moving, later, unit_came)

    unit_grads = jnp.concatenate(add_second(unit_came, *unit_firsts), axis=1)
    grad_norm_one = add_wide(moving, norm_terms[0])
    grad_tokens_wide, grad_gain_self = norm_one_back(grad_norm_one)
    grad_tokens = (grad_tokens_wide + grad_first).astype(jnp.bfloat16)
    gains = jnp.stack([grad_gain_self, grad_gain_cross, grad_gain_feed])
    gains = gains.reshape(-1, dp_size * seq_size, part_rows).transpose(1, 0, 2)
    gains = jnp.sum(
        lax.all_to_all(gains, ("dp", "seq"), split_axis=0, concat_axis=0, tiled=True), axis=0
    )
    split = later[:, :, : 2 * width].reshape(seq_size, part_rows, 2, width).transpose(0, 2, 1, 3)
    grad_cross_out, grad_cross_query, grad_cross_kv, grad_self_out = (
        jnp.sum(p[:, n].astype(jnp.float32), axis=0)
        for p, n in ((placed, 0), (placed, 1), (split, 1), (split, 0))
    )
    kv_rows = part_rows // 2
    grad_qkv = (
        later[:, :, 2 * width :]
        .reshape(seq_size, part_rows, pairs, 3, LANES)
        .transpose(3, 1, 0, 2, 4)
        .reshape(3, part_rows, seq_size, pairs * LANES)[..., :head_width]
        .reshape(3, part_rows, width)
        .astype(jnp.float32)
    )
    return (
        output,
        grad_tokens,
        gains[0],
        gains[1],
        gains[2],
        grad_qkv[0],
        grad_qkv[1],
        grad_qkv[2],
        grad_self_out,
        grad_cross_query,
        grad_cross_kv[:kv_rows],
        grad_cross_kv[kv_rows:],
        grad_cross_out,
        unit_grads[0],
        unit_grads[1],
        unit_grads[2],
    )


def solution(mesh):
    placed = (
        P(("dp", "seq"), None),
        P("dp", None, None, None),
        P("dp", None),
        P(),
        P(),
        P(),
        P(("dp", "seq"), None),
        P(("dp", "seq"), None),
        P(("dp", "seq"), None),
        P(("dp", "seq"), None),
        P(("dp", "seq"), None),
        P(("dp", "seq"), None),
        P(("dp", "seq"), None),
        P(("dp", "seq"), None),
        P(("dp", "seq"), None),
        P(("dp", "seq"), None),
        P(("dp", "seq"), None),
        P(("dp", "seq"), None),
    )
    return jax.shard_map(
        local,
        mesh=mesh,
        in_specs=placed,
        out_specs=(
            P(("dp", "seq"), None),
            P(("dp", "seq"), None),
            P(("dp", "seq")),
            P(("dp", "seq")),
            P(("dp", "seq")),
            P(("dp", "seq"), None),
            P(("dp", "seq"), None),
            P(("dp", "seq"), None),
            P(("dp", "seq"), None),
            P(("dp", "seq"), None),
            P(("dp", "seq"), None),
            P(("dp", "seq"), None),
            P(("dp", "seq"), None),
            P(("dp", "seq"), None),
            P(("dp", "seq"), None),
            P(("dp", "seq"), None),
        ),
        check_vma=False,
    )
```

```python
import jax
import jax.numpy as jnp
from jax import lax
from jax.experimental import pallas as pl
from jax.experimental.pallas import tpu as pltpu
from jax.sharding import PartitionSpec as P

HEADS = 24
HDIM = 64
ROT = 32


EPSILON = 1e-05
NEG_FILL = -1e30


def layer_norm(values, gain_vector):
    average = jnp.mean(values, axis=-1, keepdims=True)
    centered = values - average
    variance = jnp.mean(centered * centered, axis=-1, keepdims=True)
    return centered * lax.rsqrt(variance + EPSILON) * gain_vector


def layout(lengths, row_ids):
    first_end = lengths[0]
    second_end = lengths[0] + lengths[1]
    segment = jnp.where(row_ids < first_end, 0, jnp.where(row_ids < second_end, 1, 2)).astype(
        jnp.int32
    )
    seg_start = jnp.where(segment == 0, 0, jnp.where(segment == 1, first_end, second_end))
    return (segment, row_ids - seg_start)


def matmul(left, right):
    return jnp.dot(left, right, preferred_element_type=jnp.float32)


def contract_rows(left, right):
    return lax.dot_general(
        left, right, (((0,), (0,)), ((), ())), preferred_element_type=jnp.float32
    )


def contract_cols(left, right):
    return lax.dot_general(
        left, right, (((1,), (1,)), ((), ())), preferred_element_type=jnp.float32
    )


LANES = 128
PAIR = LANES // HDIM
LOG2E = 1.4426950408889634


def taking(microseconds):
    return pl.CostEstimate(
        flops=0, bytes_accessed=int(3e6 * microseconds), transcendentals=0
    )


def turn(values, cosine, sine_low, sine_high, sign):
    half_rot = ROT // 2
    ahead = pltpu.roll(values, LANES - half_rot, 1)
    behind = pltpu.roll(values, half_rot, 1)
    return values * cosine + sign * (behind * sine_high - ahead * sine_low)


def dot(left, right, left_dim, right_dim):
    return lax.dot_general(
        left, right, (((left_dim,), (right_dim,)), ((), ())), preferred_element_type=jnp.float32
    )


def lane_tables(position):
    half_rot = ROT // 2
    feature = jnp.arange(LANES, dtype=jnp.int32) % HDIM
    frequency = 10000.0 ** (-(feature % half_rot).astype(jnp.float32) / half_rot)
    angles = position.astype(jnp.float32)[:, None] * frequency[None, :]
    cosine = jnp.where(feature < ROT, jnp.cos(angles), 1.0)
    sine = jnp.sin(angles)
    return (
        cosine,
        jnp.where(feature < half_rot, sine, 0.0),
        jnp.where((feature >= half_rot) & (feature < ROT), sine, 0.0),
    )


def seq_distance_order(block, seq_size):
    place = lax.axis_index("seq")
    return lax.rem(place + (seq_size - block), seq_size)


def part(kind, head):
    return slice(kind * LANES + head * HDIM, kind * LANES + (head + 1) * HDIM)


def self_forward(norms, qkv_cols, tables, segments):
    seq_size, (block, width) = len(norms), norms[0].shape
    length = block * seq_size
    group = 3 * LANES
    pairs = qkv_cols.shape[1] // group
    scale = HDIM ** (-0.5) * LOG2E

    def body(*refs):
        norm_refs = refs[:seq_size]
        cols_ref, cos_ref, low_ref, high_ref, seg_col, seg_row, qkv_out, mixed_ref, total_ref = refs[
            seq_size:
        ]
        for number in range(seq_size):
            rows = slice(number * block, (number + 1) * block)
            tables = cos_ref[rows], low_ref[rows], high_ref[rows]
            projected = dot(norm_refs[number][...], cols_ref[...], 1, 0)
            for kind in range(3):
                cols = slice(kind * LANES, (kind + 1) * LANES)
                values = projected[:, cols]
                if kind < 2:
                    values = turn(values, *tables, 1.0)
                qkv_out[rows, cols] = values.astype(jnp.bfloat16)
        for number in range(seq_size):
            rows = slice(number * block, (number + 1) * block)
            same = seg_col[...] == seg_row[:, rows]
            mixed = []
            for head in range(PAIR):
                scores = dot(qkv_out[:, part(1, head)], qkv_out[rows, part(0, head)], 1, 1)
                scores = jnp.where(same, scores, NEG_FILL)
                highest = jnp.max(scores, axis=0, keepdims=True)
                raised = jnp.exp2((scores - highest) * scale)
                total = jnp.sum(raised, axis=0, keepdims=True)
                mixed.append(dot(qkv_out[:, part(2, head)], raised.astype(jnp.bfloat16), 0, 0) / total)
                total_ref[0, head : head + 1, rows] = highest * scale + jnp.log2(total)
            place = seq_distance_order(number, seq_size)
            target = pl.ds(pl.multiple_of(place * block, block), block)
            mixed_ref[target, :] = jnp.concatenate(mixed).T.astype(jnp.bfloat16)

    whole = pl.BlockSpec((length, LANES), lambda p: (0, 0))
    return pl.pallas_call(
        body,
        grid=(pairs,),
        in_specs=[pl.BlockSpec((block, width), lambda p: (0, 0))] * seq_size
        + [pl.BlockSpec((width, group), lambda p: (0, p))]
        + [whole] * 3
        + [
            pl.BlockSpec((length, 1), lambda p: (0, 0)),
            pl.BlockSpec((1, length), lambda p: (0, 0)),
        ],
        out_specs=[
            pl.BlockSpec((length, group), lambda p: (0, p)),
            pl.BlockSpec((length, LANES), lambda p: (0, p)),
            pl.BlockSpec((1, PAIR, length), lambda p: (p, 0, 0)),
        ],
        out_shape=[
            jax.ShapeDtypeStruct((length, pairs * group), jnp.bfloat16),
            jax.ShapeDtypeStruct((length, pairs * LANES), jnp.bfloat16),
            jax.ShapeDtypeStruct((pairs, PAIR, length), jnp.float32),
        ],
        compiler_params=pltpu.CompilerParams(vmem_limit_bytes=40 << 20),
        cost_estimate=taking(8),
    )(*norms, qkv_cols, *tables, *segments)


def self_backward(qkv, grad_out, log_total, tables, segments, seq_size):
    length = qkv.shape[0]
    group = 3 * LANES
    pairs = qkv.shape[1] // group
    block = length // seq_size
    scaling = HDIM ** (-0.5)
    scale = scaling * LOG2E

    def body(qkv_ref, grad_ref, total_ref, *rest):
        cos_ref, low_ref, high_ref, seg_col, seg_row, out_ref, dk_sum, dv_sum = rest
        for number in range(seq_size):
            rows = slice(number * block, (number + 1) * block)
            same = seg_col[...] == seg_row[:, rows]
            place = seq_distance_order(number, seq_size)
            grads = grad_ref[pl.ds(pl.multiple_of(place * block, block), block), :]
            grad_queries = []
            for head in range(PAIR):
                cols = slice(head * HDIM, (head + 1) * HDIM)
                grad_head = grads[:, cols]
                query_head = qkv_ref[rows, part(0, head)]
                key_head = qkv_ref[:, part(1, head)]
                scores = dot(key_head, query_head, 1, 1) * scale - total_ref[
                    0, head : head + 1, rows
                ]
                chance = jnp.exp2(jnp.where(same, scores, NEG_FILL))
                grad_chance = dot(qkv_ref[:, part(2, head)], grad_head, 1, 1)
                inner = jnp.sum(chance * grad_chance, axis=0, keepdims=True)
                grad_scores = (chance * (grad_chance - inner)).astype(jnp.bfloat16)
                grad_queries.append(dot(key_head, grad_scores, 0, 0))
                grad_keys = dot(grad_scores, query_head, 1, 0)
                grad_values = dot(chance.astype(jnp.bfloat16), grad_head, 1, 0)
                if number == 0:
                    dk_sum[:, cols] = grad_keys
                    dv_sum[:, cols] = grad_values
                else:
                    dk_sum[:, cols] += grad_keys
                    dv_sum[:, cols] += grad_values
            tables = cos_ref[rows], low_ref[rows], high_ref[rows]
            turned = turn(jnp.concatenate(grad_queries).T * scaling, *tables, -1.0)
            out_ref[rows, :LANES] = turned.astype(jnp.bfloat16)
        tables = cos_ref[...], low_ref[...], high_ref[...]
        turned = turn(dk_sum[...] * scaling, *tables, -1.0)
        out_ref[:, LANES : 2 * LANES] = turned.astype(jnp.bfloat16)
        out_ref[:, 2 * LANES :] = dv_sum[...].astype(jnp.bfloat16)

    whole = pl.BlockSpec((length, LANES), lambda p: (0, 0))
    return pl.pallas_call(
        body,
        grid=(pairs,),
        in_specs=[
            pl.BlockSpec((length, group), lambda p: (0, p)),
            pl.BlockSpec((length, LANES), lambda p: (0, p)),
            pl.BlockSpec((1, PAIR, length), lambda p: (p, 0, 0)),
        ]
        + [whole] * 3
        + [
            pl.BlockSpec((length, 1), lambda p: (0, 0)),
            pl.BlockSpec((1, length), lambda p: (0, 0)),
        ],
        out_specs=pl.BlockSpec((length, group), lambda p: (0, p)),
        out_shape=jax.ShapeDtypeStruct(qkv.shape, jnp.bfloat16),
        scratch_shapes=[pltpu.VMEM((length, LANES), jnp.float32)] * 2,
        compiler_params=pltpu.CompilerParams(vmem_limit_bytes=40 << 20),
        cost_estimate=taking(9),
    )(qkv, grad_out, log_total, *tables, *segments)


CROSS_HEADS = 8


def cross_softmax(queries, key_rows, item_row):
    scale = HDIM ** (-0.5) * LOG2E
    scores = dot(key_rows, queries, 1, 1)
    count = key_rows.shape[0]
    key_item = (lax.broadcasted_iota(jnp.int32, (count, 1), 0) >= count // 2).astype(jnp.int32)
    scores = jnp.where(key_item == item_row, scores, NEG_FILL)
    raised = jnp.exp2((scores - jnp.max(scores, axis=0, keepdims=True)) * scale)
    return raised / jnp.sum(raised, axis=0, keepdims=True)


def cross_call(body, arrays, item_row, out_rows, flops):
    width = arrays[0].shape[1]
    lanes = CROSS_HEADS * HDIM
    blocks = [pl.BlockSpec((a.shape[0], lanes), lambda p: (0, p)) for a in arrays]
    return pl.pallas_call(
        body,
        grid=(width // lanes,),
        in_specs=blocks + [pl.BlockSpec(item_row.shape, lambda p: (0, 0))],
        out_specs=[pl.BlockSpec((rows, lanes), lambda p: (0, p)) for rows in out_rows],
        out_shape=[jax.ShapeDtypeStruct((rows, width), jnp.bfloat16) for rows in out_rows],
        compiler_params=pltpu.CompilerParams(vmem_limit_bytes=32 << 20),
        cost_estimate=taking(4),
    )(*arrays, item_row)


def cross_forward(queries, key_rows, value_rows, item_row):
    def body(q_ref, k_ref, v_ref, item_ref, mixed_ref):
        mixed = []
        for head in range(CROSS_HEADS):
            cols = slice(head * HDIM, (head + 1) * HDIM)
            chance = cross_softmax(q_ref[:, cols], k_ref[:, cols], item_ref[...])
            mixed.append(dot(v_ref[:, cols], chance.astype(jnp.bfloat16), 0, 0))
        mixed_ref[...] = jnp.concatenate(mixed).T.astype(jnp.bfloat16)

    return cross_call(
        body, (queries, key_rows, value_rows), item_row, [queries.shape[0]], 4
    )[0]


def cross_backward(queries, key_rows, value_rows, grad_mixed, item_row):
    scaling = HDIM ** (-0.5)

    def body(q_ref, k_ref, v_ref, grad_ref, item_ref, dq_ref, dk_ref, dv_ref):
        grad_queries = []
        for head in range(CROSS_HEADS):
            cols = slice(head * HDIM, (head + 1) * HDIM)
            query_head, key_head, grad_head = q_ref[:, cols], k_ref[:, cols], grad_ref[:, cols]
            chance = cross_softmax(query_head, key_head, item_ref[...])
            grad_chance = dot(v_ref[:, cols], grad_head, 1, 1)
            inner = jnp.sum(chance * grad_chance, axis=0, keepdims=True)
            grad_scores = (chance * (grad_chance - inner)).astype(jnp.bfloat16)
            grad_queries.append(dot(key_head, grad_scores, 0, 0))
            dk_ref[:, cols] = (dot(grad_scores, query_head, 1, 0) * scaling).astype(jnp.bfloat16)
            dv_ref[:, cols] = dot(chance.astype(jnp.bfloat16), grad_head, 1, 0).astype(
                jnp.bfloat16
            )
        dq_ref[...] = (jnp.concatenate(grad_queries).T * scaling).astype(jnp.bfloat16)

    rows, keys = queries.shape[0], key_rows.shape[0]
    return cross_call(
        body, (queries, key_rows, value_rows, grad_mixed), item_row, [rows, keys, keys], 10
    )


def feed_block(normed, grads, gate_up, down, number, count, held):
    rows, width = normed.shape
    units = down.shape[0]
    steps = 3
    tile = units // steps

    def body(x_ref, g_ref, gate_ref, up_ref, down_ref, *rest):
        act_ref, dgate_ref, dup_ref, out_ref, dx_ref, out_sum, dx_sum = rest[-7:]
        step = pl.program_id(0)
        values, grad_rows = x_ref[...], g_ref[...]
        gate = dot(values, gate_ref[...], 1, 1)
        up = dot(values, up_ref[...], 1, 1)
        grad_act = dot(grad_rows, down_ref[...], 1, 1)
        chance = jax.nn.sigmoid(gate)
        silu = gate * chance
        act = (silu * up).astype(jnp.bfloat16)
        grad_gate = (grad_act * up * (chance + silu * (1.0 - chance))).astype(jnp.bfloat16)
        grad_up = (grad_act * silu).astype(jnp.bfloat16)
        act_ref[...] = act
        dgate_ref[...] = grad_gate
        dup_ref[...] = grad_up
        out_part = dot(act, down_ref[...], 1, 0)
        dx_part = dot(grad_gate, gate_ref[...], 1, 0) + dot(grad_up, up_ref[...], 1, 0)

        @pl.when(step == 0)
        def _():
            out_sum[...] = out_part
            dx_sum[...] = dx_part

        @pl.when(step > 0)
        def _():
            out_sum[...] += out_part
            dx_sum[...] += dx_part

        @pl.when(step == steps - 1)
        def _():
            out_ref[...] = out_sum[...].astype(jnp.bfloat16)
            dx_ref[...] = dx_sum[...].astype(jnp.bfloat16)

    full = pl.BlockSpec((rows, width), lambda t: (0, 0))
    block = pl.BlockSpec((rows, tile), lambda t: (number, t))
    unit_shape = jax.ShapeDtypeStruct((rows * count, units), jnp.bfloat16)
    row_shape = jax.ShapeDtypeStruct((rows, width), jnp.bfloat16)
    held = [] if held is None else list(held)
    return pl.pallas_call(
        body,
        grid=(steps,),
        in_specs=[
            full,
            full,
            pl.BlockSpec((tile, width), lambda t: (t, 0)),
            pl.BlockSpec((tile, width), lambda t: (steps + t, 0)),
            pl.BlockSpec((tile, width), lambda t: (t, 0)),
        ]
        + [pl.BlockSpec(memory_space=pl.ANY)] * len(held),
        out_specs=[block] * 3 + [full] * 2,
        out_shape=[unit_shape] * 3 + [row_shape] * 2,
        scratch_shapes=[pltpu.VMEM((rows, width), jnp.float32)] * 2,
        input_output_aliases={5 + n: n for n in range(len(held))},
        compiler_params=pltpu.CompilerParams(vmem_limit_bytes=40 << 20),
        cost_estimate=taking(4),
    )(normed, grads, gate_up, gate_up, down, *held)


def unit_products(units, norms, grads, core, arrived=None):
    seq_size, (block, width) = len(norms), norms[0].shape
    length, count = units[0].shape
    steps = 3
    tile = count // (2 * steps)

    def body(*refs):
        unit_refs, refs = refs[:3], refs[3:]
        norm_refs, grad_refs, refs = refs[:seq_size], refs[seq_size : 2 * seq_size], refs[2 * seq_size :]
        out_ref, all_norms, all_grads = refs[-3:]

        @pl.when(pl.program_id(0) == 0)
        def _():
            for k in range(seq_size):
                rows = slice(k * block, (k + 1) * block)
                all_norms[rows, :] = norm_refs[k][...]
                all_grads[rows, :] = grad_refs[k][...]

        for kind in range(3):
            rows = (all_grads if kind == 2 else all_norms)[...]
            total = dot(unit_refs[kind][...], rows, 0, 0)
            if arrived is not None:
                total += refs[0][kind].astype(jnp.float32)
            out_ref[kind] = total.astype(jnp.bfloat16)

    out_block = pl.BlockSpec((3, tile, width), lambda t: (0, t, 0))
    extra = [] if arrived is None else [arrived]
    return pl.pallas_call(
        body,
        grid=(steps,),
        in_specs=[pl.BlockSpec((length, tile), lambda t: (0, core * steps + t))] * 3
        + [pl.BlockSpec((block, width), lambda t: (0, 0))] * (2 * seq_size)
        + [out_block] * len(extra),
        out_specs=out_block,
        out_shape=jax.ShapeDtypeStruct((3, count // 2, width), jnp.bfloat16),
        scratch_shapes=[pltpu.VMEM((length, width), jnp.bfloat16)] * 2,
        compiler_params=pltpu.CompilerParams(vmem_limit_bytes=56 << 20),
        cost_estimate=taking(5),
    )(*units, *norms, *grads, *extra)


def weight_products(lefts, rights, slot=0, slots=1, held=None):
    dp_size = lax.axis_size("dp")
    y_size = dp_size // 4
    rows, height = lefts[0].shape
    columns = rights[0].shape[1]
    tile = 3 * LANES
    place_rows = height // dp_size
    half_rows = place_rows * len(rights) // 2
    per_step = tile // place_rows

    def body(*refs):
        left_refs, refs = refs[: len(lefts)], refs[len(lefts) :]
        right_refs, (own_ref, other_ref, product) = refs[: len(rights)], refs[-3:]
        dp_place = lax.axis_index("dp")
        step = pl.program_id(0)
        for number, right_ref in enumerate(right_refs):
            total = None
            for k, left_ref in enumerate(left_refs):
                term = dot(left_ref[...], right_ref[k * rows : (k + 1) * rows, :], 0, 0)
                total = term if total is None else total + term
            product[...] = total.astype(jnp.bfloat16)
            for chip in range(per_step // 2):
                chip_place = step * (per_step // 2) + chip
                y_back = lax.rem((dp_place >> 2) + y_size - (chip_place >> 1), y_size)
                x_back = ((dp_place >> 1) ^ chip_place) & 1
                for target, core in ((own_ref, dp_place & 1), (other_ref, 1 - (dp_place & 1))):
                    first_row = (2 * chip + core) * place_rows
                    for half in range(2 // len(rights)):
                        begin = pl.multiple_of(first_row + half * half_rows, 16)
                        target[0, number + half, y_back, x_back] = product[
                            pl.ds(begin, half_rows), :
                        ]

    whole = (1, 2, y_size, 2, half_rows, columns)
    out_block = pl.BlockSpec(whole, lambda t: (slot, 0, 0, 0, 0, 0))
    out_shape = jax.ShapeDtypeStruct((slots,) + whole[1:], jnp.bfloat16)
    held = [] if held is None else list(held)
    return pl.pallas_call(
        body,
        grid=(height // tile,),
        in_specs=[pl.BlockSpec((rows, tile), lambda t: (0, t))] * len(lefts)
        + [pl.BlockSpec(r.shape, lambda t: (0, 0)) for r in rights]
        + [pl.BlockSpec(memory_space=pl.ANY)] * len(held),
        out_specs=[out_block] * 2,
        out_shape=[out_shape] * 2,
        scratch_shapes=[pltpu.VMEM((tile, columns), jnp.bfloat16)],
        input_output_aliases={len(lefts) + len(rights) + n: n for n in range(len(held))},
        compiler_params=pltpu.CompilerParams(vmem_limit_bytes=40 << 20),
        cost_estimate=taking(1.5),
    )(*lefts, *rights, *held)


def swap_core(values):
    return lax.ppermute(values, "dp", [(d, d ^ 1) for d in range(lax.axis_size("dp"))])


def shift_dp(values, y, x):
    size = lax.axis_size("dp")
    return lax.ppermute(values, "dp", [(d, ((d + 4 * y) % size) ^ (2 * x)) for d in range(size)])


def shift_seq(values, step=1):
    size = lax.axis_size("seq")
    return lax.ppermute(values, "seq", [(s, (s + step) % size) for s in range(size)])


def gather_rest(pieces):
    last = shift_seq(pieces[0], -1)
    pieces = list(pieces)
    for _ in range(lax.axis_size("seq") - 3):
        pieces.append(shift_seq(pieces[-1]))
    return pieces + [last]


def reduce_ahead(blocks):
    size = lax.axis_size("seq")
    total = blocks[size // 2 + 1]
    for k in range(size // 2 + 2, size):
        total = add_low(shift_seq(total), blocks[k])
    return total


def reduce_middle(total, blocks):
    for k in range(lax.axis_size("seq") // 2 - 1, 1, -1):
        total = shift_seq(add_low(total, blocks[k]), -1)
    return add_low(total, blocks[1])


def swap_seq(values):
    return lax.all_to_all(values, "seq", split_axis=0, concat_axis=0, tiled=True)


def gather_places(values):
    size = lax.axis_size("seq")
    return swap_seq(jnp.broadcast_to(values[None], (size,) + values.shape))


def add_wide(left, right):
    return left.astype(jnp.float32) + right.astype(jnp.float32)


def add_low(left, right):
    return add_wide(left, right).astype(jnp.bfloat16)


def stage(*values):
    return lax.optimization_barrier(values)


def spread_first(first, second):
    held = {(0, 0, 0): first, (1, 0, 0): second, (0, 0, 1): shift_dp(first, 0, 1)}
    for y in range(1, lax.axis_size("dp") // 4):
        held[1, y, 0] = shift_dp(held[1, y - 1, 0], 1, 0)
    return held


def spread_second(held):
    held = dict(held)
    for half, y, x in [(h, y, 0) for h, y, _ in held if h == 1]:
        held[half, y, 1] = shift_dp(held[half, y, x], 0, 1)
    for x in range(2):
        for y in range(1, lax.axis_size("dp") // 4):
            held[0, y, x] = shift_dp(held[0, y - 1, x], 1, 0)
    return held


def with_cores(plane):
    return {(core,) + p: swap_core(v) if core else v for core in range(2) for p, v in plane.items()}


def low(values):
    return values.astype(jnp.bfloat16)


def terms(own, arrived, *index):
    index = (slice(None),) + index
    values = own[index].astype(jnp.float32)
    return values if arrived is None else values + arrived[index].astype(jnp.float32)


def pack_first(own, arrived=None):
    y_size = own.shape[2]
    total = low(terms(own, arrived, 0, y_size - 1))
    for y in range(y_size - 2, 0, -1):
        total = low(shift_dp(total, -1, 0).astype(jnp.float32) + terms(own, arrived, 0, y))
    return total, low(terms(own, arrived, 1, slice(None), 1))


def send_first(packed):
    return shift_dp(packed[0], -1, 0), shift_dp(packed[1], 0, 1)


def add_first(came, own, arrived=None):
    return (
        low(came[0].astype(jnp.float32) + terms(own, arrived, 0, 0)),
        low(came[1].astype(jnp.float32) + terms(own, arrived, 1, slice(None), 0)),
    )


def pack_second(first, second):
    total = second[:, -1]
    for y in range(second.shape[1] - 2, 0, -1):
        total = add_low(shift_dp(total, -1, 0), second[:, y])
    return first[:, 1], total


def send_second(packed):
    return shift_dp(packed[0], 0, 1), shift_dp(packed[1], -1, 0)


def add_second(came, first, second):
    return add_wide(first[:, 0], came[0]), add_wide(second[:, 0], came[1])


def assemble(pieces, out_shapes, copies):
    count = len(pieces)

    def body(*refs):
        sources, targets = refs[:count], refs[count : count + len(out_shapes)]
        held, loaded, stored = refs[count + len(out_shapes) : -2], refs[-2], refs[-1]
        loads = [pltpu.make_async_copy(sources[n], held[n], loaded.at[n]) for n in range(count)]
        for load in loads:
            load.start()
        stores = []
        for n in range(count):
            loads[n].wait()
            for number, (piece, source, out, target) in enumerate(copies):
                if piece == n:
                    stores.append(
                        pltpu.make_async_copy(
                            held[n].at[source],
                            targets[out].at[target],
                            stored.at[number],
                        )
                    )
                    stores[-1].start()
        for store in stores:
            store.wait()

    return pl.pallas_call(
        body,
        out_shape=[jax.ShapeDtypeStruct(s, jnp.bfloat16) for s in out_shapes],
        in_specs=[pl.BlockSpec(memory_space=pl.ANY)] * count,
        out_specs=[pl.BlockSpec(memory_space=pl.ANY)] * len(out_shapes),
        scratch_shapes=[pltpu.VMEM(p.shape, p.dtype) for p in pieces]
        + [pltpu.SemaphoreType.DMA((count,)), pltpu.SemaphoreType.DMA((len(copies),))],
        compiler_params=pltpu.CompilerParams(vmem_limit_bytes=32 << 20),
        cost_estimate=taking(2),
    )(*pieces)


def local(
    tokens,
    context,
    item_lengths,
    gain_self,
    gain_cross,
    gain_feed,
    self_query,
    self_key,
    self_value,
    self_out,
    cross_query,
    cross_key,
    cross_value,
    cross_out,
    feed_gate,
    feed_up,
    feed_down,
    cotangent,
):
    rows_dev, width = tokens.shape
    dp_size, seq_size = lax.axis_size("dp"), lax.axis_size("seq")
    seq_place = lax.axis_index("seq")
    y_size = dp_size // 4
    head_width = HEADS // seq_size * HDIM
    pairs = -(-head_width // LANES)
    part_rows = self_query.shape[0]

    def whole_rows(rows):
        return lax.all_gather(rows, "dp", axis=0, tiled=False).reshape(-1, rows.shape[-1])

    qkv_parts = jnp.stack([self_query, self_key, self_value]).reshape(
        3, part_rows, seq_size, head_width
    )
    qkv_parts = jnp.pad(qkv_parts, ((0, 0),) * 3 + ((0, pairs * LANES - head_width),))
    qkv_parts = qkv_parts.reshape(3, part_rows, seq_size, pairs, LANES).transpose(2, 1, 3, 0, 4)
    qkv_parts = qkv_parts.reshape(seq_size, part_rows, pairs * 3 * LANES)
    qkv_parts, tokens, feed_gate, feed_up, feed_down, cotangent, item_lengths = stage(
        qkv_parts, tokens, feed_gate, feed_up, feed_down, cotangent, item_lengths
    )
    qkv_rows = swap_seq(qkv_parts)
    token_values = tokens.astype(jnp.float32)
    norm_one, norm_one_back = jax.vjp(layer_norm, token_values, gain_self.astype(jnp.float32))
    norm_one = norm_one.astype(jnp.bfloat16)
    feed_parts = jnp.stack([feed_gate, feed_up, feed_down])
    half_units = feed_parts.shape[1] // 2
    feed_parts = feed_parts[:, :half_units], feed_parts[:, half_units:]
    row_ids = jnp.concatenate(
        [
            lax.rem(seq_place + (seq_size - k), seq_size) * rows_dev
            + jnp.arange(rows_dev, dtype=jnp.int32)
            for k in range(seq_size)
        ]
    )
    segment, position = layout(item_lengths[0], row_ids)
    row_segment = segment[:rows_dev]
    tables = lane_tables(position)
    valid_rows = (row_segment < 2).astype(jnp.float32)[:, None]
    grad_output_low = (cotangent.astype(jnp.float32) * valid_rows).astype(jnp.bfloat16)
    qkv_rows, norm_one, feed_parts, self_out, cross_query = stage(
        qkv_rows, norm_one, feed_parts, self_out, cross_query
    )
    qkv_cols = whole_rows(qkv_rows)

    norms_one = [norm_one, shift_seq(norm_one)]
    out_rows = gather_places(self_out)
    feed_held = spread_first(*feed_parts)
    segments = segment[:, None], segment[None, :]
    (
        norms_one,
        tables,
        segments,
        feed_held,
        out_rows,
        cross_query,
        grad_output_low,
        cross_rows,
    ) = stage(
        norms_one,
        tables,
        segments,
        feed_held,
        out_rows,
        cross_query,
        grad_output_low,
        jnp.stack([jnp.concatenate([cross_key, cross_value]), cross_out]),
    )
    full_out = whole_rows(out_rows)

    norms_one = gather_rest(norms_one)
    query_rows = gather_places(cross_query)
    for y in range(1, y_size):
        feed_held[0, y, 0] = shift_dp(feed_held[0, y - 1, 0], 1, 0)
    feed_held[1, 0, 1] = shift_dp(feed_held[1, 0, 0], 0, 1)
    norms_one, qkv_cols, feed_held, cross_rows, query_rows, grad_output_low = stage(
        norms_one, qkv_cols, feed_held, cross_rows, query_rows, grad_output_low
    )
    full_cross_query = whole_rows(query_rows)

    cross_rows = gather_places(cross_rows)
    for y in range(1, y_size):
        feed_held[0, y, 1] = shift_dp(feed_held[0, y - 1, 1], 1, 0)
        feed_held[1, y, 1] = shift_dp(feed_held[1, y, 0], 0, 1)
    all_grads = [grad_output_low, shift_seq(grad_output_low)]
    qkv, head_attended, log_total = self_forward(norms_one, qkv_cols, tables, segments)
    cross_rows, feed_held, head_attended, all_grads = stage(
        cross_rows, feed_held, head_attended, all_grads
    )
    full_cross_kv = whole_rows(cross_rows[:, 0]).reshape(dp_size * seq_size, 2, -1, width)
    full_cross_out = whole_rows(cross_rows[:, 1])

    attended = swap_seq(head_attended[:, :head_width].reshape(seq_size, rows_dev, head_width))
    feed_cores = with_cores(feed_held)
    places = [
        (core, half, y, x)
        for core in range(2)
        for half in range(2)
        for y in range(y_size)
        for x in range(2)
    ]
    unit_gate_up, unit_down = assemble(
        [feed_cores[p] for p in places],
        [(2, len(places), half_units, width), (1, len(places), half_units, width)],
        [
            (n, (kind,), kind // 2, (kind % 2, n))
            for n in range(len(places))
            for kind in range(3)
        ],
    )
    unit_gate_up, unit_down = unit_gate_up.reshape(-1, width), unit_down.reshape(-1, width)
    attended, unit_gate_up, unit_down, all_grads = stage(
        attended, unit_gate_up, unit_down, all_grads
    )

    last_grad = shift_seq(all_grads[0], -1)
    attended = jnp.concatenate([attended[s] for s in range(seq_size)], axis=1)
    first_sum = token_values + matmul(attended, full_out)
    norm_two, norm_two_back = jax.vjp(layer_norm, first_sum, gain_cross.astype(jnp.float32))
    norm_two = norm_two.astype(jnp.bfloat16)
    cross_queries = matmul(norm_two, full_cross_query).astype(jnp.bfloat16)
    all_grads, last_grad, cross_queries = stage(all_grads, last_grad, cross_queries)

    for _ in range(seq_size - 3):
        all_grads.append(shift_seq(all_grads[-1]))
    all_grads.append(last_grad)
    memory = context[0].reshape(-1, context.shape[3])
    full_cross_key = full_cross_kv[:, 0].reshape(-1, width)
    full_cross_value = full_cross_kv[:, 1].reshape(-1, width)
    memory_keys = matmul(memory, full_cross_key).astype(jnp.bfloat16)
    memory_values = matmul(memory, full_cross_value).astype(jnp.bfloat16)
    item_row = (row_segment == 1).astype(jnp.int32)[None, :]
    cross_mixed = cross_forward(cross_queries, memory_keys, memory_values, item_row)
    second_sum = first_sum + matmul(cross_mixed, full_cross_out)
    norm_three, norm_three_back = jax.vjp(layer_norm, second_sum, gain_feed.astype(jnp.float32))
    norm_three = norm_three.astype(jnp.bfloat16)
    all_grads, norm_three = stage(all_grads, norm_three)

    held, feed_out, feed_dx, moving = None, {}, {}, None

    def run_block(k, held):
        *held, feed_out[k], feed_dx[k] = feed_block(
            norms[k], all_grads[k], unit_gate_up, unit_down, k, seq_size, held
        )
        return held

    norms = [norm_three, shift_seq(norm_three)]
    held = run_block(0, held)
    norms, all_grads, held, feed_out, feed_dx = stage(norms, all_grads, held, feed_out, feed_dx)
    for k in range(1, seq_size):
        if k + 1 < seq_size:
            norms.append(shift_seq(norms[-1]))
        arrived = None if k == 1 else shift_seq(moving)
        held = run_block(k, held)
        norms, arrived, held, feed_out, feed_dx = stage(norms, arrived, held, feed_out, feed_dx)
        moving = feed_dx[k] if k == 1 else add_low(arrived, feed_dx[k])
    activation, grad_gate, grad_up = held
    held = (grad_gate, grad_up, activation)
    arrived = shift_seq(moving)
    other_units = unit_products(held, norms, all_grads, 1)
    arrived, other_units, feed_out = stage(arrived, other_units, feed_out)
    other_units = swap_core(other_units)
    grad_norm_three = add_wide(arrived, feed_dx[0])

    def seq_blocks(first, second):
        blocks = jnp.concatenate([first.astype(jnp.bfloat16), second.astype(jnp.bfloat16)])
        return blocks.reshape(seq_size, part_rows, blocks.shape[1])

    feed_came = shift_seq(feed_out[seq_size // 2], -1)
    grad_output = cotangent.astype(jnp.float32) * valid_rows
    grad_second, grad_gain_feed = norm_three_back(grad_norm_three)
    grad_second = grad_second + grad_output
    second_low = grad_second.astype(jnp.bfloat16)
    grad_mixed = contract_cols(second_low, full_cross_out).astype(jnp.bfloat16)
    cross_out_own, cross_out_other = weight_products([cross_mixed], [second_low])
    cross_out_other = swap_core(cross_out_other)
    grad_cross_queries, grad_memory_keys, grad_memory_values = cross_backward(
        cross_queries, memory_keys, memory_values, grad_mixed, item_row
    )
    grad_norm_two = contract_cols(grad_cross_queries, full_cross_query)
    grad_first, grad_gain_cross = norm_two_back(grad_norm_two)
    grad_first = grad_first + grad_second
    first_low = grad_first.astype(jnp.bfloat16)
    grad_attended = contract_cols(first_low, full_out).astype(jnp.bfloat16)
    grad_attended = jnp.stack(
        [grad_attended[:, s * head_width : (s + 1) * head_width] for s in range(seq_size)]
    )
    products = weight_products([norm_two], [grad_cross_queries], 0, 3)
    products = weight_products([attended], [first_low], 1, 3, products)
    weight_own, weight_other = weight_products(
        [memory], [grad_memory_keys, grad_memory_values], 2, 3, products
    )
    cross_out_packed = pack_first(cross_out_own, cross_out_other)
    feed_came, cross_out_packed, grad_attended, weight_other, other_units = stage(
        feed_came, cross_out_packed, grad_attended, weight_other, other_units
    )

    head_grad = swap_seq(grad_attended)
    cross_out_came = send_first(cross_out_packed)
    weight_other = swap_core(weight_other)
    own_units = unit_products(held, norms, all_grads, 0, other_units)
    head_grad, cross_out_came, weight_other, own_units = stage(
        head_grad, cross_out_came, weight_other, own_units
    )

    weight_packed = pack_first(weight_own, weight_other)
    cross_out_firsts = add_first(cross_out_came, cross_out_own, cross_out_other)
    head_grad = head_grad.reshape(rows_dev * seq_size, head_width)
    head_grad = jnp.pad(head_grad, ((0, 0), (0, pairs * LANES - head_width)))
    feed_moving = reduce_middle(feed_came, feed_out), reduce_ahead(feed_out)
    head_grad, weight_packed, feed_moving, cross_out_firsts = stage(
        head_grad, weight_packed, feed_moving, cross_out_firsts
    )
    feed_moving = shift_seq(feed_moving[0], -1), shift_seq(feed_moving[1])
    weight_came = send_first(weight_packed)
    turned = self_backward(qkv, head_grad, log_total, tables, segments, seq_size)
    weight_came, turned, feed_moving, cross_out_firsts = stage(
        weight_came, turned, feed_moving, cross_out_firsts
    )

    norm_terms = low(contract_cols(turned, qkv_cols))
    norm_terms = [norm_terms[k * rows_dev : (k + 1) * rows_dev] for k in range(seq_size)]
    norm_terms, turned, own_units, feed_moving = stage(norm_terms, turned, own_units, feed_moving)
    moving = shift_seq(norm_terms[seq_size // 2], -1), shift_seq(reduce_ahead(norm_terms))
    weight_firsts = add_first(weight_came, weight_own, weight_other)
    weight_firsts = [jnp.concatenate(pair) for pair in zip(weight_firsts, cross_out_firsts)]
    weight_packed = pack_second(*weight_firsts)
    weight_came = send_second(weight_packed)
    qkv_own, qkv_other = weight_products(norms_one, [turned])
    grad_gain_self = sum(
        jnp.sum(term.astype(jnp.float32) * norm.astype(jnp.float32), axis=0)
        for term, norm in zip(norm_terms, norms_one)
    ) / gain_self.astype(jnp.float32)
    gains = jnp.stack([grad_gain_self, grad_gain_cross, grad_gain_feed])
    gains = gains.reshape(-1, dp_size * seq_size, part_rows).transpose(1, 0, 2)
    gains = lax.all_to_all(gains, ("dp", "seq"), split_axis=0, concat_axis=0, tiled=True)
    moving, weight_came, qkv_own, qkv_other, gains = stage(
        moving, weight_came, qkv_own, qkv_other, gains
    )
    gains = jnp.sum(gains, axis=0)

    qkv_other = swap_core(qkv_other)
    norm_came = shift_seq(reduce_middle(moving[0], norm_terms), -1)
    own_units = own_units.reshape(3, 2, y_size, 2, half_units, width)
    unit_came = send_first(pack_first(own_units))
    weight_seconds = add_second(weight_came, *weight_firsts)
    placed = swap_seq(
        jnp.stack(
            [
                seq_blocks(*(s[n] for s in weight_seconds))
                for n in (3, 0, 1)
            ],
            axis=1,
        )
    )
    kv_blocks = jnp.stack(
        [low(s[2]).reshape(seq_size, -1, width) for s in weight_seconds], axis=1
    )
    qkv_came = send_first(pack_first(qkv_own, qkv_other))
    qkv_firsts = add_first(qkv_came, qkv_own, qkv_other)
    qkv_seconds = add_second(send_second(pack_second(*qkv_firsts)), *qkv_firsts)
    later = jnp.concatenate(
        [
            kv_blocks.reshape(seq_size, part_rows, width),
            seq_blocks(*(s[0] for s in qkv_seconds)),
        ],
        axis=2,
    )
    output = low(
        second_sum + add_wide(feed_moving[0], feed_out[0]) + feed_moving[1].astype(jnp.float32)
    )
    norm_came, placed, unit_came, later = stage(norm_came, placed, unit_came, later)

    later = swap_seq(later)
    unit_firsts = add_first(unit_came, own_units)
    unit_came = send_second(pack_second(*unit_firsts))
    grad_norm_one = add_wide(norm_came, norm_terms[0]) + moving[1].astype(jnp.float32)
    grad_tokens_wide = norm_one_back(grad_norm_one)[0]
    grad_tokens = low(grad_tokens_wide + grad_first)
    grad_cross_out, grad_cross_query, grad_self_out = (
        jnp.sum(placed[:, n].astype(jnp.float32), axis=0) for n in range(3)
    )
    unit_grads = jnp.concatenate(add_second(unit_came, *unit_firsts), axis=1)
    grad_cross_kv = jnp.sum(later[:, :, :width].astype(jnp.float32), axis=0)
    kv_rows = part_rows // 2
    grad_qkv = (
        later[:, :, width:]
        .reshape(seq_size, part_rows, pairs, 3, LANES)
        .transpose(3, 1, 0, 2, 4)
        .reshape(3, part_rows, seq_size, pairs * LANES)[..., :head_width]
        .reshape(3, part_rows, width)
        .astype(jnp.float32)
    )
    return (
        output,
        grad_tokens,
        gains[0],
        gains[1],
        gains[2],
        grad_qkv[0],
        grad_qkv[1],
        grad_qkv[2],
        grad_self_out,
        grad_cross_query,
        grad_cross_kv[:kv_rows],
        grad_cross_kv[kv_rows:],
        grad_cross_out,
        unit_grads[0],
        unit_grads[1],
        unit_grads[2],
    )


def solution(mesh):
    placed = (
        P(("dp", "seq"), None),
        P("dp", None, None, None),
        P("dp", None),
        P(),
        P(),
        P(),
        P(("dp", "seq"), None),
        P(("dp", "seq"), None),
        P(("dp", "seq"), None),
        P(("dp", "seq"), None),
        P(("dp", "seq"), None),
        P(("dp", "seq"), None),
        P(("dp", "seq"), None),
        P(("dp", "seq"), None),
        P(("dp", "seq"), None),
        P(("dp", "seq"), None),
        P(("dp", "seq"), None),
        P(("dp", "seq"), None),
    )
    return jax.shard_map(
        local,
        mesh=mesh,
        in_specs=placed,
        out_specs=(
            P(("dp", "seq"), None),
            P(("dp", "seq"), None),
            P(("dp", "seq")),
            P(("dp", "seq")),
            P(("dp", "seq")),
            P(("dp", "seq"), None),
            P(("dp", "seq"), None),
            P(("dp", "seq"), None),
            P(("dp", "seq"), None),
            P(("dp", "seq"), None),
            P(("dp", "seq"), None),
            P(("dp", "seq"), None),
            P(("dp", "seq"), None),
            P(("dp", "seq"), None),
            P(("dp", "seq"), None),
            P(("dp", "seq"), None),
        ),
        check_vma=False,
    )
```

```python
import jax
import jax.numpy as jnp
from jax import lax
from jax.experimental import pallas as pl
from jax.experimental.pallas import tpu as pltpu
from jax.sharding import PartitionSpec as P

HEADS = 24
HDIM = 64
ROT = 32


EPSILON = 1e-05
NEG_FILL = -1e30


def layer_norm(values, gain_vector):
    average = jnp.mean(values, axis=-1, keepdims=True)
    centered = values - average
    variance = jnp.mean(centered * centered, axis=-1, keepdims=True)
    return centered * lax.rsqrt(variance + EPSILON) * gain_vector


def layout(lengths, row_ids):
    first_end = lengths[0]
    second_end = lengths[0] + lengths[1]
    segment = jnp.where(row_ids < first_end, 0, jnp.where(row_ids < second_end, 1, 2)).astype(
        jnp.int32
    )
    seg_start = jnp.where(segment == 0, 0, jnp.where(segment == 1, first_end, second_end))
    return (segment, row_ids - seg_start)


def matmul(left, right):
    return jnp.dot(left, right, preferred_element_type=jnp.float32)


def contract_rows(left, right):
    return lax.dot_general(
        left, right, (((0,), (0,)), ((), ())), preferred_element_type=jnp.float32
    )


def contract_cols(left, right):
    return lax.dot_general(
        left, right, (((1,), (1,)), ((), ())), preferred_element_type=jnp.float32
    )


LANES = 128
PAIR = LANES // HDIM
LOG2E = 1.4426950408889634


def taking(microseconds):
    return pl.CostEstimate(
        flops=0, bytes_accessed=int(3e6 * microseconds), transcendentals=0
    )


def turn(values, cosine, sine_low, sine_high, sign):
    half_rot = ROT // 2
    ahead = pltpu.roll(values, LANES - half_rot, 1)
    behind = pltpu.roll(values, half_rot, 1)
    return values * cosine + sign * (behind * sine_high - ahead * sine_low)


def dot(left, right, left_dim, right_dim):
    return lax.dot_general(
        left, right, (((left_dim,), (right_dim,)), ((), ())), preferred_element_type=jnp.float32
    )


def lane_tables(position):
    half_rot = ROT // 2
    feature = jnp.arange(LANES, dtype=jnp.int32) % HDIM
    frequency = 10000.0 ** (-(feature % half_rot).astype(jnp.float32) / half_rot)
    angles = position.astype(jnp.float32)[:, None] * frequency[None, :]
    cosine = jnp.where(feature < ROT, jnp.cos(angles), 1.0)
    sine = jnp.sin(angles)
    return (
        cosine,
        jnp.where(feature < half_rot, sine, 0.0),
        jnp.where((feature >= half_rot) & (feature < ROT), sine, 0.0),
    )


def seq_distance_order(block, seq_size):
    place = lax.axis_index("seq")
    return lax.rem(place + (seq_size - block), seq_size)


def part(kind, head):
    return slice(kind * LANES + head * HDIM, kind * LANES + (head + 1) * HDIM)


def self_forward(norms, qkv_cols, tables, segments):
    seq_size, (block, width) = len(norms), norms[0].shape
    length = block * seq_size
    group = 3 * LANES
    pairs = qkv_cols.shape[1] // group
    scale = HDIM ** (-0.5) * LOG2E

    def body(*refs):
        norm_refs = refs[:seq_size]
        cols_ref, cos_ref, low_ref, high_ref, seg_col, seg_row, *outs = refs[seq_size:]
        qkv_out, mixed_ref, total_ref, exact_ref = outs
        for number in range(seq_size):
            rows = slice(number * block, (number + 1) * block)
            tables = cos_ref[rows], low_ref[rows], high_ref[rows]
            projected = dot(norm_refs[number][...], cols_ref[...], 1, 0)
            for kind in range(3):
                cols = slice(kind * LANES, (kind + 1) * LANES)
                values = projected[:, cols]
                if kind < 2:
                    values = turn(values, *tables, 1.0)
                qkv_out[rows, cols] = values.astype(jnp.bfloat16)
        for number in range(seq_size):
            rows = slice(number * block, (number + 1) * block)
            same = seg_col[...] == seg_row[:, rows]
            mixed = []
            for head in range(PAIR):
                scores = dot(qkv_out[:, part(1, head)], qkv_out[rows, part(0, head)], 1, 1)
                scores = jnp.where(same, scores, NEG_FILL)
                highest = jnp.max(scores, axis=0, keepdims=True)
                raised = jnp.exp2((scores - highest) * scale)
                total = jnp.sum(raised, axis=0, keepdims=True)
                mixed.append(dot(qkv_out[:, part(2, head)], raised.astype(jnp.bfloat16), 0, 0) / total)
                total_ref[0, head : head + 1, rows] = highest * scale + jnp.log2(total)
            place = seq_distance_order(number, seq_size)
            target = pl.ds(pl.multiple_of(place * block, block), block)
            mixed = jnp.concatenate(mixed)
            exact_ref[0, :, rows] = mixed
            mixed_ref[target, :] = mixed.T.astype(jnp.bfloat16)

    whole = pl.BlockSpec((length, LANES), lambda p: (0, 0))
    return pl.pallas_call(
        body,
        grid=(pairs,),
        in_specs=[pl.BlockSpec((block, width), lambda p: (0, 0))] * seq_size
        + [pl.BlockSpec((width, group), lambda p: (0, p))]
        + [whole] * 3
        + [
            pl.BlockSpec((length, 1), lambda p: (0, 0)),
            pl.BlockSpec((1, length), lambda p: (0, 0)),
        ],
        out_specs=[
            pl.BlockSpec((length, group), lambda p: (0, p)),
            pl.BlockSpec((length, LANES), lambda p: (0, p)),
            pl.BlockSpec((1, PAIR, length), lambda p: (p, 0, 0)),
            pl.BlockSpec((1, LANES, length), lambda p: (p, 0, 0)),
        ],
        out_shape=[
            jax.ShapeDtypeStruct((length, pairs * group), jnp.bfloat16),
            jax.ShapeDtypeStruct((length, pairs * LANES), jnp.bfloat16),
            jax.ShapeDtypeStruct((pairs, PAIR, length), jnp.float32),
            jax.ShapeDtypeStruct((pairs, LANES, length), jnp.float32),
        ],
        compiler_params=pltpu.CompilerParams(vmem_limit_bytes=40 << 20),
        cost_estimate=taking(8),
    )(*norms, qkv_cols, *tables, *segments)


def self_backward(qkv, grad_out, log_total, exact, tables, segments, seq_size):
    length = qkv.shape[0]
    group = 3 * LANES
    pairs = qkv.shape[1] // group
    block = length // seq_size
    scaling = HDIM ** (-0.5)
    scale = scaling * LOG2E

    def body(qkv_ref, grad_ref, total_ref, exact_ref, *rest):
        cos_ref, low_ref, high_ref, seg_col, seg_row, out_ref, dk_sum, dv_sum = rest
        for number in range(seq_size):
            rows = slice(number * block, (number + 1) * block)
            same = seg_col[...] == seg_row[:, rows]
            place = seq_distance_order(number, seq_size)
            grads = grad_ref[pl.ds(pl.multiple_of(place * block, block), block), :]
            inner = grads.astype(jnp.float32).T * exact_ref[0, :, rows]
            grad_queries = []
            for head in range(PAIR):
                cols = slice(head * HDIM, (head + 1) * HDIM)
                head_inner = jnp.sum(inner[cols, :], axis=0, keepdims=True)
                grad_head = grads[:, cols]
                query_head = qkv_ref[rows, part(0, head)]
                key_head = qkv_ref[:, part(1, head)]
                scores = dot(key_head, query_head, 1, 1) * scale - total_ref[
                    0, head : head + 1, rows
                ]
                chance = jnp.exp2(jnp.where(same, scores, NEG_FILL))
                grad_chance = dot(qkv_ref[:, part(2, head)], grad_head, 1, 1)
                grad_scores = (chance * (grad_chance - head_inner)).astype(jnp.bfloat16)
                grad_queries.append(dot(key_head, grad_scores, 0, 0))
                grad_keys = dot(query_head, grad_scores, 0, 1)
                grad_values = dot(grad_head, chance.astype(jnp.bfloat16), 0, 1)
                if number == 0:
                    dk_sum[cols, :] = grad_keys
                    dv_sum[cols, :] = grad_values
                else:
                    dk_sum[cols, :] += grad_keys
                    dv_sum[cols, :] += grad_values
            tables = cos_ref[rows], low_ref[rows], high_ref[rows]
            turned = turn(jnp.concatenate(grad_queries).T * scaling, *tables, -1.0)
            out_ref[rows, :LANES] = turned.astype(jnp.bfloat16)
        tables = cos_ref[...], low_ref[...], high_ref[...]
        turned = turn(dk_sum[...].T * scaling, *tables, -1.0)
        out_ref[:, LANES : 2 * LANES] = turned.astype(jnp.bfloat16)
        out_ref[:, 2 * LANES :] = dv_sum[...].T.astype(jnp.bfloat16)

    whole = pl.BlockSpec((length, LANES), lambda p: (0, 0))
    return pl.pallas_call(
        body,
        grid=(pairs,),
        in_specs=[
            pl.BlockSpec((length, group), lambda p: (0, p)),
            pl.BlockSpec((length, LANES), lambda p: (0, p)),
            pl.BlockSpec((1, PAIR, length), lambda p: (p, 0, 0)),
            pl.BlockSpec((1, LANES, length), lambda p: (p, 0, 0)),
        ]
        + [whole] * 3
        + [
            pl.BlockSpec((length, 1), lambda p: (0, 0)),
            pl.BlockSpec((1, length), lambda p: (0, 0)),
        ],
        out_specs=pl.BlockSpec((length, group), lambda p: (0, p)),
        out_shape=jax.ShapeDtypeStruct(qkv.shape, jnp.bfloat16),
        scratch_shapes=[pltpu.VMEM((LANES, length), jnp.float32)] * 2,
        compiler_params=pltpu.CompilerParams(vmem_limit_bytes=40 << 20),
        cost_estimate=taking(7),
    )(qkv, grad_out, log_total, exact, *tables, *segments)


CROSS_HEADS = 8


def cross_softmax(queries, key_rows, item_row):
    scale = HDIM ** (-0.5) * LOG2E
    scores = dot(key_rows, queries, 1, 1)
    count = key_rows.shape[0]
    key_item = (lax.broadcasted_iota(jnp.int32, (count, 1), 0) >= count // 2).astype(jnp.int32)
    scores = jnp.where(key_item == item_row, scores, NEG_FILL)
    raised = jnp.exp2((scores - jnp.max(scores, axis=0, keepdims=True)) * scale)
    return raised / jnp.sum(raised, axis=0, keepdims=True)


def cross_call(body, arrays, item_row, out_rows, flops):
    width = arrays[0].shape[1]
    lanes = CROSS_HEADS * HDIM
    blocks = [pl.BlockSpec((a.shape[0], lanes), lambda p: (0, p)) for a in arrays]
    return pl.pallas_call(
        body,
        grid=(width // lanes,),
        in_specs=blocks + [pl.BlockSpec(item_row.shape, lambda p: (0, 0))],
        out_specs=[pl.BlockSpec((rows, lanes), lambda p: (0, p)) for rows in out_rows],
        out_shape=[jax.ShapeDtypeStruct((rows, width), jnp.bfloat16) for rows in out_rows],
        compiler_params=pltpu.CompilerParams(vmem_limit_bytes=32 << 20),
        cost_estimate=taking(4),
    )(*arrays, item_row)


def cross_forward(queries, key_rows, value_rows, item_row):
    def body(q_ref, k_ref, v_ref, item_ref, mixed_ref):
        mixed = []
        for head in range(CROSS_HEADS):
            cols = slice(head * HDIM, (head + 1) * HDIM)
            chance = cross_softmax(q_ref[:, cols], k_ref[:, cols], item_ref[...])
            mixed.append(dot(v_ref[:, cols], chance.astype(jnp.bfloat16), 0, 0))
        mixed_ref[...] = jnp.concatenate(mixed).T.astype(jnp.bfloat16)

    return cross_call(
        body, (queries, key_rows, value_rows), item_row, [queries.shape[0]], 4
    )[0]


def cross_backward(queries, key_rows, value_rows, grad_mixed, item_row):
    scaling = HDIM ** (-0.5)

    def body(q_ref, k_ref, v_ref, grad_ref, item_ref, dq_ref, dk_ref, dv_ref):
        grad_queries = []
        for head in range(CROSS_HEADS):
            cols = slice(head * HDIM, (head + 1) * HDIM)
            query_head, key_head, grad_head = q_ref[:, cols], k_ref[:, cols], grad_ref[:, cols]
            chance = cross_softmax(query_head, key_head, item_ref[...])
            grad_chance = dot(v_ref[:, cols], grad_head, 1, 1)
            inner = jnp.sum(chance * grad_chance, axis=0, keepdims=True)
            grad_scores = (chance * (grad_chance - inner)).astype(jnp.bfloat16)
            grad_queries.append(dot(key_head, grad_scores, 0, 0))
            dk_ref[:, cols] = (dot(grad_scores, query_head, 1, 0) * scaling).astype(jnp.bfloat16)
            dv_ref[:, cols] = dot(chance.astype(jnp.bfloat16), grad_head, 1, 0).astype(
                jnp.bfloat16
            )
        dq_ref[...] = (jnp.concatenate(grad_queries).T * scaling).astype(jnp.bfloat16)

    rows, keys = queries.shape[0], key_rows.shape[0]
    return cross_call(
        body, (queries, key_rows, value_rows, grad_mixed), item_row, [rows, keys, keys], 10
    )


def feed_block(normed, grads, gate_up, down, number, count, held):
    rows, width = normed.shape
    units = down.shape[0]
    steps = 3
    tile = units // steps

    def body(x_ref, g_ref, gate_ref, up_ref, down_ref, *rest):
        act_ref, dgate_ref, dup_ref, out_ref, dx_ref, out_sum, dx_sum = rest[-7:]
        step = pl.program_id(0)
        values, grad_rows = x_ref[...], g_ref[...]
        gate = dot(values, gate_ref[...], 1, 1)
        up = dot(values, up_ref[...], 1, 1)
        grad_act = dot(grad_rows, down_ref[...], 1, 1)
        chance = jax.nn.sigmoid(gate)
        silu = gate * chance
        act = (silu * up).astype(jnp.bfloat16)
        grad_gate = (grad_act * up * (chance + silu * (1.0 - chance))).astype(jnp.bfloat16)
        grad_up = (grad_act * silu).astype(jnp.bfloat16)
        act_ref[...] = act
        dgate_ref[...] = grad_gate
        dup_ref[...] = grad_up
        out_part = dot(act, down_ref[...], 1, 0)
        dx_part = dot(grad_gate, gate_ref[...], 1, 0) + dot(grad_up, up_ref[...], 1, 0)

        @pl.when(step == 0)
        def _():
            out_sum[...] = out_part
            dx_sum[...] = dx_part

        @pl.when(step > 0)
        def _():
            out_sum[...] += out_part
            dx_sum[...] += dx_part

        @pl.when(step == steps - 1)
        def _():
            out_ref[...] = out_sum[...].astype(jnp.bfloat16)
            dx_ref[...] = dx_sum[...].astype(jnp.bfloat16)

    full = pl.BlockSpec((rows, width), lambda t: (0, 0))
    block = pl.BlockSpec((rows, tile), lambda t: (number, t))
    unit_shape = jax.ShapeDtypeStruct((rows * count, units), jnp.bfloat16)
    row_shape = jax.ShapeDtypeStruct((rows, width), jnp.bfloat16)
    held = [] if held is None else list(held)
    return pl.pallas_call(
        body,
        grid=(steps,),
        in_specs=[
            full,
            full,
            pl.BlockSpec((tile, width), lambda t: (t, 0)),
            pl.BlockSpec((tile, width), lambda t: (steps + t, 0)),
            pl.BlockSpec((tile, width), lambda t: (t, 0)),
        ]
        + [pl.BlockSpec(memory_space=pl.ANY)] * len(held),
        out_specs=[block] * 3 + [full] * 2,
        out_shape=[unit_shape] * 3 + [row_shape] * 2,
        scratch_shapes=[pltpu.VMEM((rows, width), jnp.float32)] * 2,
        input_output_aliases={5 + n: n for n in range(len(held))},
        compiler_params=pltpu.CompilerParams(vmem_limit_bytes=40 << 20),
        cost_estimate=taking(4),
    )(normed, grads, gate_up, gate_up, down, *held)


def unit_products(units, norms, grads, core, arrived=None):
    seq_size, (block, width) = len(norms), norms[0].shape
    length, count = units[0].shape
    steps = 3
    tile = count // (2 * steps)

    def body(*refs):
        unit_refs, refs = refs[:3], refs[3:]
        norm_refs, grad_refs, refs = refs[:seq_size], refs[seq_size : 2 * seq_size], refs[2 * seq_size :]
        out_ref, all_norms, all_grads = refs[-3:]

        @pl.when(pl.program_id(0) == 0)
        def _():
            for k in range(seq_size):
                rows = slice(k * block, (k + 1) * block)
                all_norms[rows, :] = norm_refs[k][...]
                all_grads[rows, :] = grad_refs[k][...]

        for kind in range(3):
            rows = (all_grads if kind == 2 else all_norms)[...]
            total = dot(unit_refs[kind][...], rows, 0, 0)
            if arrived is not None:
                total += refs[0][kind].astype(jnp.float32)
            out_ref[kind] = total.astype(jnp.bfloat16)

    out_block = pl.BlockSpec((3, tile, width), lambda t: (0, t, 0))
    extra = [] if arrived is None else [arrived]
    return pl.pallas_call(
        body,
        grid=(steps,),
        in_specs=[pl.BlockSpec((length, tile), lambda t: (0, core * steps + t))] * 3
        + [pl.BlockSpec((block, width), lambda t: (0, 0))] * (2 * seq_size)
        + [out_block] * len(extra),
        out_specs=out_block,
        out_shape=jax.ShapeDtypeStruct((3, count // 2, width), jnp.bfloat16),
        scratch_shapes=[pltpu.VMEM((length, width), jnp.bfloat16)] * 2,
        compiler_params=pltpu.CompilerParams(vmem_limit_bytes=56 << 20),
        cost_estimate=taking(5),
    )(*units, *norms, *grads, *extra)


def weight_products(lefts, rights, slot=0, slots=1, held=None):
    dp_size = lax.axis_size("dp")
    y_size = dp_size // 4
    rows, height = lefts[0].shape
    columns = rights[0].shape[1]
    tile = 3 * LANES
    place_rows = height // dp_size
    half_rows = place_rows * len(rights) // 2
    per_step = tile // place_rows

    def body(*refs):
        left_refs, refs = refs[: len(lefts)], refs[len(lefts) :]
        right_refs, (own_ref, other_ref, product) = refs[: len(rights)], refs[-3:]
        dp_place = lax.axis_index("dp")
        step = pl.program_id(0)
        for number, right_ref in enumerate(right_refs):
            total = None
            for k, left_ref in enumerate(left_refs):
                term = dot(left_ref[...], right_ref[k * rows : (k + 1) * rows, :], 0, 0)
                total = term if total is None else total + term
            product[...] = total.astype(jnp.bfloat16)
            for chip in range(per_step // 2):
                chip_place = step * (per_step // 2) + chip
                y_back = lax.rem((dp_place >> 2) + y_size - (chip_place >> 1), y_size)
                x_back = ((dp_place >> 1) ^ chip_place) & 1
                for target, core in ((own_ref, dp_place & 1), (other_ref, 1 - (dp_place & 1))):
                    first_row = (2 * chip + core) * place_rows
                    for half in range(2 // len(rights)):
                        begin = pl.multiple_of(first_row + half * half_rows, 16)
                        target[0, number + half, y_back, x_back] = product[
                            pl.ds(begin, half_rows), :
                        ]

    whole = (1, 2, y_size, 2, half_rows, columns)
    out_block = pl.BlockSpec(whole, lambda t: (slot, 0, 0, 0, 0, 0))
    out_shape = jax.ShapeDtypeStruct((slots,) + whole[1:], jnp.bfloat16)
    held = [] if held is None else list(held)
    return pl.pallas_call(
        body,
        grid=(height // tile,),
        in_specs=[pl.BlockSpec((rows, tile), lambda t: (0, t))] * len(lefts)
        + [pl.BlockSpec(r.shape, lambda t: (0, 0)) for r in rights]
        + [pl.BlockSpec(memory_space=pl.ANY)] * len(held),
        out_specs=[out_block] * 2,
        out_shape=[out_shape] * 2,
        scratch_shapes=[pltpu.VMEM((tile, columns), jnp.bfloat16)],
        input_output_aliases={len(lefts) + len(rights) + n: n for n in range(len(held))},
        compiler_params=pltpu.CompilerParams(vmem_limit_bytes=40 << 20),
        cost_estimate=taking(1.5),
    )(*lefts, *rights, *held)


def swap_core(values):
    return lax.ppermute(values, "dp", [(d, d ^ 1) for d in range(lax.axis_size("dp"))])


def shift_dp(values, y, x):
    size = lax.axis_size("dp")
    return lax.ppermute(values, "dp", [(d, ((d + 4 * y) % size) ^ (2 * x)) for d in range(size)])


def shift_seq(values, step=1):
    size = lax.axis_size("seq")
    return lax.ppermute(values, "seq", [(s, (s + step) % size) for s in range(size)])


def gather_rest(pieces):
    last = shift_seq(pieces[0], -1)
    pieces = list(pieces)
    for _ in range(lax.axis_size("seq") - 3):
        pieces.append(shift_seq(pieces[-1]))
    return pieces + [last]


def reduce_ahead(blocks):
    size = lax.axis_size("seq")
    total = blocks[size // 2 + 1]
    for k in range(size // 2 + 2, size):
        total = add_low(shift_seq(total), blocks[k])
    return total


def reduce_middle(total, blocks):
    for k in range(lax.axis_size("seq") // 2 - 1, 1, -1):
        total = shift_seq(add_low(total, blocks[k]), -1)
    return add_low(total, blocks[1])


def swap_seq(values):
    return lax.all_to_all(values, "seq", split_axis=0, concat_axis=0, tiled=True)


def gather_places(values):
    size = lax.axis_size("seq")
    return swap_seq(jnp.broadcast_to(values[None], (size,) + values.shape))


def add_wide(left, right):
    return left.astype(jnp.float32) + right.astype(jnp.float32)


def add_low(left, right):
    return add_wide(left, right).astype(jnp.bfloat16)


def stage(*values):
    return lax.optimization_barrier(values)


def spread_first(first, second):
    held = {(0, 0, 0): first, (1, 0, 0): second, (0, 0, 1): shift_dp(first, 0, 1)}
    for y in range(1, lax.axis_size("dp") // 4):
        held[1, y, 0] = shift_dp(held[1, y - 1, 0], 1, 0)
    return held


def spread_second(held):
    held = dict(held)
    for half, y, x in [(h, y, 0) for h, y, _ in held if h == 1]:
        held[half, y, 1] = shift_dp(held[half, y, x], 0, 1)
    for x in range(2):
        for y in range(1, lax.axis_size("dp") // 4):
            held[0, y, x] = shift_dp(held[0, y - 1, x], 1, 0)
    return held


def with_cores(plane):
    return {(core,) + p: swap_core(v) if core else v for core in range(2) for p, v in plane.items()}


def low(values):
    return values.astype(jnp.bfloat16)


def terms(own, arrived, *index):
    index = (slice(None),) + index
    values = own[index].astype(jnp.float32)
    return values if arrived is None else values + arrived[index].astype(jnp.float32)


def pack_first(own, arrived=None):
    y_size = own.shape[2]
    total = low(terms(own, arrived, 0, y_size - 1))
    for y in range(y_size - 2, 0, -1):
        total = low(shift_dp(total, -1, 0).astype(jnp.float32) + terms(own, arrived, 0, y))
    return total, low(terms(own, arrived, 1, slice(None), 1))


def send_first(packed):
    return shift_dp(packed[0], -1, 0), shift_dp(packed[1], 0, 1)


def add_first(came, own, arrived=None):
    return (
        low(came[0].astype(jnp.float32) + terms(own, arrived, 0, 0)),
        low(came[1].astype(jnp.float32) + terms(own, arrived, 1, slice(None), 0)),
    )


def pack_second(first, second):
    total = second[:, -1]
    for y in range(second.shape[1] - 2, 0, -1):
        total = add_low(shift_dp(total, -1, 0), second[:, y])
    return first[:, 1], total


def send_second(packed):
    return shift_dp(packed[0], 0, 1), shift_dp(packed[1], -1, 0)


def add_second(came, first, second):
    return add_wide(first[:, 0], came[0]), add_wide(second[:, 0], came[1])


def assemble(pieces, out_shapes, copies):
    count = len(pieces)

    def body(*refs):
        sources, targets = refs[:count], refs[count : count + len(out_shapes)]
        held, loaded, stored = refs[count + len(out_shapes) : -2], refs[-2], refs[-1]
        loads = [pltpu.make_async_copy(sources[n], held[n], loaded.at[n]) for n in range(count)]
        for load in loads:
            load.start()
        stores = []
        for n in range(count):
            loads[n].wait()
            for number, (piece, source, out, target) in enumerate(copies):
                if piece == n:
                    stores.append(
                        pltpu.make_async_copy(
                            held[n].at[source],
                            targets[out].at[target],
                            stored.at[number],
                        )
                    )
                    stores[-1].start()
        for store in stores:
            store.wait()

    return pl.pallas_call(
        body,
        out_shape=[jax.ShapeDtypeStruct(s, jnp.bfloat16) for s in out_shapes],
        in_specs=[pl.BlockSpec(memory_space=pl.ANY)] * count,
        out_specs=[pl.BlockSpec(memory_space=pl.ANY)] * len(out_shapes),
        scratch_shapes=[pltpu.VMEM(p.shape, p.dtype) for p in pieces]
        + [pltpu.SemaphoreType.DMA((count,)), pltpu.SemaphoreType.DMA((len(copies),))],
        compiler_params=pltpu.CompilerParams(vmem_limit_bytes=32 << 20),
        cost_estimate=taking(2),
    )(*pieces)


def local(
    tokens,
    context,
    item_lengths,
    gain_self,
    gain_cross,
    gain_feed,
    self_query,
    self_key,
    self_value,
    self_out,
    cross_query,
    cross_key,
    cross_value,
    cross_out,
    feed_gate,
    feed_up,
    feed_down,
    cotangent,
):
    rows_dev, width = tokens.shape
    dp_size, seq_size = lax.axis_size("dp"), lax.axis_size("seq")
    seq_place = lax.axis_index("seq")
    y_size = dp_size // 4
    head_width = HEADS // seq_size * HDIM
    pairs = -(-head_width // LANES)
    part_rows = self_query.shape[0]

    def whole_rows(rows):
        return lax.all_gather(rows, "dp", axis=0, tiled=False).reshape(-1, rows.shape[-1])

    qkv_parts = jnp.stack([self_query, self_key, self_value]).reshape(
        3, part_rows, seq_size, head_width
    )
    qkv_parts = jnp.pad(qkv_parts, ((0, 0),) * 3 + ((0, pairs * LANES - head_width),))
    qkv_parts = qkv_parts.reshape(3, part_rows, seq_size, pairs, LANES).transpose(2, 1, 3, 0, 4)
    qkv_parts = qkv_parts.reshape(seq_size, part_rows, pairs * 3 * LANES)
    qkv_parts, tokens, feed_gate, feed_up, feed_down, cotangent, item_lengths = stage(
        qkv_parts, tokens, feed_gate, feed_up, feed_down, cotangent, item_lengths
    )
    qkv_rows = swap_seq(qkv_parts)
    token_values = tokens.astype(jnp.float32)
    norm_one, norm_one_back = jax.vjp(layer_norm, token_values, gain_self.astype(jnp.float32))
    norm_one = norm_one.astype(jnp.bfloat16)
    feed_parts = jnp.stack([feed_gate, feed_up, feed_down])
    half_units = feed_parts.shape[1] // 2
    feed_parts = feed_parts[:, :half_units], feed_parts[:, half_units:]
    row_ids = jnp.concatenate(
        [
            lax.rem(seq_place + (seq_size - k), seq_size) * rows_dev
            + jnp.arange(rows_dev, dtype=jnp.int32)
            for k in range(seq_size)
        ]
    )
    segment, position = layout(item_lengths[0], row_ids)
    row_segment = segment[:rows_dev]
    tables = lane_tables(position)
    valid_rows = (row_segment < 2).astype(jnp.float32)[:, None]
    grad_output_low = (cotangent.astype(jnp.float32) * valid_rows).astype(jnp.bfloat16)
    qkv_rows, norm_one, feed_parts, self_out, cross_query = stage(
        qkv_rows, norm_one, feed_parts, self_out, cross_query
    )
    qkv_cols = whole_rows(qkv_rows)

    norms_one = [norm_one, shift_seq(norm_one)]
    out_rows = gather_places(self_out)
    feed_held = spread_first(*feed_parts)
    segments = segment[:, None], segment[None, :]
    (
        norms_one,
        tables,
        segments,
        feed_held,
        out_rows,
        cross_query,
        grad_output_low,
        cross_rows,
    ) = stage(
        norms_one,
        tables,
        segments,
        feed_held,
        out_rows,
        cross_query,
        grad_output_low,
        jnp.stack([jnp.concatenate([cross_key, cross_value]), cross_out]),
    )
    full_out = whole_rows(out_rows)

    norms_one = gather_rest(norms_one)
    query_rows = gather_places(cross_query)
    for y in range(1, y_size):
        feed_held[0, y, 0] = shift_dp(feed_held[0, y - 1, 0], 1, 0)
    feed_held[1, 0, 1] = shift_dp(feed_held[1, 0, 0], 0, 1)
    norms_one, qkv_cols, feed_held, cross_rows, query_rows, grad_output_low = stage(
        norms_one, qkv_cols, feed_held, cross_rows, query_rows, grad_output_low
    )
    full_cross_query = whole_rows(query_rows)

    cross_rows = gather_places(cross_rows)
    for y in range(1, y_size):
        feed_held[0, y, 1] = shift_dp(feed_held[0, y - 1, 1], 1, 0)
        feed_held[1, y, 1] = shift_dp(feed_held[1, y, 0], 0, 1)
    all_grads = [grad_output_low, shift_seq(grad_output_low)]
    qkv, head_attended, log_total, exact = self_forward(norms_one, qkv_cols, tables, segments)
    cross_rows, feed_held, head_attended, all_grads = stage(
        cross_rows, feed_held, head_attended, all_grads
    )
    full_cross_kv = whole_rows(cross_rows[:, 0]).reshape(dp_size * seq_size, 2, -1, width)
    full_cross_out = whole_rows(cross_rows[:, 1])

    attended = swap_seq(head_attended[:, :head_width].reshape(seq_size, rows_dev, head_width))
    feed_cores = with_cores(feed_held)
    places = [
        (core, half, y, x)
        for core in range(2)
        for half in range(2)
        for y in range(y_size)
        for x in range(2)
    ]
    unit_gate_up, unit_down = assemble(
        [feed_cores[p] for p in places],
        [(2, len(places), half_units, width), (1, len(places), half_units, width)],
        [
            (n, (kind,), kind // 2, (kind % 2, n))
            for n in range(len(places))
            for kind in range(3)
        ],
    )
    unit_gate_up, unit_down = unit_gate_up.reshape(-1, width), unit_down.reshape(-1, width)
    attended, unit_gate_up, unit_down, all_grads = stage(
        attended, unit_gate_up, unit_down, all_grads
    )

    last_grad = shift_seq(all_grads[0], -1)
    attended = jnp.concatenate([attended[s] for s in range(seq_size)], axis=1)
    first_sum = token_values + matmul(attended, full_out)
    norm_two, norm_two_back = jax.vjp(layer_norm, first_sum, gain_cross.astype(jnp.float32))
    norm_two = norm_two.astype(jnp.bfloat16)
    cross_queries = matmul(norm_two, full_cross_query).astype(jnp.bfloat16)
    all_grads, last_grad, cross_queries = stage(all_grads, last_grad, cross_queries)

    for _ in range(seq_size - 3):
        all_grads.append(shift_seq(all_grads[-1]))
    all_grads.append(last_grad)
    memory = context[0].reshape(-1, context.shape[3])
    full_cross_key = full_cross_kv[:, 0].reshape(-1, width)
    full_cross_value = full_cross_kv[:, 1].reshape(-1, width)
    memory_keys = matmul(memory, full_cross_key).astype(jnp.bfloat16)
    memory_values = matmul(memory, full_cross_value).astype(jnp.bfloat16)
    item_row = (row_segment == 1).astype(jnp.int32)[None, :]
    cross_mixed = cross_forward(cross_queries, memory_keys, memory_values, item_row)
    second_sum = first_sum + matmul(cross_mixed, full_cross_out)
    norm_three, norm_three_back = jax.vjp(layer_norm, second_sum, gain_feed.astype(jnp.float32))
    norm_three = norm_three.astype(jnp.bfloat16)
    all_grads, norm_three = stage(all_grads, norm_three)

    held, feed_out, feed_dx, moving = None, {}, {}, None

    def run_block(k, held):
        *held, feed_out[k], feed_dx[k] = feed_block(
            norms[k], all_grads[k], unit_gate_up, unit_down, k, seq_size, held
        )
        return held

    norms = [norm_three, shift_seq(norm_three)]
    held = run_block(0, held)
    norms, all_grads, held, feed_out, feed_dx = stage(norms, all_grads, held, feed_out, feed_dx)
    for k in range(1, seq_size):
        if k + 1 < seq_size:
            norms.append(shift_seq(norms[-1]))
        arrived = None if k == 1 else shift_seq(moving)
        held = run_block(k, held)
        norms, arrived, held, feed_out, feed_dx = stage(norms, arrived, held, feed_out, feed_dx)
        moving = feed_dx[k] if k == 1 else add_low(arrived, feed_dx[k])
    activation, grad_gate, grad_up = held
    held = (grad_gate, grad_up, activation)
    arrived = shift_seq(moving)
    other_units = unit_products(held, norms, all_grads, 1)
    arrived, other_units, feed_out = stage(arrived, other_units, feed_out)
    other_units = swap_core(other_units)
    grad_norm_three = add_wide(arrived, feed_dx[0])

    def seq_blocks(first, second):
        blocks = jnp.concatenate([first.astype(jnp.bfloat16), second.astype(jnp.bfloat16)])
        return blocks.reshape(seq_size, part_rows, blocks.shape[1])

    feed_came = shift_seq(feed_out[seq_size // 2], -1)
    grad_output = cotangent.astype(jnp.float32) * valid_rows
    grad_second, grad_gain_feed = norm_three_back(grad_norm_three)
    grad_second = grad_second + grad_output
    second_low = grad_second.astype(jnp.bfloat16)
    grad_mixed = contract_cols(second_low, full_cross_out).astype(jnp.bfloat16)
    cross_out_own, cross_out_other = weight_products([cross_mixed], [second_low])
    cross_out_other = swap_core(cross_out_other)
    grad_cross_queries, grad_memory_keys, grad_memory_values = cross_backward(
        cross_queries, memory_keys, memory_values, grad_mixed, item_row
    )
    grad_norm_two = contract_cols(grad_cross_queries, full_cross_query)
    grad_first, grad_gain_cross = norm_two_back(grad_norm_two)
    grad_first = grad_first + grad_second
    first_low = grad_first.astype(jnp.bfloat16)
    grad_attended = contract_cols(first_low, full_out).astype(jnp.bfloat16)
    grad_attended = jnp.stack(
        [grad_attended[:, s * head_width : (s + 1) * head_width] for s in range(seq_size)]
    )
    products = weight_products([norm_two], [grad_cross_queries], 0, 3)
    products = weight_products([attended], [first_low], 1, 3, products)
    weight_own, weight_other = weight_products(
        [memory], [grad_memory_keys, grad_memory_values], 2, 3, products
    )
    cross_out_packed = pack_first(cross_out_own, cross_out_other)
    feed_came, cross_out_packed, grad_attended, weight_other, other_units = stage(
        feed_came, cross_out_packed, grad_attended, weight_other, other_units
    )

    head_grad = swap_seq(grad_attended)
    cross_out_came = send_first(cross_out_packed)
    weight_other = swap_core(weight_other)
    own_units = unit_products(held, norms, all_grads, 0, other_units)
    head_grad, cross_out_came, weight_other, own_units = stage(
        head_grad, cross_out_came, weight_other, own_units
    )

    weight_packed = pack_first(weight_own, weight_other)
    head_grad = head_grad.reshape(rows_dev * seq_size, head_width)
    head_grad = jnp.pad(head_grad, ((0, 0), (0, pairs * LANES - head_width)))
    feed_moving = reduce_middle(feed_came, feed_out), reduce_ahead(feed_out)
    head_grad, weight_packed, feed_moving = stage(head_grad, weight_packed, feed_moving)
    feed_moving = shift_seq(feed_moving[0], -1), shift_seq(feed_moving[1])
    weight_came = send_first(weight_packed)
    turned = self_backward(qkv, head_grad, log_total, exact, tables, segments, seq_size)
    norm_terms = low(contract_cols(turned, qkv_cols))
    norm_terms = [norm_terms[k * rows_dev : (k + 1) * rows_dev] for k in range(seq_size)]
    qkv_own, qkv_other = weight_products(norms_one, [turned])
    weight_came, norm_terms, qkv_own, qkv_other, feed_moving, cross_out_came, own_units = stage(
        weight_came, norm_terms, qkv_own, qkv_other, feed_moving, cross_out_came, own_units
    )
    cross_out_firsts = add_first(cross_out_came, cross_out_own, cross_out_other)

    moving = shift_seq(norm_terms[seq_size // 2], -1), shift_seq(reduce_ahead(norm_terms))
    weight_firsts = add_first(weight_came, weight_own, weight_other)
    weight_firsts = [jnp.concatenate(pair) for pair in zip(weight_firsts, cross_out_firsts)]
    weight_packed = pack_second(*weight_firsts)
    weight_came = send_second(weight_packed)
    qkv_other = swap_core(qkv_other)
    grad_gain_self = sum(
        jnp.sum(term.astype(jnp.float32) * norm.astype(jnp.float32), axis=0)
        for term, norm in zip(norm_terms, norms_one)
    ) / gain_self.astype(jnp.float32)
    gains = jnp.stack([grad_gain_self, grad_gain_cross, grad_gain_feed])
    gains = gains.reshape(-1, dp_size * seq_size, part_rows).transpose(1, 0, 2)
    gains = lax.all_to_all(gains, ("dp", "seq"), split_axis=0, concat_axis=0, tiled=True)
    moving, weight_came, qkv_own, qkv_other, gains = stage(
        moving, weight_came, qkv_own, qkv_other, gains
    )
    gains = jnp.sum(gains, axis=0)

    norm_came = shift_seq(reduce_middle(moving[0], norm_terms), -1)
    own_units = own_units.reshape(3, 2, y_size, 2, half_units, width)
    unit_came = send_first(pack_first(own_units))
    weight_seconds = add_second(weight_came, *weight_firsts)
    placed = swap_seq(
        jnp.stack(
            [
                seq_blocks(*(s[n] for s in weight_seconds))
                for n in (3, 0, 1)
            ],
            axis=1,
        )
    )
    kv_blocks = jnp.stack(
        [low(s[2]).reshape(seq_size, -1, width) for s in weight_seconds], axis=1
    )
    qkv_came = send_first(pack_first(qkv_own, qkv_other))
    qkv_firsts = add_first(qkv_came, qkv_own, qkv_other)
    qkv_seconds = add_second(send_second(pack_second(*qkv_firsts)), *qkv_firsts)
    later = jnp.concatenate(
        [
            kv_blocks.reshape(seq_size, part_rows, width),
            seq_blocks(*(s[0] for s in qkv_seconds)),
        ],
        axis=2,
    )
    output = low(
        second_sum + add_wide(feed_moving[0], feed_out[0]) + feed_moving[1].astype(jnp.float32)
    )
    norm_came, placed, unit_came, later = stage(norm_came, placed, unit_came, later)

    later = swap_seq(later)
    unit_firsts = add_first(unit_came, own_units)
    unit_came = send_second(pack_second(*unit_firsts))
    grad_norm_one = add_wide(norm_came, norm_terms[0]) + moving[1].astype(jnp.float32)
    grad_tokens_wide = norm_one_back(grad_norm_one)[0]
    grad_tokens = low(grad_tokens_wide + grad_first)
    grad_cross_out, grad_cross_query, grad_self_out = (
        jnp.sum(placed[:, n].astype(jnp.float32), axis=0) for n in range(3)
    )
    unit_grads = jnp.concatenate(add_second(unit_came, *unit_firsts), axis=1)
    grad_cross_kv = jnp.sum(later[:, :, :width].astype(jnp.float32), axis=0)
    kv_rows = part_rows // 2
    grad_qkv = (
        later[:, :, width:]
        .reshape(seq_size, part_rows, pairs, 3, LANES)
        .transpose(3, 1, 0, 2, 4)
        .reshape(3, part_rows, seq_size, pairs * LANES)[..., :head_width]
        .reshape(3, part_rows, width)
        .astype(jnp.float32)
    )
    return (
        output,
        grad_tokens,
        gains[0],
        gains[1],
        gains[2],
        grad_qkv[0],
        grad_qkv[1],
        grad_qkv[2],
        grad_self_out,
        grad_cross_query,
        grad_cross_kv[:kv_rows],
        grad_cross_kv[kv_rows:],
        grad_cross_out,
        unit_grads[0],
        unit_grads[1],
        unit_grads[2],
    )


def solution(mesh):
    placed = (
        P(("dp", "seq"), None),
        P("dp", None, None, None),
        P("dp", None),
        P(),
        P(),
        P(),
        P(("dp", "seq"), None),
        P(("dp", "seq"), None),
        P(("dp", "seq"), None),
        P(("dp", "seq"), None),
        P(("dp", "seq"), None),
        P(("dp", "seq"), None),
        P(("dp", "seq"), None),
        P(("dp", "seq"), None),
        P(("dp", "seq"), None),
        P(("dp", "seq"), None),
        P(("dp", "seq"), None),
        P(("dp", "seq"), None),
    )
    return jax.shard_map(
        local,
        mesh=mesh,
        in_specs=placed,
        out_specs=(
            P(("dp", "seq"), None),
            P(("dp", "seq"), None),
            P(("dp", "seq")),
            P(("dp", "seq")),
            P(("dp", "seq")),
            P(("dp", "seq"), None),
            P(("dp", "seq"), None),
            P(("dp", "seq"), None),
            P(("dp", "seq"), None),
            P(("dp", "seq"), None),
            P(("dp", "seq"), None),
            P(("dp", "seq"), None),
            P(("dp", "seq"), None),
            P(("dp", "seq"), None),
            P(("dp", "seq"), None),
            P(("dp", "seq"), None),
        ),
        check_vma=False,
    )
```

```python
import jax
import jax.numpy as jnp
from jax import lax
from jax.experimental import pallas as pl
from jax.experimental.pallas import tpu as pltpu
from jax.sharding import PartitionSpec as P

HEADS = 24
HDIM = 64
ROT = 32


EPSILON = 1e-05
NEG_FILL = -1e30


def layer_norm(values, gain_vector):
    average = jnp.mean(values, axis=-1, keepdims=True)
    centered = values - average
    variance = jnp.mean(centered * centered, axis=-1, keepdims=True)
    return centered * lax.rsqrt(variance + EPSILON) * gain_vector


def layout(lengths, row_ids):
    first_end = lengths[0]
    second_end = lengths[0] + lengths[1]
    segment = jnp.where(row_ids < first_end, 0, jnp.where(row_ids < second_end, 1, 2)).astype(
        jnp.int32
    )
    seg_start = jnp.where(segment == 0, 0, jnp.where(segment == 1, first_end, second_end))
    return (segment, row_ids - seg_start)


def matmul(left, right):
    return jnp.dot(left, right, preferred_element_type=jnp.float32)


def contract_rows(left, right):
    return lax.dot_general(
        left, right, (((0,), (0,)), ((), ())), preferred_element_type=jnp.float32
    )


def contract_cols(left, right):
    return lax.dot_general(
        left, right, (((1,), (1,)), ((), ())), preferred_element_type=jnp.float32
    )


LANES = 128
PAIR = LANES // HDIM
LOG2E = 1.4426950408889634


def taking(microseconds):
    return pl.CostEstimate(
        flops=0, bytes_accessed=int(3e6 * microseconds), transcendentals=0
    )


def turn(values, cosine, sine_low, sine_high, sign):
    half_rot = ROT // 2
    ahead = pltpu.roll(values, LANES - half_rot, 1)
    behind = pltpu.roll(values, half_rot, 1)
    return values * cosine + sign * (behind * sine_high - ahead * sine_low)


def dot(left, right, left_dim, right_dim):
    return lax.dot_general(
        left, right, (((left_dim,), (right_dim,)), ((), ())), preferred_element_type=jnp.float32
    )


def lane_tables(position):
    half_rot = ROT // 2
    feature = jnp.arange(LANES, dtype=jnp.int32) % HDIM
    frequency = 10000.0 ** (-(feature % half_rot).astype(jnp.float32) / half_rot)
    angles = position.astype(jnp.float32)[:, None] * frequency[None, :]
    cosine = jnp.where(feature < ROT, jnp.cos(angles), 1.0)
    sine = jnp.sin(angles)
    return (
        cosine,
        jnp.where(feature < half_rot, sine, 0.0),
        jnp.where((feature >= half_rot) & (feature < ROT), sine, 0.0),
    )


def seq_distance_order(block, seq_size):
    place = lax.axis_index("seq")
    return lax.rem(place + (seq_size - block), seq_size)


def part(kind, head):
    return slice(kind * LANES + head * HDIM, kind * LANES + (head + 1) * HDIM)


def self_forward(norms, qkv_cols, tables, segments):
    seq_size, (block, width) = len(norms), norms[0].shape
    length = block * seq_size
    group = 3 * LANES
    pairs = qkv_cols.shape[1] // group
    scale = HDIM ** (-0.5) * LOG2E

    def body(*refs):
        norm_refs = refs[:seq_size]
        cols_ref, cos_ref, low_ref, high_ref, seg_col, seg_row, *outs = refs[seq_size:]
        qkv_out, mixed_ref, total_ref, exact_ref = outs
        for number in range(seq_size):
            rows = slice(number * block, (number + 1) * block)
            tables = cos_ref[rows], low_ref[rows], high_ref[rows]
            projected = dot(norm_refs[number][...], cols_ref[...], 1, 0)
            for kind in range(3):
                cols = slice(kind * LANES, (kind + 1) * LANES)
                values = projected[:, cols]
                if kind < 2:
                    values = turn(values, *tables, 1.0)
                qkv_out[rows, cols] = values.astype(jnp.bfloat16)
        for number in range(seq_size):
            rows = slice(number * block, (number + 1) * block)
            same = seg_col[...] == seg_row[:, rows]
            mixed = []
            for head in range(PAIR):
                scores = dot(qkv_out[:, part(1, head)], qkv_out[rows, part(0, head)], 1, 1)
                scores = jnp.where(same, scores, NEG_FILL)
                highest = jnp.max(scores, axis=0, keepdims=True)
                raised = jnp.exp2((scores - highest) * scale)
                total = jnp.sum(raised, axis=0, keepdims=True)
                mixed.append(dot(qkv_out[:, part(2, head)], raised.astype(jnp.bfloat16), 0, 0) / total)
                total_ref[0, head : head + 1, rows] = highest * scale + jnp.log2(total)
            place = seq_distance_order(number, seq_size)
            target = pl.ds(pl.multiple_of(place * block, block), block)
            mixed = jnp.concatenate(mixed)
            exact_ref[0, :, rows] = mixed
            mixed_ref[target, :] = mixed.T.astype(jnp.bfloat16)

    whole = pl.BlockSpec((length, LANES), lambda p: (0, 0))
    return pl.pallas_call(
        body,
        grid=(pairs,),
        in_specs=[pl.BlockSpec((block, width), lambda p: (0, 0))] * seq_size
        + [pl.BlockSpec((width, group), lambda p: (0, p))]
        + [whole] * 3
        + [
            pl.BlockSpec((length, 1), lambda p: (0, 0)),
            pl.BlockSpec((1, length), lambda p: (0, 0)),
        ],
        out_specs=[
            pl.BlockSpec((length, group), lambda p: (0, p)),
            pl.BlockSpec((length, LANES), lambda p: (0, p)),
            pl.BlockSpec((1, PAIR, length), lambda p: (p, 0, 0)),
            pl.BlockSpec((1, LANES, length), lambda p: (p, 0, 0)),
        ],
        out_shape=[
            jax.ShapeDtypeStruct((length, pairs * group), jnp.bfloat16),
            jax.ShapeDtypeStruct((length, pairs * LANES), jnp.bfloat16),
            jax.ShapeDtypeStruct((pairs, PAIR, length), jnp.float32),
            jax.ShapeDtypeStruct((pairs, LANES, length), jnp.float32),
        ],
        compiler_params=pltpu.CompilerParams(vmem_limit_bytes=40 << 20),
        cost_estimate=taking(8),
    )(*norms, qkv_cols, *tables, *segments)


def self_backward(qkv, grad_out, log_total, exact, tables, segments, seq_size):
    length = qkv.shape[0]
    group = 3 * LANES
    pairs = qkv.shape[1] // group
    block = length // seq_size
    scaling = HDIM ** (-0.5)
    scale = scaling * LOG2E

    def body(qkv_ref, grad_ref, total_ref, exact_ref, *rest):
        cos_ref, low_ref, high_ref, seg_col, seg_row, out_ref, dk_sum, dv_sum = rest
        for number in range(seq_size):
            rows = slice(number * block, (number + 1) * block)
            same = seg_col[...] == seg_row[:, rows]
            place = seq_distance_order(number, seq_size)
            grads = grad_ref[pl.ds(pl.multiple_of(place * block, block), block), :]
            inner = grads.astype(jnp.float32).T * exact_ref[0, :, rows]
            grad_queries = []
            for head in range(PAIR):
                cols = slice(head * HDIM, (head + 1) * HDIM)
                head_inner = jnp.sum(inner[cols, :], axis=0, keepdims=True)
                grad_head = grads[:, cols]
                query_head = qkv_ref[rows, part(0, head)]
                key_head = qkv_ref[:, part(1, head)]
                scores = dot(key_head, query_head, 1, 1) * scale - total_ref[
                    0, head : head + 1, rows
                ]
                chance = jnp.exp2(jnp.where(same, scores, NEG_FILL))
                grad_chance = dot(qkv_ref[:, part(2, head)], grad_head, 1, 1)
                grad_scores = (chance * (grad_chance - head_inner)).astype(jnp.bfloat16)
                grad_queries.append(dot(key_head, grad_scores, 0, 0))
                grad_keys = dot(query_head, grad_scores, 0, 1)
                grad_values = dot(grad_head, chance.astype(jnp.bfloat16), 0, 1)
                if number == 0:
                    dk_sum[cols, :] = grad_keys
                    dv_sum[cols, :] = grad_values
                else:
                    dk_sum[cols, :] += grad_keys
                    dv_sum[cols, :] += grad_values
            tables = cos_ref[rows], low_ref[rows], high_ref[rows]
            turned = turn(jnp.concatenate(grad_queries).T * scaling, *tables, -1.0)
            out_ref[rows, :LANES] = turned.astype(jnp.bfloat16)
        tables = cos_ref[...], low_ref[...], high_ref[...]
        turned = turn(dk_sum[...].T * scaling, *tables, -1.0)
        out_ref[:, LANES : 2 * LANES] = turned.astype(jnp.bfloat16)
        out_ref[:, 2 * LANES :] = dv_sum[...].T.astype(jnp.bfloat16)

    whole = pl.BlockSpec((length, LANES), lambda p: (0, 0))
    return pl.pallas_call(
        body,
        grid=(pairs,),
        in_specs=[
            pl.BlockSpec((length, group), lambda p: (0, p)),
            pl.BlockSpec((length, LANES), lambda p: (0, p)),
            pl.BlockSpec((1, PAIR, length), lambda p: (p, 0, 0)),
            pl.BlockSpec((1, LANES, length), lambda p: (p, 0, 0)),
        ]
        + [whole] * 3
        + [
            pl.BlockSpec((length, 1), lambda p: (0, 0)),
            pl.BlockSpec((1, length), lambda p: (0, 0)),
        ],
        out_specs=pl.BlockSpec((length, group), lambda p: (0, p)),
        out_shape=jax.ShapeDtypeStruct(qkv.shape, jnp.bfloat16),
        scratch_shapes=[pltpu.VMEM((LANES, length), jnp.float32)] * 2,
        compiler_params=pltpu.CompilerParams(vmem_limit_bytes=40 << 20),
        cost_estimate=taking(7),
    )(qkv, grad_out, log_total, exact, *tables, *segments)


CROSS_HEADS = 8


def cross_scores(queries, key_rows, item_row):
    scores = dot(key_rows, queries, 1, 1)
    count = key_rows.shape[0]
    key_item = (lax.broadcasted_iota(jnp.int32, (count, 1), 0) >= count // 2).astype(jnp.int32)
    return jnp.where(key_item == item_row, scores, NEG_FILL)


def cross_forward(queries, key_rows, value_rows, item_row):
    scale = HDIM ** (-0.5) * LOG2E

    def body(q_ref, k_ref, v_ref, item_ref, mixed_ref, total_ref, exact_ref):
        mixed = []
        for head in range(CROSS_HEADS):
            cols = slice(head * HDIM, (head + 1) * HDIM)
            scores = cross_scores(q_ref[:, cols], k_ref[:, cols], item_ref[...])
            highest = jnp.max(scores, axis=0, keepdims=True)
            raised = jnp.exp2((scores - highest) * scale)
            total = jnp.sum(raised, axis=0, keepdims=True)
            mixed.append(dot(v_ref[:, cols], raised.astype(jnp.bfloat16), 0, 0) / total)
            total_ref[0, head : head + 1, :] = highest * scale + jnp.log2(total)
        mixed = jnp.concatenate(mixed)
        exact_ref[...] = mixed
        mixed_ref[...] = mixed.T.astype(jnp.bfloat16)

    (rows, width), keys = queries.shape, key_rows.shape[0]
    lanes = CROSS_HEADS * HDIM
    steps = width // lanes
    return pl.pallas_call(
        body,
        grid=(steps,),
        in_specs=[pl.BlockSpec((n, lanes), lambda p: (0, p)) for n in (rows, keys, keys)]
        + [pl.BlockSpec(item_row.shape, lambda p: (0, 0))],
        out_specs=[
            pl.BlockSpec((rows, lanes), lambda p: (0, p)),
            pl.BlockSpec((1, CROSS_HEADS, rows), lambda p: (p, 0, 0)),
            pl.BlockSpec((lanes, rows), lambda p: (p, 0)),
        ],
        out_shape=[
            jax.ShapeDtypeStruct((rows, width), jnp.bfloat16),
            jax.ShapeDtypeStruct((steps, CROSS_HEADS, rows), jnp.float32),
            jax.ShapeDtypeStruct((width, rows), jnp.float32),
        ],
        compiler_params=pltpu.CompilerParams(vmem_limit_bytes=32 << 20),
        cost_estimate=taking(4),
    )(queries, key_rows, value_rows, item_row)


def cross_backward(queries, key_rows, value_rows, grad_mixed, item_row, log_total, exact):
    scaling = HDIM ** (-0.5)
    scale = scaling * LOG2E

    def body(q_ref, k_ref, v_ref, grad_ref, item_ref, total_ref, exact_ref, dq_ref, dk_ref, dv_ref):
        grad_queries = []
        inner = grad_ref[...].astype(jnp.float32).T * exact_ref[...]
        for head in range(CROSS_HEADS):
            cols = slice(head * HDIM, (head + 1) * HDIM)
            query_head, key_head, grad_head = q_ref[:, cols], k_ref[:, cols], grad_ref[:, cols]
            scores = cross_scores(query_head, key_head, item_ref[...])
            chance = jnp.exp2(scores * scale - total_ref[0, head : head + 1, :])
            grad_chance = dot(v_ref[:, cols], grad_head, 1, 1)
            head_inner = jnp.sum(inner[cols, :], axis=0, keepdims=True)
            grad_scores = (chance * (grad_chance - head_inner)).astype(jnp.bfloat16)
            grad_queries.append(dot(key_head, grad_scores, 0, 0))
            dk_ref[:, cols] = (dot(grad_scores, query_head, 1, 0) * scaling).astype(jnp.bfloat16)
            dv_ref[:, cols] = dot(chance.astype(jnp.bfloat16), grad_head, 1, 0).astype(
                jnp.bfloat16
            )
        dq_ref[...] = (jnp.concatenate(grad_queries).T * scaling).astype(jnp.bfloat16)

    (rows, width), keys = queries.shape, key_rows.shape[0]
    lanes = CROSS_HEADS * HDIM
    sizes = (rows, keys, keys)
    return pl.pallas_call(
        body,
        grid=(width // lanes,),
        in_specs=[pl.BlockSpec((n, lanes), lambda p: (0, p)) for n in sizes + (rows,)]
        + [
            pl.BlockSpec(item_row.shape, lambda p: (0, 0)),
            pl.BlockSpec((1, CROSS_HEADS, rows), lambda p: (p, 0, 0)),
            pl.BlockSpec((lanes, rows), lambda p: (p, 0)),
        ],
        out_specs=[pl.BlockSpec((n, lanes), lambda p: (0, p)) for n in sizes],
        out_shape=[jax.ShapeDtypeStruct((n, width), jnp.bfloat16) for n in sizes],
        compiler_params=pltpu.CompilerParams(vmem_limit_bytes=32 << 20),
        cost_estimate=taking(4),
    )(queries, key_rows, value_rows, grad_mixed, item_row, log_total, exact)


def feed_block(normed, grads, gate_up, down, number, count, held):
    rows, width = normed.shape
    units = down.shape[0]
    steps = 3
    tile = units // steps

    def body(x_ref, g_ref, gate_ref, up_ref, down_ref, *rest):
        act_ref, dgate_ref, dup_ref, out_ref, dx_ref, out_sum, dx_sum = rest[-7:]
        step = pl.program_id(0)
        values, grad_rows = x_ref[...], g_ref[...]
        gate = dot(values, gate_ref[...], 1, 1)
        up = dot(values, up_ref[...], 1, 1)
        grad_act = dot(grad_rows, down_ref[...], 1, 1)
        chance = jax.nn.sigmoid(gate)
        silu = gate * chance
        act = (silu * up).astype(jnp.bfloat16)
        grad_gate = (grad_act * up * (chance + silu * (1.0 - chance))).astype(jnp.bfloat16)
        grad_up = (grad_act * silu).astype(jnp.bfloat16)
        act_ref[...] = act
        dgate_ref[...] = grad_gate
        dup_ref[...] = grad_up
        out_part = dot(act, down_ref[...], 1, 0)
        dx_part = dot(grad_gate, gate_ref[...], 1, 0) + dot(grad_up, up_ref[...], 1, 0)

        @pl.when(step == 0)
        def _():
            out_sum[...] = out_part
            dx_sum[...] = dx_part

        @pl.when(step > 0)
        def _():
            out_sum[...] += out_part
            dx_sum[...] += dx_part

        @pl.when(step == steps - 1)
        def _():
            out_ref[...] = out_sum[...].astype(jnp.bfloat16)
            dx_ref[...] = dx_sum[...].astype(jnp.bfloat16)

    full = pl.BlockSpec((rows, width), lambda t: (0, 0))
    block = pl.BlockSpec((rows, tile), lambda t: (number, t))
    unit_shape = jax.ShapeDtypeStruct((rows * count, units), jnp.bfloat16)
    row_shape = jax.ShapeDtypeStruct((rows, width), jnp.bfloat16)
    held = [] if held is None else list(held)
    return pl.pallas_call(
        body,
        grid=(steps,),
        in_specs=[
            full,
            full,
            pl.BlockSpec((tile, width), lambda t: (t, 0)),
            pl.BlockSpec((tile, width), lambda t: (steps + t, 0)),
            pl.BlockSpec((tile, width), lambda t: (t, 0)),
        ]
        + [pl.BlockSpec(memory_space=pl.ANY)] * len(held),
        out_specs=[block] * 3 + [full] * 2,
        out_shape=[unit_shape] * 3 + [row_shape] * 2,
        scratch_shapes=[pltpu.VMEM((rows, width), jnp.float32)] * 2,
        input_output_aliases={5 + n: n for n in range(len(held))},
        compiler_params=pltpu.CompilerParams(vmem_limit_bytes=40 << 20),
        cost_estimate=taking(4),
    )(normed, grads, gate_up, gate_up, down, *held)


def unit_products(units, norms, grads, core, arrived=None):
    seq_size, (block, width) = len(norms), norms[0].shape
    length, count = units[0].shape
    steps = 3
    tile = count // (2 * steps)

    def body(*refs):
        unit_refs, refs = refs[:3], refs[3:]
        norm_refs, grad_refs, refs = refs[:seq_size], refs[seq_size : 2 * seq_size], refs[2 * seq_size :]
        out_ref, all_norms, all_grads = refs[-3:]

        @pl.when(pl.program_id(0) == 0)
        def _():
            for k in range(seq_size):
                rows = slice(k * block, (k + 1) * block)
                all_norms[rows, :] = norm_refs[k][...]
                all_grads[rows, :] = grad_refs[k][...]

        for kind in range(3):
            rows = (all_grads if kind == 2 else all_norms)[...]
            total = dot(unit_refs[kind][...], rows, 0, 0)
            if arrived is not None:
                total += refs[0][kind].astype(jnp.float32)
            out_ref[kind] = total.astype(jnp.bfloat16)

    out_block = pl.BlockSpec((3, tile, width), lambda t: (0, t, 0))
    extra = [] if arrived is None else [arrived]
    return pl.pallas_call(
        body,
        grid=(steps,),
        in_specs=[pl.BlockSpec((length, tile), lambda t: (0, core * steps + t))] * 3
        + [pl.BlockSpec((block, width), lambda t: (0, 0))] * (2 * seq_size)
        + [out_block] * len(extra),
        out_specs=out_block,
        out_shape=jax.ShapeDtypeStruct((3, count // 2, width), jnp.bfloat16),
        scratch_shapes=[pltpu.VMEM((length, width), jnp.bfloat16)] * 2,
        compiler_params=pltpu.CompilerParams(vmem_limit_bytes=56 << 20),
        cost_estimate=taking(5),
    )(*units, *norms, *grads, *extra)


def weight_products(lefts, rights, slot=0, slots=1, held=None):
    dp_size = lax.axis_size("dp")
    y_size = dp_size // 4
    rows, height = lefts[0].shape
    columns = rights[0].shape[1]
    tile = 3 * LANES
    place_rows = height // dp_size
    half_rows = place_rows * len(rights) // 2
    per_step = tile // place_rows

    def body(*refs):
        left_refs, refs = refs[: len(lefts)], refs[len(lefts) :]
        right_refs, (own_ref, other_ref, product) = refs[: len(rights)], refs[-3:]
        dp_place = lax.axis_index("dp")
        step = pl.program_id(0)
        for number, right_ref in enumerate(right_refs):
            total = None
            for k, left_ref in enumerate(left_refs):
                term = dot(left_ref[...], right_ref[k * rows : (k + 1) * rows, :], 0, 0)
                total = term if total is None else total + term
            product[...] = total.astype(jnp.bfloat16)
            for chip in range(per_step // 2):
                chip_place = step * (per_step // 2) + chip
                y_back = lax.rem((dp_place >> 2) + y_size - (chip_place >> 1), y_size)
                x_back = ((dp_place >> 1) ^ chip_place) & 1
                for target, core in ((own_ref, dp_place & 1), (other_ref, 1 - (dp_place & 1))):
                    first_row = (2 * chip + core) * place_rows
                    for half in range(2 // len(rights)):
                        begin = pl.multiple_of(first_row + half * half_rows, 16)
                        target[0, number + half, y_back, x_back] = product[
                            pl.ds(begin, half_rows), :
                        ]

    whole = (1, 2, y_size, 2, half_rows, columns)
    out_block = pl.BlockSpec(whole, lambda t: (slot, 0, 0, 0, 0, 0))
    out_shape = jax.ShapeDtypeStruct((slots,) + whole[1:], jnp.bfloat16)
    held = [] if held is None else list(held)
    return pl.pallas_call(
        body,
        grid=(height // tile,),
        in_specs=[pl.BlockSpec((rows, tile), lambda t: (0, t))] * len(lefts)
        + [pl.BlockSpec(r.shape, lambda t: (0, 0)) for r in rights]
        + [pl.BlockSpec(memory_space=pl.ANY)] * len(held),
        out_specs=[out_block] * 2,
        out_shape=[out_shape] * 2,
        scratch_shapes=[pltpu.VMEM((tile, columns), jnp.bfloat16)],
        input_output_aliases={len(lefts) + len(rights) + n: n for n in range(len(held))},
        compiler_params=pltpu.CompilerParams(vmem_limit_bytes=40 << 20),
        cost_estimate=taking(1.5),
    )(*lefts, *rights, *held)


def swap_core(values):
    return lax.ppermute(values, "dp", [(d, d ^ 1) for d in range(lax.axis_size("dp"))])


def shift_dp(values, y, x):
    size = lax.axis_size("dp")
    return lax.ppermute(values, "dp", [(d, ((d + 4 * y) % size) ^ (2 * x)) for d in range(size)])


def shift_seq(values, step=1):
    size = lax.axis_size("seq")
    return lax.ppermute(values, "seq", [(s, (s + step) % size) for s in range(size)])


def gather_rest(pieces):
    last = shift_seq(pieces[0], -1)
    pieces = list(pieces)
    for _ in range(lax.axis_size("seq") - 3):
        pieces.append(shift_seq(pieces[-1]))
    return pieces + [last]


def reduce_ahead(blocks):
    size = lax.axis_size("seq")
    total = blocks[size // 2 + 1]
    for k in range(size // 2 + 2, size):
        total = add_low(shift_seq(total), blocks[k])
    return total


def reduce_middle(total, blocks):
    for k in range(lax.axis_size("seq") // 2 - 1, 1, -1):
        total = shift_seq(add_low(total, blocks[k]), -1)
    return add_low(total, blocks[1])


def swap_seq(values):
    return lax.all_to_all(values, "seq", split_axis=0, concat_axis=0, tiled=True)


def gather_places(values):
    size = lax.axis_size("seq")
    return swap_seq(jnp.broadcast_to(values[None], (size,) + values.shape))


def add_wide(left, right):
    return left.astype(jnp.float32) + right.astype(jnp.float32)


def add_low(left, right):
    return add_wide(left, right).astype(jnp.bfloat16)


def stage(*values):
    return lax.optimization_barrier(values)


def spread_first(first, second):
    held = {(0, 0, 0): first, (1, 0, 0): second, (0, 0, 1): shift_dp(first, 0, 1)}
    for y in range(1, lax.axis_size("dp") // 4):
        held[1, y, 0] = shift_dp(held[1, y - 1, 0], 1, 0)
    return held


def spread_second(held):
    held = dict(held)
    for half, y, x in [(h, y, 0) for h, y, _ in held if h == 1]:
        held[half, y, 1] = shift_dp(held[half, y, x], 0, 1)
    for x in range(2):
        for y in range(1, lax.axis_size("dp") // 4):
            held[0, y, x] = shift_dp(held[0, y - 1, x], 1, 0)
    return held


def with_cores(plane):
    return {(core,) + p: swap_core(v) if core else v for core in range(2) for p, v in plane.items()}


def low(values):
    return values.astype(jnp.bfloat16)


def terms(own, arrived, *index):
    index = (slice(None),) + index
    values = own[index].astype(jnp.float32)
    return values if arrived is None else values + arrived[index].astype(jnp.float32)


def pack_first(own, arrived=None):
    y_size = own.shape[2]
    total = low(terms(own, arrived, 0, y_size - 1))
    for y in range(y_size - 2, 0, -1):
        total = low(shift_dp(total, -1, 0).astype(jnp.float32) + terms(own, arrived, 0, y))
    return total, low(terms(own, arrived, 1, slice(None), 1))


def send_first(packed):
    return shift_dp(packed[0], -1, 0), shift_dp(packed[1], 0, 1)


def add_first(came, own, arrived=None):
    return (
        low(came[0].astype(jnp.float32) + terms(own, arrived, 0, 0)),
        low(came[1].astype(jnp.float32) + terms(own, arrived, 1, slice(None), 0)),
    )


def pack_second(first, second):
    total = second[:, -1]
    for y in range(second.shape[1] - 2, 0, -1):
        total = add_low(shift_dp(total, -1, 0), second[:, y])
    return first[:, 1], total


def send_second(packed):
    return shift_dp(packed[0], 0, 1), shift_dp(packed[1], -1, 0)


def add_second(came, first, second):
    return add_wide(first[:, 0], came[0]), add_wide(second[:, 0], came[1])


def assemble(pieces, out_shapes, copies):
    count = len(pieces)

    def body(*refs):
        sources, targets = refs[:count], refs[count : count + len(out_shapes)]
        held, loaded, stored = refs[count + len(out_shapes) : -2], refs[-2], refs[-1]
        loads = [pltpu.make_async_copy(sources[n], held[n], loaded.at[n]) for n in range(count)]
        for load in loads:
            load.start()
        stores = []
        for n in range(count):
            loads[n].wait()
            for number, (piece, source, out, target) in enumerate(copies):
                if piece == n:
                    stores.append(
                        pltpu.make_async_copy(
                            held[n].at[source],
                            targets[out].at[target],
                            stored.at[number],
                        )
                    )
                    stores[-1].start()
        for store in stores:
            store.wait()

    return pl.pallas_call(
        body,
        out_shape=[jax.ShapeDtypeStruct(s, jnp.bfloat16) for s in out_shapes],
        in_specs=[pl.BlockSpec(memory_space=pl.ANY)] * count,
        out_specs=[pl.BlockSpec(memory_space=pl.ANY)] * len(out_shapes),
        scratch_shapes=[pltpu.VMEM(p.shape, p.dtype) for p in pieces]
        + [pltpu.SemaphoreType.DMA((count,)), pltpu.SemaphoreType.DMA((len(copies),))],
        compiler_params=pltpu.CompilerParams(vmem_limit_bytes=32 << 20),
        cost_estimate=taking(2),
    )(*pieces)


def local(
    tokens,
    context,
    item_lengths,
    gain_self,
    gain_cross,
    gain_feed,
    self_query,
    self_key,
    self_value,
    self_out,
    cross_query,
    cross_key,
    cross_value,
    cross_out,
    feed_gate,
    feed_up,
    feed_down,
    cotangent,
):
    rows_dev, width = tokens.shape
    dp_size, seq_size = lax.axis_size("dp"), lax.axis_size("seq")
    seq_place = lax.axis_index("seq")
    y_size = dp_size // 4
    head_width = HEADS // seq_size * HDIM
    pairs = -(-head_width // LANES)
    part_rows = self_query.shape[0]

    def whole_rows(rows):
        return lax.all_gather(rows, "dp", axis=0, tiled=False).reshape(-1, rows.shape[-1])

    qkv_parts = jnp.stack([self_query, self_key, self_value]).reshape(
        3, part_rows, seq_size, head_width
    )
    qkv_parts = jnp.pad(qkv_parts, ((0, 0),) * 3 + ((0, pairs * LANES - head_width),))
    qkv_parts = qkv_parts.reshape(3, part_rows, seq_size, pairs, LANES).transpose(2, 1, 3, 0, 4)
    qkv_parts = qkv_parts.reshape(seq_size, part_rows, pairs * 3 * LANES)
    qkv_parts, tokens, feed_gate, feed_up, feed_down, cotangent, item_lengths = stage(
        qkv_parts, tokens, feed_gate, feed_up, feed_down, cotangent, item_lengths
    )
    qkv_rows = swap_seq(qkv_parts)
    token_values = tokens.astype(jnp.float32)
    norm_one, norm_one_back = jax.vjp(layer_norm, token_values, gain_self.astype(jnp.float32))
    norm_one = norm_one.astype(jnp.bfloat16)
    feed_parts = jnp.stack([feed_gate, feed_up, feed_down])
    half_units = feed_parts.shape[1] // 2
    feed_parts = feed_parts[:, :half_units], feed_parts[:, half_units:]
    row_ids = jnp.concatenate(
        [
            lax.rem(seq_place + (seq_size - k), seq_size) * rows_dev
            + jnp.arange(rows_dev, dtype=jnp.int32)
            for k in range(seq_size)
        ]
    )
    segment, position = layout(item_lengths[0], row_ids)
    row_segment = segment[:rows_dev]
    tables = lane_tables(position)
    valid_rows = (row_segment < 2).astype(jnp.float32)[:, None]
    grad_output_low = (cotangent.astype(jnp.float32) * valid_rows).astype(jnp.bfloat16)
    qkv_rows, norm_one, feed_parts, self_out, cross_query = stage(
        qkv_rows, norm_one, feed_parts, self_out, cross_query
    )
    qkv_cols = whole_rows(qkv_rows)

    norms_one = [norm_one, shift_seq(norm_one)]
    out_rows = gather_places(self_out)
    feed_held = spread_first(*feed_parts)
    segments = segment[:, None], segment[None, :]
    (
        norms_one,
        tables,
        segments,
        feed_held,
        out_rows,
        cross_query,
        grad_output_low,
        cross_rows,
    ) = stage(
        norms_one,
        tables,
        segments,
        feed_held,
        out_rows,
        cross_query,
        grad_output_low,
        jnp.stack([jnp.concatenate([cross_key, cross_value]), cross_out]),
    )
    full_out = whole_rows(out_rows)

    norms_one = gather_rest(norms_one)
    query_rows = gather_places(cross_query)
    for y in range(1, y_size):
        feed_held[0, y, 0] = shift_dp(feed_held[0, y - 1, 0], 1, 0)
    feed_held[1, 0, 1] = shift_dp(feed_held[1, 0, 0], 0, 1)
    norms_one, qkv_cols, feed_held, cross_rows, query_rows, grad_output_low = stage(
        norms_one, qkv_cols, feed_held, cross_rows, query_rows, grad_output_low
    )
    full_cross_query = whole_rows(query_rows)

    cross_rows = gather_places(cross_rows)
    for y in range(1, y_size):
        feed_held[0, y, 1] = shift_dp(feed_held[0, y - 1, 1], 1, 0)
        feed_held[1, y, 1] = shift_dp(feed_held[1, y, 0], 0, 1)
    all_grads = [grad_output_low, shift_seq(grad_output_low)]
    qkv, head_attended, log_total, exact = self_forward(norms_one, qkv_cols, tables, segments)
    cross_rows, feed_held, head_attended, all_grads = stage(
        cross_rows, feed_held, head_attended, all_grads
    )
    full_cross_kv = whole_rows(cross_rows[:, 0]).reshape(dp_size * seq_size, 2, -1, width)
    full_cross_out = whole_rows(cross_rows[:, 1])

    attended = swap_seq(head_attended[:, :head_width].reshape(seq_size, rows_dev, head_width))
    feed_cores = with_cores(feed_held)
    places = [
        (core, half, y, x)
        for core in range(2)
        for half in range(2)
        for y in range(y_size)
        for x in range(2)
    ]
    unit_gate_up, unit_down = assemble(
        [feed_cores[p] for p in places],
        [(2, len(places), half_units, width), (1, len(places), half_units, width)],
        [
            (n, (kind,), kind // 2, (kind % 2, n))
            for n in range(len(places))
            for kind in range(3)
        ],
    )
    unit_gate_up, unit_down = unit_gate_up.reshape(-1, width), unit_down.reshape(-1, width)
    attended, unit_gate_up, unit_down, all_grads = stage(
        attended, unit_gate_up, unit_down, all_grads
    )

    last_grad = shift_seq(all_grads[0], -1)
    attended = jnp.concatenate([attended[s] for s in range(seq_size)], axis=1)
    first_sum = token_values + matmul(attended, full_out)
    norm_two, norm_two_back = jax.vjp(layer_norm, first_sum, gain_cross.astype(jnp.float32))
    norm_two = norm_two.astype(jnp.bfloat16)
    cross_queries = matmul(norm_two, full_cross_query).astype(jnp.bfloat16)
    all_grads, last_grad, cross_queries = stage(all_grads, last_grad, cross_queries)

    for _ in range(seq_size - 3):
        all_grads.append(shift_seq(all_grads[-1]))
    all_grads.append(last_grad)
    memory = context[0].reshape(-1, context.shape[3])
    full_cross_key = full_cross_kv[:, 0].reshape(-1, width)
    full_cross_value = full_cross_kv[:, 1].reshape(-1, width)
    memory_keys = matmul(memory, full_cross_key).astype(jnp.bfloat16)
    memory_values = matmul(memory, full_cross_value).astype(jnp.bfloat16)
    item_row = (row_segment == 1).astype(jnp.int32)[None, :]
    cross_mixed, cross_total, cross_exact = cross_forward(
        cross_queries, memory_keys, memory_values, item_row
    )
    second_sum = first_sum + matmul(cross_mixed, full_cross_out)
    norm_three, norm_three_back = jax.vjp(layer_norm, second_sum, gain_feed.astype(jnp.float32))
    norm_three = norm_three.astype(jnp.bfloat16)
    all_grads, norm_three = stage(all_grads, norm_three)

    held, feed_out, feed_dx, moving = None, {}, {}, None

    def run_block(k, held):
        *held, feed_out[k], feed_dx[k] = feed_block(
            norms[k], all_grads[k], unit_gate_up, unit_down, k, seq_size, held
        )
        return held

    norms = [norm_three, shift_seq(norm_three)]
    held = run_block(0, held)
    norms, all_grads, held, feed_out, feed_dx = stage(norms, all_grads, held, feed_out, feed_dx)
    for k in range(1, seq_size):
        if k + 1 < seq_size:
            norms.append(shift_seq(norms[-1]))
        arrived = None if k == 1 else shift_seq(moving)
        held = run_block(k, held)
        norms, arrived, held, feed_out, feed_dx = stage(norms, arrived, held, feed_out, feed_dx)
        moving = feed_dx[k] if k == 1 else add_low(arrived, feed_dx[k])
    activation, grad_gate, grad_up = held
    held = (grad_gate, grad_up, activation)
    arrived = shift_seq(moving)
    other_units = unit_products(held, norms, all_grads, 1)
    arrived, other_units, feed_out = stage(arrived, other_units, feed_out)
    other_units = swap_core(other_units)
    grad_norm_three = add_wide(arrived, feed_dx[0])

    def seq_blocks(first, second):
        blocks = jnp.concatenate([first.astype(jnp.bfloat16), second.astype(jnp.bfloat16)])
        return blocks.reshape(seq_size, part_rows, blocks.shape[1])

    feed_came = shift_seq(feed_out[seq_size // 2], -1)
    grad_output = cotangent.astype(jnp.float32) * valid_rows
    grad_second, grad_gain_feed = norm_three_back(grad_norm_three)
    grad_second = grad_second + grad_output
    second_low = grad_second.astype(jnp.bfloat16)
    grad_mixed = contract_cols(second_low, full_cross_out).astype(jnp.bfloat16)
    cross_out_own, cross_out_other = weight_products([cross_mixed], [second_low])
    cross_out_other = swap_core(cross_out_other)
    grad_cross_queries, grad_memory_keys, grad_memory_values = cross_backward(
        cross_queries,
        memory_keys,
        memory_values,
        grad_mixed,
        item_row,
        cross_total,
        cross_exact,
    )
    grad_norm_two = contract_cols(grad_cross_queries, full_cross_query)
    grad_first, grad_gain_cross = norm_two_back(grad_norm_two)
    grad_first = grad_first + grad_second
    first_low = grad_first.astype(jnp.bfloat16)
    grad_attended = contract_cols(first_low, full_out).astype(jnp.bfloat16)
    grad_attended = jnp.stack(
        [grad_attended[:, s * head_width : (s + 1) * head_width] for s in range(seq_size)]
    )
    products = weight_products([norm_two], [grad_cross_queries], 0, 3)
    products = weight_products([attended], [first_low], 1, 3, products)
    weight_own, weight_other = weight_products(
        [memory], [grad_memory_keys, grad_memory_values], 2, 3, products
    )
    cross_out_packed = pack_first(cross_out_own, cross_out_other)
    feed_came, cross_out_packed, grad_attended, weight_other, other_units = stage(
        feed_came, cross_out_packed, grad_attended, weight_other, other_units
    )

    head_grad = swap_seq(grad_attended)
    cross_out_came = send_first(cross_out_packed)
    weight_other = swap_core(weight_other)
    own_units = unit_products(held, norms, all_grads, 0, other_units)
    head_grad, cross_out_came, weight_other, own_units = stage(
        head_grad, cross_out_came, weight_other, own_units
    )

    weight_packed = pack_first(weight_own, weight_other)
    head_grad = head_grad.reshape(rows_dev * seq_size, head_width)
    head_grad = jnp.pad(head_grad, ((0, 0), (0, pairs * LANES - head_width)))
    feed_moving = reduce_middle(feed_came, feed_out), reduce_ahead(feed_out)
    head_grad, weight_packed, feed_moving = stage(head_grad, weight_packed, feed_moving)
    feed_moving = shift_seq(feed_moving[0], -1), shift_seq(feed_moving[1])
    weight_came = send_first(weight_packed)
    turned = self_backward(qkv, head_grad, log_total, exact, tables, segments, seq_size)
    norm_terms = low(contract_cols(turned, qkv_cols))
    norm_terms = [norm_terms[k * rows_dev : (k + 1) * rows_dev] for k in range(seq_size)]
    qkv_own, qkv_other = weight_products(norms_one, [turned])
    weight_came, norm_terms, qkv_own, qkv_other, feed_moving, cross_out_came, own_units = stage(
        weight_came, norm_terms, qkv_own, qkv_other, feed_moving, cross_out_came, own_units
    )
    cross_out_firsts = add_first(cross_out_came, cross_out_own, cross_out_other)

    moving = shift_seq(norm_terms[seq_size // 2], -1), shift_seq(reduce_ahead(norm_terms))
    weight_firsts = add_first(weight_came, weight_own, weight_other)
    weight_firsts = [jnp.concatenate(pair) for pair in zip(weight_firsts, cross_out_firsts)]
    weight_packed = pack_second(*weight_firsts)
    weight_came = send_second(weight_packed)
    qkv_other = swap_core(qkv_other)
    grad_gain_self = sum(
        jnp.sum(term.astype(jnp.float32) * norm.astype(jnp.float32), axis=0)
        for term, norm in zip(norm_terms, norms_one)
    ) / gain_self.astype(jnp.float32)
    gains = jnp.stack([grad_gain_self, grad_gain_cross, grad_gain_feed])
    gains = gains.reshape(-1, dp_size * seq_size, part_rows).transpose(1, 0, 2)
    gains = lax.all_to_all(gains, ("dp", "seq"), split_axis=0, concat_axis=0, tiled=True)
    moving, weight_came, qkv_own, qkv_other, gains = stage(
        moving, weight_came, qkv_own, qkv_other, gains
    )
    gains = jnp.sum(gains, axis=0)

    norm_came = shift_seq(reduce_middle(moving[0], norm_terms), -1)
    own_units = own_units.reshape(3, 2, y_size, 2, half_units, width)
    unit_came = send_first(pack_first(own_units))
    weight_seconds = add_second(weight_came, *weight_firsts)
    placed = swap_seq(
        jnp.stack(
            [
                seq_blocks(*(s[n] for s in weight_seconds))
                for n in (3, 0, 1)
            ],
            axis=1,
        )
    )
    kv_blocks = jnp.stack(
        [low(s[2]).reshape(seq_size, -1, width) for s in weight_seconds], axis=1
    )
    qkv_came = send_first(pack_first(qkv_own, qkv_other))
    qkv_firsts = add_first(qkv_came, qkv_own, qkv_other)
    qkv_seconds = add_second(send_second(pack_second(*qkv_firsts)), *qkv_firsts)
    later = jnp.concatenate(
        [
            kv_blocks.reshape(seq_size, part_rows, width),
            seq_blocks(*(s[0] for s in qkv_seconds)),
        ],
        axis=2,
    )
    output = low(
        second_sum + add_wide(feed_moving[0], feed_out[0]) + feed_moving[1].astype(jnp.float32)
    )
    norm_came, placed, unit_came, later = stage(norm_came, placed, unit_came, later)

    later = swap_seq(later)
    unit_firsts = add_first(unit_came, own_units)
    unit_came = send_second(pack_second(*unit_firsts))
    grad_norm_one = add_wide(norm_came, norm_terms[0]) + moving[1].astype(jnp.float32)
    grad_tokens_wide = norm_one_back(grad_norm_one)[0]
    grad_tokens = low(grad_tokens_wide + grad_first)
    grad_cross_out, grad_cross_query, grad_self_out = (
        jnp.sum(placed[:, n].astype(jnp.float32), axis=0) for n in range(3)
    )
    unit_grads = jnp.concatenate(add_second(unit_came, *unit_firsts), axis=1)
    grad_cross_kv = jnp.sum(later[:, :, :width].astype(jnp.float32), axis=0)
    kv_rows = part_rows // 2
    grad_qkv = (
        later[:, :, width:]
        .reshape(seq_size, part_rows, pairs, 3, LANES)
        .transpose(3, 1, 0, 2, 4)
        .reshape(3, part_rows, seq_size, pairs * LANES)[..., :head_width]
        .reshape(3, part_rows, width)
        .astype(jnp.float32)
    )
    return (
        output,
        grad_tokens,
        gains[0],
        gains[1],
        gains[2],
        grad_qkv[0],
        grad_qkv[1],
        grad_qkv[2],
        grad_self_out,
        grad_cross_query,
        grad_cross_kv[:kv_rows],
        grad_cross_kv[kv_rows:],
        grad_cross_out,
        unit_grads[0],
        unit_grads[1],
        unit_grads[2],
    )


def solution(mesh):
    placed = (
        P(("dp", "seq"), None),
        P("dp", None, None, None),
        P("dp", None),
        P(),
        P(),
        P(),
        P(("dp", "seq"), None),
        P(("dp", "seq"), None),
        P(("dp", "seq"), None),
        P(("dp", "seq"), None),
        P(("dp", "seq"), None),
        P(("dp", "seq"), None),
        P(("dp", "seq"), None),
        P(("dp", "seq"), None),
        P(("dp", "seq"), None),
        P(("dp", "seq"), None),
        P(("dp", "seq"), None),
        P(("dp", "seq"), None),
    )
    return jax.shard_map(
        local,
        mesh=mesh,
        in_specs=placed,
        out_specs=(
            P(("dp", "seq"), None),
            P(("dp", "seq"), None),
            P(("dp", "seq")),
            P(("dp", "seq")),
            P(("dp", "seq")),
            P(("dp", "seq"), None),
            P(("dp", "seq"), None),
            P(("dp", "seq"), None),
            P(("dp", "seq"), None),
            P(("dp", "seq"), None),
            P(("dp", "seq"), None),
            P(("dp", "seq"), None),
            P(("dp", "seq"), None),
            P(("dp", "seq"), None),
            P(("dp", "seq"), None),
            P(("dp", "seq"), None),
        ),
        check_vma=False,
    )
```

```python
import jax
import jax.numpy as jnp
from jax import lax
from jax.experimental import pallas as pl
from jax.experimental.pallas import tpu as pltpu
from jax.sharding import PartitionSpec as P

HEADS = 24
HDIM = 64
ROT = 32


EPSILON = 1e-05
NEG_FILL = -1e30


def layer_norm(values, gain_vector):
    average = jnp.mean(values, axis=-1, keepdims=True)
    centered = values - average
    variance = jnp.mean(centered * centered, axis=-1, keepdims=True)
    return centered * lax.rsqrt(variance + EPSILON) * gain_vector


def layout(lengths, row_ids):
    first_end = lengths[0]
    second_end = lengths[0] + lengths[1]
    segment = jnp.where(row_ids < first_end, 0, jnp.where(row_ids < second_end, 1, 2)).astype(
        jnp.int32
    )
    seg_start = jnp.where(segment == 0, 0, jnp.where(segment == 1, first_end, second_end))
    return (segment, row_ids - seg_start)


def matmul(left, right):
    return jnp.dot(left, right, preferred_element_type=jnp.float32)


def contract_rows(left, right):
    return lax.dot_general(
        left, right, (((0,), (0,)), ((), ())), preferred_element_type=jnp.float32
    )


def contract_cols(left, right):
    return lax.dot_general(
        left, right, (((1,), (1,)), ((), ())), preferred_element_type=jnp.float32
    )


LANES = 128
PAIR = LANES // HDIM
LOG2E = 1.4426950408889634


def taking(microseconds):
    return pl.CostEstimate(
        flops=0, bytes_accessed=int(3e6 * microseconds), transcendentals=0
    )


def turn(values, cosine, sine_low, sine_high, sign):
    half_rot = ROT // 2
    ahead = pltpu.roll(values, LANES - half_rot, 1)
    behind = pltpu.roll(values, half_rot, 1)
    return values * cosine + sign * (behind * sine_high - ahead * sine_low)


def dot(left, right, left_dim, right_dim):
    return lax.dot_general(
        left, right, (((left_dim,), (right_dim,)), ((), ())), preferred_element_type=jnp.float32
    )


def lane_tables(position):
    half_rot = ROT // 2
    feature = jnp.arange(LANES, dtype=jnp.int32) % HDIM
    frequency = 10000.0 ** (-(feature % half_rot).astype(jnp.float32) / half_rot)
    angles = position.astype(jnp.float32)[:, None] * frequency[None, :]
    cosine = jnp.where(feature < ROT, jnp.cos(angles), 1.0)
    sine = jnp.sin(angles)
    return (
        cosine,
        jnp.where(feature < half_rot, sine, 0.0),
        jnp.where((feature >= half_rot) & (feature < ROT), sine, 0.0),
    )


def seq_distance_order(block, seq_size):
    place = lax.axis_index("seq")
    return lax.rem(place + (seq_size - block), seq_size)


def part(kind, head):
    return slice(kind * LANES + head * HDIM, kind * LANES + (head + 1) * HDIM)


def self_forward(norms, qkv_cols, tables, segments):
    seq_size, (block, width) = len(norms), norms[0].shape
    length = block * seq_size
    group = 3 * LANES
    pairs = qkv_cols.shape[1] // group
    scale = HDIM ** (-0.5) * LOG2E

    def body(*refs):
        norm_refs = refs[:seq_size]
        cols_ref, cos_ref, low_ref, high_ref, seg_col, seg_row, *outs = refs[seq_size:]
        qkv_out, mixed_ref, total_ref, exact_ref = outs
        for number in range(seq_size):
            rows = slice(number * block, (number + 1) * block)
            tables = cos_ref[rows], low_ref[rows], high_ref[rows]
            projected = dot(norm_refs[number][...], cols_ref[...], 1, 0)
            for kind in range(3):
                cols = slice(kind * LANES, (kind + 1) * LANES)
                values = projected[:, cols]
                if kind < 2:
                    values = turn(values, *tables, 1.0)
                qkv_out[rows, cols] = values.astype(jnp.bfloat16)
        for number in range(seq_size):
            rows = slice(number * block, (number + 1) * block)
            same = seg_col[...] == seg_row[:, rows]
            mixed = []
            for head in range(PAIR):
                scores = dot(qkv_out[:, part(1, head)], qkv_out[rows, part(0, head)], 1, 1)
                scores = jnp.where(same, scores, NEG_FILL)
                highest = jnp.max(scores, axis=0, keepdims=True)
                raised = jnp.exp2((scores - highest) * scale)
                total = jnp.sum(raised, axis=0, keepdims=True)
                mixed.append(dot(qkv_out[:, part(2, head)], raised.astype(jnp.bfloat16), 0, 0) / total)
                total_ref[0, head : head + 1, rows] = highest * scale + jnp.log2(total)
            place = seq_distance_order(number, seq_size)
            target = pl.ds(pl.multiple_of(place * block, block), block)
            mixed = jnp.concatenate(mixed)
            exact_ref[0, :, rows] = mixed
            mixed_ref[target, :] = mixed.T.astype(jnp.bfloat16)

    whole = pl.BlockSpec((length, LANES), lambda p: (0, 0))
    return pl.pallas_call(
        body,
        grid=(pairs,),
        in_specs=[pl.BlockSpec((block, width), lambda p: (0, 0))] * seq_size
        + [pl.BlockSpec((width, group), lambda p: (0, p))]
        + [whole] * 3
        + [
            pl.BlockSpec((length, 1), lambda p: (0, 0)),
            pl.BlockSpec((1, length), lambda p: (0, 0)),
        ],
        out_specs=[
            pl.BlockSpec((length, group), lambda p: (0, p)),
            pl.BlockSpec((length, LANES), lambda p: (0, p)),
            pl.BlockSpec((1, PAIR, length), lambda p: (p, 0, 0)),
            pl.BlockSpec((1, LANES, length), lambda p: (p, 0, 0)),
        ],
        out_shape=[
            jax.ShapeDtypeStruct((length, pairs * group), jnp.bfloat16),
            jax.ShapeDtypeStruct((length, pairs * LANES), jnp.bfloat16),
            jax.ShapeDtypeStruct((pairs, PAIR, length), jnp.float32),
            jax.ShapeDtypeStruct((pairs, LANES, length), jnp.float32),
        ],
        compiler_params=pltpu.CompilerParams(vmem_limit_bytes=40 << 20),
        cost_estimate=taking(8),
    )(*norms, qkv_cols, *tables, *segments)


def self_backward(qkv, grad_out, log_total, exact, tables, segments, seq_size):
    length = qkv.shape[0]
    group = 3 * LANES
    pairs = qkv.shape[1] // group
    block = length // seq_size
    scaling = HDIM ** (-0.5)
    scale = scaling * LOG2E

    def body(qkv_ref, grad_ref, total_ref, exact_ref, *rest):
        cos_ref, low_ref, high_ref, seg_col, seg_row, out_ref, dk_sum, dv_sum = rest
        for number in range(seq_size):
            rows = slice(number * block, (number + 1) * block)
            same = seg_col[...] == seg_row[:, rows]
            place = seq_distance_order(number, seq_size)
            grads = grad_ref[pl.ds(pl.multiple_of(place * block, block), block), :]
            inner = grads.astype(jnp.float32).T * exact_ref[0, :, rows]
            grad_queries = []
            for head in range(PAIR):
                cols = slice(head * HDIM, (head + 1) * HDIM)
                head_inner = jnp.sum(inner[cols, :], axis=0, keepdims=True)
                grad_head = grads[:, cols]
                query_head = qkv_ref[rows, part(0, head)]
                key_head = qkv_ref[:, part(1, head)]
                scores = dot(key_head, query_head, 1, 1) * scale - total_ref[
                    0, head : head + 1, rows
                ]
                chance = jnp.exp2(jnp.where(same, scores, NEG_FILL))
                grad_chance = dot(qkv_ref[:, part(2, head)], grad_head, 1, 1)
                grad_scores = (chance * (grad_chance - head_inner)).astype(jnp.bfloat16)
                grad_queries.append(dot(key_head, grad_scores, 0, 0))
                grad_keys = dot(query_head, grad_scores, 0, 1)
                grad_values = dot(grad_head, chance.astype(jnp.bfloat16), 0, 1)
                if number == 0:
                    dk_sum[cols, :] = grad_keys
                    dv_sum[cols, :] = grad_values
                else:
                    dk_sum[cols, :] += grad_keys
                    dv_sum[cols, :] += grad_values
            tables = cos_ref[rows], low_ref[rows], high_ref[rows]
            turned = turn(jnp.concatenate(grad_queries).T * scaling, *tables, -1.0)
            out_ref[rows, :LANES] = turned.astype(jnp.bfloat16)
        tables = cos_ref[...], low_ref[...], high_ref[...]
        turned = turn(dk_sum[...].T * scaling, *tables, -1.0)
        out_ref[:, LANES : 2 * LANES] = turned.astype(jnp.bfloat16)
        out_ref[:, 2 * LANES :] = dv_sum[...].T.astype(jnp.bfloat16)

    whole = pl.BlockSpec((length, LANES), lambda p: (0, 0))
    return pl.pallas_call(
        body,
        grid=(pairs,),
        in_specs=[
            pl.BlockSpec((length, group), lambda p: (0, p)),
            pl.BlockSpec((length, LANES), lambda p: (0, p)),
            pl.BlockSpec((1, PAIR, length), lambda p: (p, 0, 0)),
            pl.BlockSpec((1, LANES, length), lambda p: (p, 0, 0)),
        ]
        + [whole] * 3
        + [
            pl.BlockSpec((length, 1), lambda p: (0, 0)),
            pl.BlockSpec((1, length), lambda p: (0, 0)),
        ],
        out_specs=pl.BlockSpec((length, group), lambda p: (0, p)),
        out_shape=jax.ShapeDtypeStruct(qkv.shape, jnp.bfloat16),
        scratch_shapes=[pltpu.VMEM((LANES, length), jnp.float32)] * 2,
        compiler_params=pltpu.CompilerParams(vmem_limit_bytes=40 << 20),
        cost_estimate=taking(7),
    )(qkv, grad_out, log_total, exact, *tables, *segments)


CROSS_HEADS = 12


def cross_scores(queries, key_rows, item_row):
    scores = dot(key_rows, queries, 1, 1)
    count = key_rows.shape[0]
    key_item = (lax.broadcasted_iota(jnp.int32, (count, 1), 0) >= count // 2).astype(jnp.int32)
    return jnp.where(key_item == item_row, scores, NEG_FILL)


def cross_forward(queries, key_rows, value_rows, item_row):
    scale = HDIM ** (-0.5) * LOG2E

    def body(q_ref, k_ref, v_ref, item_ref, mixed_ref, total_ref, exact_ref):
        mixed = []
        for head in range(CROSS_HEADS):
            cols = slice(head * HDIM, (head + 1) * HDIM)
            scores = cross_scores(q_ref[:, cols], k_ref[:, cols], item_ref[...])
            highest = jnp.max(scores, axis=0, keepdims=True)
            raised = jnp.exp2((scores - highest) * scale)
            total = jnp.sum(raised, axis=0, keepdims=True)
            mixed.append(dot(v_ref[:, cols], raised.astype(jnp.bfloat16), 0, 0) / total)
            total_ref[0, head : head + 1, :] = highest * scale + jnp.log2(total)
        mixed = jnp.concatenate(mixed)
        exact_ref[...] = mixed
        mixed_ref[...] = mixed.T.astype(jnp.bfloat16)

    (rows, width), keys = queries.shape, key_rows.shape[0]
    lanes = CROSS_HEADS * HDIM
    steps = width // lanes
    return pl.pallas_call(
        body,
        grid=(steps,),
        in_specs=[pl.BlockSpec((n, lanes), lambda p: (0, p)) for n in (rows, keys, keys)]
        + [pl.BlockSpec(item_row.shape, lambda p: (0, 0))],
        out_specs=[
            pl.BlockSpec((rows, lanes), lambda p: (0, p)),
            pl.BlockSpec((1, CROSS_HEADS, rows), lambda p: (p, 0, 0)),
            pl.BlockSpec((lanes, rows), lambda p: (p, 0)),
        ],
        out_shape=[
            jax.ShapeDtypeStruct((rows, width), jnp.bfloat16),
            jax.ShapeDtypeStruct((steps, CROSS_HEADS, rows), jnp.float32),
            jax.ShapeDtypeStruct((width, rows), jnp.float32),
        ],
        compiler_params=pltpu.CompilerParams(vmem_limit_bytes=32 << 20),
        cost_estimate=taking(4),
    )(queries, key_rows, value_rows, item_row)


def cross_backward(queries, key_rows, value_rows, grad_mixed, item_row, log_total, exact):
    scaling = HDIM ** (-0.5)
    scale = scaling * LOG2E

    def body(q_ref, k_ref, v_ref, grad_ref, item_ref, total_ref, exact_ref, dq_ref, dk_ref, dv_ref):
        grad_queries = []
        inner = grad_ref[...].astype(jnp.float32).T * exact_ref[...]
        for head in range(CROSS_HEADS):
            cols = slice(head * HDIM, (head + 1) * HDIM)
            query_head, key_head, grad_head = q_ref[:, cols], k_ref[:, cols], grad_ref[:, cols]
            scores = cross_scores(query_head, key_head, item_ref[...])
            chance = jnp.exp2(scores * scale - total_ref[0, head : head + 1, :])
            grad_chance = dot(v_ref[:, cols], grad_head, 1, 1)
            head_inner = jnp.sum(inner[cols, :], axis=0, keepdims=True)
            grad_scores = (chance * (grad_chance - head_inner)).astype(jnp.bfloat16)
            grad_queries.append(dot(key_head, grad_scores, 0, 0))
            dk_ref[:, cols] = (dot(grad_scores, query_head, 1, 0) * scaling).astype(jnp.bfloat16)
            dv_ref[:, cols] = dot(chance.astype(jnp.bfloat16), grad_head, 1, 0).astype(
                jnp.bfloat16
            )
        dq_ref[...] = (jnp.concatenate(grad_queries).T * scaling).astype(jnp.bfloat16)

    (rows, width), keys = queries.shape, key_rows.shape[0]
    lanes = CROSS_HEADS * HDIM
    sizes = (rows, keys, keys)
    return pl.pallas_call(
        body,
        grid=(width // lanes,),
        in_specs=[pl.BlockSpec((n, lanes), lambda p: (0, p)) for n in sizes + (rows,)]
        + [
            pl.BlockSpec(item_row.shape, lambda p: (0, 0)),
            pl.BlockSpec((1, CROSS_HEADS, rows), lambda p: (p, 0, 0)),
            pl.BlockSpec((lanes, rows), lambda p: (p, 0)),
        ],
        out_specs=[pl.BlockSpec((n, lanes), lambda p: (0, p)) for n in sizes],
        out_shape=[jax.ShapeDtypeStruct((n, width), jnp.bfloat16) for n in sizes],
        compiler_params=pltpu.CompilerParams(vmem_limit_bytes=32 << 20),
        cost_estimate=taking(4),
    )(queries, key_rows, value_rows, grad_mixed, item_row, log_total, exact)


def feed_block(normed, grads, gate_up, down, number, count, held):
    rows, width = normed.shape
    units = down.shape[0]
    steps = 3
    tile = units // steps

    def body(x_ref, g_ref, gate_ref, up_ref, down_ref, *rest):
        act_ref, dgate_ref, dup_ref, out_ref, dx_ref, out_sum, dx_sum = rest[-7:]
        step = pl.program_id(0)
        values, grad_rows = x_ref[...], g_ref[...]
        gate = dot(values, gate_ref[...], 1, 1)
        up = dot(values, up_ref[...], 1, 1)
        grad_act = dot(grad_rows, down_ref[...], 1, 1)
        chance = jax.nn.sigmoid(gate)
        silu = gate * chance
        act = (silu * up).astype(jnp.bfloat16)
        grad_gate = (grad_act * up * (chance + silu * (1.0 - chance))).astype(jnp.bfloat16)
        grad_up = (grad_act * silu).astype(jnp.bfloat16)
        act_ref[...] = act
        dgate_ref[...] = grad_gate
        dup_ref[...] = grad_up
        out_part = dot(act, down_ref[...], 1, 0)
        dx_part = dot(grad_gate, gate_ref[...], 1, 0) + dot(grad_up, up_ref[...], 1, 0)

        @pl.when(step == 0)
        def _():
            out_sum[...] = out_part
            dx_sum[...] = dx_part

        @pl.when(step > 0)
        def _():
            out_sum[...] += out_part
            dx_sum[...] += dx_part

        @pl.when(step == steps - 1)
        def _():
            out_ref[...] = out_sum[...].astype(jnp.bfloat16)
            dx_ref[...] = dx_sum[...].astype(jnp.bfloat16)

    full = pl.BlockSpec((rows, width), lambda t: (0, 0))
    block = pl.BlockSpec((rows, tile), lambda t: (number, t))
    unit_shape = jax.ShapeDtypeStruct((rows * count, units), jnp.bfloat16)
    row_shape = jax.ShapeDtypeStruct((rows, width), jnp.bfloat16)
    held = [] if held is None else list(held)
    return pl.pallas_call(
        body,
        grid=(steps,),
        in_specs=[
            full,
            full,
            pl.BlockSpec((tile, width), lambda t: (t, 0)),
            pl.BlockSpec((tile, width), lambda t: (steps + t, 0)),
            pl.BlockSpec((tile, width), lambda t: (t, 0)),
        ]
        + [pl.BlockSpec(memory_space=pl.ANY)] * len(held),
        out_specs=[block] * 3 + [full] * 2,
        out_shape=[unit_shape] * 3 + [row_shape] * 2,
        scratch_shapes=[pltpu.VMEM((rows, width), jnp.float32)] * 2,
        input_output_aliases={5 + n: n for n in range(len(held))},
        compiler_params=pltpu.CompilerParams(vmem_limit_bytes=40 << 20),
        cost_estimate=taking(4),
    )(normed, grads, gate_up, gate_up, down, *held)


def unit_products(units, norms, grads, core, arrived=None):
    seq_size, (block, width) = len(norms), norms[0].shape
    length, count = units[0].shape
    steps = 3
    tile = count // (2 * steps)

    def body(*refs):
        unit_refs, refs = refs[:3], refs[3:]
        norm_refs, grad_refs, refs = refs[:seq_size], refs[seq_size : 2 * seq_size], refs[2 * seq_size :]
        out_ref, all_norms, all_grads = refs[-3:]

        @pl.when(pl.program_id(0) == 0)
        def _():
            for k in range(seq_size):
                rows = slice(k * block, (k + 1) * block)
                all_norms[rows, :] = norm_refs[k][...]
                all_grads[rows, :] = grad_refs[k][...]

        for kind in range(3):
            rows = (all_grads if kind == 2 else all_norms)[...]
            total = dot(unit_refs[kind][...], rows, 0, 0)
            if arrived is not None:
                total += refs[0][kind].astype(jnp.float32)
            out_ref[kind] = total.astype(jnp.bfloat16)

    out_block = pl.BlockSpec((3, tile, width), lambda t: (0, t, 0))
    extra = [] if arrived is None else [arrived]
    return pl.pallas_call(
        body,
        grid=(steps,),
        in_specs=[pl.BlockSpec((length, tile), lambda t: (0, core * steps + t))] * 3
        + [pl.BlockSpec((block, width), lambda t: (0, 0))] * (2 * seq_size)
        + [out_block] * len(extra),
        out_specs=out_block,
        out_shape=jax.ShapeDtypeStruct((3, count // 2, width), jnp.bfloat16),
        scratch_shapes=[pltpu.VMEM((length, width), jnp.bfloat16)] * 2,
        compiler_params=pltpu.CompilerParams(vmem_limit_bytes=56 << 20),
        cost_estimate=taking(5),
    )(*units, *norms, *grads, *extra)


def weight_products(lefts, rights, slot=0, slots=1, held=None):
    dp_size = lax.axis_size("dp")
    y_size = dp_size // 4
    rows, height = lefts[0].shape
    columns = rights[0].shape[1]
    tile = 3 * LANES
    place_rows = height // dp_size
    half_rows = place_rows * len(rights) // 2
    per_step = tile // place_rows

    def body(*refs):
        left_refs, refs = refs[: len(lefts)], refs[len(lefts) :]
        right_refs, (own_ref, other_ref, product) = refs[: len(rights)], refs[-3:]
        dp_place = lax.axis_index("dp")
        step = pl.program_id(0)
        for number, right_ref in enumerate(right_refs):
            total = None
            for k, left_ref in enumerate(left_refs):
                term = dot(left_ref[...], right_ref[k * rows : (k + 1) * rows, :], 0, 0)
                total = term if total is None else total + term
            product[...] = total.astype(jnp.bfloat16)
            for chip in range(per_step // 2):
                chip_place = step * (per_step // 2) + chip
                y_back = lax.rem((dp_place >> 2) + y_size - (chip_place >> 1), y_size)
                x_back = ((dp_place >> 1) ^ chip_place) & 1
                for target, core in ((own_ref, dp_place & 1), (other_ref, 1 - (dp_place & 1))):
                    first_row = (2 * chip + core) * place_rows
                    for half in range(2 // len(rights)):
                        begin = pl.multiple_of(first_row + half * half_rows, 16)
                        target[0, number + half, y_back, x_back] = product[
                            pl.ds(begin, half_rows), :
                        ]

    whole = (1, 2, y_size, 2, half_rows, columns)
    out_block = pl.BlockSpec(whole, lambda t: (slot, 0, 0, 0, 0, 0))
    out_shape = jax.ShapeDtypeStruct((slots,) + whole[1:], jnp.bfloat16)
    held = [] if held is None else list(held)
    return pl.pallas_call(
        body,
        grid=(height // tile,),
        in_specs=[pl.BlockSpec((rows, tile), lambda t: (0, t))] * len(lefts)
        + [pl.BlockSpec(r.shape, lambda t: (0, 0)) for r in rights]
        + [pl.BlockSpec(memory_space=pl.ANY)] * len(held),
        out_specs=[out_block] * 2,
        out_shape=[out_shape] * 2,
        scratch_shapes=[pltpu.VMEM((tile, columns), jnp.bfloat16)],
        input_output_aliases={len(lefts) + len(rights) + n: n for n in range(len(held))},
        compiler_params=pltpu.CompilerParams(vmem_limit_bytes=40 << 20),
        cost_estimate=taking(1.5),
    )(*lefts, *rights, *held)


def swap_core(values):
    return lax.ppermute(values, "dp", [(d, d ^ 1) for d in range(lax.axis_size("dp"))])


def shift_dp(values, y, x):
    size = lax.axis_size("dp")
    return lax.ppermute(values, "dp", [(d, ((d + 4 * y) % size) ^ (2 * x)) for d in range(size)])


def shift_seq(values, step=1):
    size = lax.axis_size("seq")
    return lax.ppermute(values, "seq", [(s, (s + step) % size) for s in range(size)])


def gather_rest(pieces):
    last = shift_seq(pieces[0], -1)
    pieces = list(pieces)
    for _ in range(lax.axis_size("seq") - 3):
        pieces.append(shift_seq(pieces[-1]))
    return pieces + [last]


def reduce_ahead(blocks):
    size = lax.axis_size("seq")
    total = blocks[size // 2 + 1]
    for k in range(size // 2 + 2, size):
        total = add_low(shift_seq(total), blocks[k])
    return total


def reduce_middle(total, blocks):
    for k in range(lax.axis_size("seq") // 2 - 1, 1, -1):
        total = shift_seq(add_low(total, blocks[k]), -1)
    return add_low(total, blocks[1])


def swap_seq(values):
    return lax.all_to_all(values, "seq", split_axis=0, concat_axis=0, tiled=True)


def gather_places(values):
    size = lax.axis_size("seq")
    return swap_seq(jnp.broadcast_to(values[None], (size,) + values.shape))


def add_wide(left, right):
    return left.astype(jnp.float32) + right.astype(jnp.float32)


def add_low(left, right):
    return add_wide(left, right).astype(jnp.bfloat16)


def stage(*values):
    return lax.optimization_barrier(values)


def spread_first(first, second):
    held = {(0, 0, 0): first, (1, 0, 0): second, (0, 0, 1): shift_dp(first, 0, 1)}
    for y in range(1, lax.axis_size("dp") // 4):
        held[1, y, 0] = shift_dp(held[1, y - 1, 0], 1, 0)
    return held


def spread_second(held):
    held = dict(held)
    for half, y, x in [(h, y, 0) for h, y, _ in held if h == 1]:
        held[half, y, 1] = shift_dp(held[half, y, x], 0, 1)
    for x in range(2):
        for y in range(1, lax.axis_size("dp") // 4):
            held[0, y, x] = shift_dp(held[0, y - 1, x], 1, 0)
    return held


def with_cores(plane):
    return {(core,) + p: swap_core(v) if core else v for core in range(2) for p, v in plane.items()}


def low(values):
    return values.astype(jnp.bfloat16)


def terms(own, arrived, *index):
    index = (slice(None),) + index
    values = own[index].astype(jnp.float32)
    return values if arrived is None else values + arrived[index].astype(jnp.float32)


def pack_first(own, arrived=None):
    y_size = own.shape[2]
    total = low(terms(own, arrived, 0, y_size - 1))
    for y in range(y_size - 2, 0, -1):
        total = low(shift_dp(total, -1, 0).astype(jnp.float32) + terms(own, arrived, 0, y))
    return total, low(terms(own, arrived, 1, slice(None), 1))


def send_first(packed):
    return shift_dp(packed[0], -1, 0), shift_dp(packed[1], 0, 1)


def add_first(came, own, arrived=None):
    return (
        low(came[0].astype(jnp.float32) + terms(own, arrived, 0, 0)),
        low(came[1].astype(jnp.float32) + terms(own, arrived, 1, slice(None), 0)),
    )


def pack_second(first, second):
    total = second[:, -1]
    for y in range(second.shape[1] - 2, 0, -1):
        total = add_low(shift_dp(total, -1, 0), second[:, y])
    return first[:, 1], total


def send_second(packed):
    return shift_dp(packed[0], 0, 1), shift_dp(packed[1], -1, 0)


def add_second(came, first, second):
    return add_wide(first[:, 0], came[0]), add_wide(second[:, 0], came[1])


def assemble(pieces, out_shapes, copies):
    count = len(pieces)

    def body(*refs):
        sources, targets = refs[:count], refs[count : count + len(out_shapes)]
        held, loaded, stored = refs[count + len(out_shapes) : -2], refs[-2], refs[-1]
        loads = [pltpu.make_async_copy(sources[n], held[n], loaded.at[n]) for n in range(count)]
        for load in loads:
            load.start()
        stores = []
        for n in range(count):
            loads[n].wait()
            for number, (piece, source, out, target) in enumerate(copies):
                if piece == n:
                    stores.append(
                        pltpu.make_async_copy(
                            held[n].at[source],
                            targets[out].at[target],
                            stored.at[number],
                        )
                    )
                    stores[-1].start()
        for store in stores:
            store.wait()

    return pl.pallas_call(
        body,
        out_shape=[jax.ShapeDtypeStruct(s, jnp.bfloat16) for s in out_shapes],
        in_specs=[pl.BlockSpec(memory_space=pl.ANY)] * count,
        out_specs=[pl.BlockSpec(memory_space=pl.ANY)] * len(out_shapes),
        scratch_shapes=[pltpu.VMEM(p.shape, p.dtype) for p in pieces]
        + [pltpu.SemaphoreType.DMA((count,)), pltpu.SemaphoreType.DMA((len(copies),))],
        compiler_params=pltpu.CompilerParams(vmem_limit_bytes=32 << 20),
        cost_estimate=taking(2),
    )(*pieces)


def local(
    tokens,
    context,
    item_lengths,
    gain_self,
    gain_cross,
    gain_feed,
    self_query,
    self_key,
    self_value,
    self_out,
    cross_query,
    cross_key,
    cross_value,
    cross_out,
    feed_gate,
    feed_up,
    feed_down,
    cotangent,
):
    rows_dev, width = tokens.shape
    dp_size, seq_size = lax.axis_size("dp"), lax.axis_size("seq")
    seq_place = lax.axis_index("seq")
    y_size = dp_size // 4
    head_width = HEADS // seq_size * HDIM
    pairs = -(-head_width // LANES)
    part_rows = self_query.shape[0]

    def whole_rows(rows):
        return lax.all_gather(rows, "dp", axis=0, tiled=False).reshape(-1, rows.shape[-1])

    qkv_parts = jnp.stack([self_query, self_key, self_value]).reshape(
        3, part_rows, seq_size, head_width
    )
    qkv_parts = jnp.pad(qkv_parts, ((0, 0),) * 3 + ((0, pairs * LANES - head_width),))
    qkv_parts = qkv_parts.reshape(3, part_rows, seq_size, pairs, LANES).transpose(2, 1, 3, 0, 4)
    qkv_parts = qkv_parts.reshape(seq_size, part_rows, pairs * 3 * LANES)
    qkv_parts, tokens, feed_gate, feed_up, feed_down, cotangent, item_lengths = stage(
        qkv_parts, tokens, feed_gate, feed_up, feed_down, cotangent, item_lengths
    )
    qkv_rows = swap_seq(qkv_parts)
    token_values = tokens.astype(jnp.float32)
    norm_one, norm_one_back = jax.vjp(layer_norm, token_values, gain_self.astype(jnp.float32))
    norm_one = norm_one.astype(jnp.bfloat16)
    feed_parts = jnp.stack([feed_gate, feed_up, feed_down])
    half_units = feed_parts.shape[1] // 2
    feed_parts = feed_parts[:, :half_units], feed_parts[:, half_units:]
    row_ids = jnp.concatenate(
        [
            lax.rem(seq_place + (seq_size - k), seq_size) * rows_dev
            + jnp.arange(rows_dev, dtype=jnp.int32)
            for k in range(seq_size)
        ]
    )
    segment, position = layout(item_lengths[0], row_ids)
    row_segment = segment[:rows_dev]
    tables = lane_tables(position)
    valid_rows = (row_segment < 2).astype(jnp.float32)[:, None]
    grad_output_low = (cotangent.astype(jnp.float32) * valid_rows).astype(jnp.bfloat16)
    qkv_rows, norm_one, feed_parts, self_out, cross_query = stage(
        qkv_rows, norm_one, feed_parts, self_out, cross_query
    )
    qkv_cols = whole_rows(qkv_rows)

    norms_one = [norm_one, shift_seq(norm_one)]
    out_rows = gather_places(self_out)
    feed_held = spread_first(*feed_parts)
    segments = segment[:, None], segment[None, :]
    (
        norms_one,
        tables,
        segments,
        feed_held,
        out_rows,
        cross_query,
        grad_output_low,
        cross_rows,
    ) = stage(
        norms_one,
        tables,
        segments,
        feed_held,
        out_rows,
        cross_query,
        grad_output_low,
        jnp.stack([jnp.concatenate([cross_key, cross_value]), cross_out]),
    )
    full_out = whole_rows(out_rows)

    norms_one = gather_rest(norms_one)
    query_rows = gather_places(cross_query)
    for y in range(1, y_size):
        feed_held[0, y, 0] = shift_dp(feed_held[0, y - 1, 0], 1, 0)
    feed_held[1, 0, 1] = shift_dp(feed_held[1, 0, 0], 0, 1)
    norms_one, qkv_cols, feed_held, cross_rows, query_rows, grad_output_low = stage(
        norms_one, qkv_cols, feed_held, cross_rows, query_rows, grad_output_low
    )
    full_cross_query = whole_rows(query_rows)

    cross_rows = gather_places(cross_rows)
    for y in range(1, y_size):
        feed_held[0, y, 1] = shift_dp(feed_held[0, y - 1, 1], 1, 0)
        feed_held[1, y, 1] = shift_dp(feed_held[1, y, 0], 0, 1)
    all_grads = [grad_output_low, shift_seq(grad_output_low)]
    qkv, head_attended, log_total, exact = self_forward(norms_one, qkv_cols, tables, segments)
    cross_rows, feed_held, head_attended, all_grads = stage(
        cross_rows, feed_held, head_attended, all_grads
    )
    full_cross_kv = whole_rows(cross_rows[:, 0]).reshape(dp_size * seq_size, 2, -1, width)
    full_cross_out = whole_rows(cross_rows[:, 1])

    attended = swap_seq(head_attended[:, :head_width].reshape(seq_size, rows_dev, head_width))
    feed_cores = with_cores(feed_held)
    places = [
        (core, half, y, x)
        for core in range(2)
        for half in range(2)
        for y in range(y_size)
        for x in range(2)
    ]
    unit_gate_up, unit_down = assemble(
        [feed_cores[p] for p in places],
        [(2, len(places), half_units, width), (1, len(places), half_units, width)],
        [
            (n, (kind,), kind // 2, (kind % 2, n))
            for n in range(len(places))
            for kind in range(3)
        ],
    )
    unit_gate_up, unit_down = unit_gate_up.reshape(-1, width), unit_down.reshape(-1, width)
    attended, unit_gate_up, unit_down, all_grads = stage(
        attended, unit_gate_up, unit_down, all_grads
    )

    last_grad = shift_seq(all_grads[0], -1)
    attended = jnp.concatenate([attended[s] for s in range(seq_size)], axis=1)
    first_sum = token_values + matmul(attended, full_out)
    norm_two, norm_two_back = jax.vjp(layer_norm, first_sum, gain_cross.astype(jnp.float32))
    norm_two = norm_two.astype(jnp.bfloat16)
    cross_queries = matmul(norm_two, full_cross_query).astype(jnp.bfloat16)
    all_grads, last_grad, cross_queries = stage(all_grads, last_grad, cross_queries)

    for _ in range(seq_size - 3):
        all_grads.append(shift_seq(all_grads[-1]))
    all_grads.append(last_grad)
    memory = context[0].reshape(-1, context.shape[3])
    full_cross_key = full_cross_kv[:, 0].reshape(-1, width)
    full_cross_value = full_cross_kv[:, 1].reshape(-1, width)
    memory_keys = matmul(memory, full_cross_key).astype(jnp.bfloat16)
    memory_values = matmul(memory, full_cross_value).astype(jnp.bfloat16)
    item_row = (row_segment == 1).astype(jnp.int32)[None, :]
    cross_mixed, cross_total, cross_exact = cross_forward(
        cross_queries, memory_keys, memory_values, item_row
    )
    second_sum = first_sum + matmul(cross_mixed, full_cross_out)
    norm_three, norm_three_back = jax.vjp(layer_norm, second_sum, gain_feed.astype(jnp.float32))
    norm_three = norm_three.astype(jnp.bfloat16)
    all_grads, norm_three = stage(all_grads, norm_three)

    held, feed_out, feed_dx, moving = None, {}, {}, None

    def run_block(k, held):
        *held, feed_out[k], feed_dx[k] = feed_block(
            norms[k], all_grads[k], unit_gate_up, unit_down, k, seq_size, held
        )
        return held

    norms = [norm_three, shift_seq(norm_three)]
    held = run_block(0, held)
    norms, all_grads, held, feed_out, feed_dx = stage(norms, all_grads, held, feed_out, feed_dx)
    for k in range(1, seq_size):
        if k + 1 < seq_size:
            norms.append(shift_seq(norms[-1]))
        arrived = None if k == 1 else shift_seq(moving)
        held = run_block(k, held)
        norms, arrived, held, feed_out, feed_dx = stage(norms, arrived, held, feed_out, feed_dx)
        moving = feed_dx[k] if k == 1 else add_low(arrived, feed_dx[k])
    activation, grad_gate, grad_up = held
    held = (grad_gate, grad_up, activation)
    arrived = shift_seq(moving)
    other_units = unit_products(held, norms, all_grads, 1)
    arrived, other_units, feed_out = stage(arrived, other_units, feed_out)
    other_units = swap_core(other_units)
    grad_norm_three = add_wide(arrived, feed_dx[0])

    def seq_blocks(first, second):
        blocks = jnp.concatenate([first.astype(jnp.bfloat16), second.astype(jnp.bfloat16)])
        return blocks.reshape(seq_size, part_rows, blocks.shape[1])

    feed_came = shift_seq(feed_out[seq_size // 2], -1)
    grad_output = cotangent.astype(jnp.float32) * valid_rows
    grad_second, grad_gain_feed = norm_three_back(grad_norm_three)
    grad_second = grad_second + grad_output
    second_low = grad_second.astype(jnp.bfloat16)
    grad_mixed = contract_cols(second_low, full_cross_out).astype(jnp.bfloat16)
    cross_out_own, cross_out_other = weight_products([cross_mixed], [second_low])
    cross_out_other = swap_core(cross_out_other)
    grad_cross_queries, grad_memory_keys, grad_memory_values = cross_backward(
        cross_queries,
        memory_keys,
        memory_values,
        grad_mixed,
        item_row,
        cross_total,
        cross_exact,
    )
    grad_norm_two = contract_cols(grad_cross_queries, full_cross_query)
    grad_first, grad_gain_cross = norm_two_back(grad_norm_two)
    grad_first = grad_first + grad_second
    first_low = grad_first.astype(jnp.bfloat16)
    grad_attended = contract_cols(first_low, full_out).astype(jnp.bfloat16)
    grad_attended = jnp.stack(
        [grad_attended[:, s * head_width : (s + 1) * head_width] for s in range(seq_size)]
    )
    products = weight_products([norm_two], [grad_cross_queries], 0, 3)
    products = weight_products([attended], [first_low], 1, 3, products)
    weight_own, weight_other = weight_products(
        [memory], [grad_memory_keys, grad_memory_values], 2, 3, products
    )
    cross_out_packed = pack_first(cross_out_own, cross_out_other)
    feed_came, cross_out_packed, grad_attended, weight_other, other_units = stage(
        feed_came, cross_out_packed, grad_attended, weight_other, other_units
    )

    head_grad = swap_seq(grad_attended)
    cross_out_came = send_first(cross_out_packed)
    weight_other = swap_core(weight_other)
    own_units = unit_products(held, norms, all_grads, 0, other_units)
    head_grad, cross_out_came, weight_other, own_units = stage(
        head_grad, cross_out_came, weight_other, own_units
    )

    weight_packed = pack_first(weight_own, weight_other)
    head_grad = head_grad.reshape(rows_dev * seq_size, head_width)
    head_grad = jnp.pad(head_grad, ((0, 0), (0, pairs * LANES - head_width)))
    feed_moving = reduce_middle(feed_came, feed_out), reduce_ahead(feed_out)
    head_grad, weight_packed, feed_moving = stage(head_grad, weight_packed, feed_moving)
    feed_moving = shift_seq(feed_moving[0], -1), shift_seq(feed_moving[1])
    weight_came = send_first(weight_packed)
    turned = self_backward(qkv, head_grad, log_total, exact, tables, segments, seq_size)
    norm_terms = low(contract_cols(turned, qkv_cols))
    norm_terms = [norm_terms[k * rows_dev : (k + 1) * rows_dev] for k in range(seq_size)]
    qkv_own, qkv_other = weight_products(norms_one, [turned])
    weight_came, norm_terms, qkv_own, qkv_other, feed_moving, cross_out_came, own_units = stage(
        weight_came, norm_terms, qkv_own, qkv_other, feed_moving, cross_out_came, own_units
    )
    cross_out_firsts = add_first(cross_out_came, cross_out_own, cross_out_other)

    moving = shift_seq(norm_terms[seq_size // 2], -1), shift_seq(reduce_ahead(norm_terms))
    weight_firsts = add_first(weight_came, weight_own, weight_other)
    weight_firsts = [jnp.concatenate(pair) for pair in zip(weight_firsts, cross_out_firsts)]
    weight_packed = pack_second(*weight_firsts)
    weight_came = send_second(weight_packed)
    qkv_other = swap_core(qkv_other)
    grad_gain_self = sum(
        jnp.sum(term.astype(jnp.float32) * norm.astype(jnp.float32), axis=0)
        for term, norm in zip(norm_terms, norms_one)
    ) / gain_self.astype(jnp.float32)
    gains = jnp.stack([grad_gain_self, grad_gain_cross, grad_gain_feed])
    gains = gains.reshape(-1, dp_size * seq_size, part_rows).transpose(1, 0, 2)
    gains = lax.all_to_all(gains, ("dp", "seq"), split_axis=0, concat_axis=0, tiled=True)
    moving, weight_came, qkv_own, qkv_other, gains = stage(
        moving, weight_came, qkv_own, qkv_other, gains
    )
    gains = jnp.sum(gains, axis=0)

    norm_came = shift_seq(reduce_middle(moving[0], norm_terms), -1)
    own_units = own_units.reshape(3, 2, y_size, 2, half_units, width)
    unit_came = send_first(pack_first(own_units))
    weight_seconds = add_second(weight_came, *weight_firsts)
    placed = swap_seq(
        jnp.stack(
            [
                seq_blocks(*(s[n] for s in weight_seconds))
                for n in (3, 0, 1)
            ],
            axis=1,
        )
    )
    kv_blocks = jnp.stack(
        [low(s[2]).reshape(seq_size, -1, width) for s in weight_seconds], axis=1
    )
    qkv_came = send_first(pack_first(qkv_own, qkv_other))
    qkv_firsts = add_first(qkv_came, qkv_own, qkv_other)
    qkv_seconds = add_second(send_second(pack_second(*qkv_firsts)), *qkv_firsts)
    later = jnp.concatenate(
        [
            kv_blocks.reshape(seq_size, part_rows, width),
            seq_blocks(*(s[0] for s in qkv_seconds)),
        ],
        axis=2,
    )
    output = low(
        second_sum + add_wide(feed_moving[0], feed_out[0]) + feed_moving[1].astype(jnp.float32)
    )
    norm_came, placed, unit_came, later = stage(norm_came, placed, unit_came, later)

    later = swap_seq(later)
    unit_firsts = add_first(unit_came, own_units)
    unit_came = send_second(pack_second(*unit_firsts))
    grad_norm_one = add_wide(norm_came, norm_terms[0]) + moving[1].astype(jnp.float32)
    grad_tokens_wide = norm_one_back(grad_norm_one)[0]
    grad_tokens = low(grad_tokens_wide + grad_first)
    grad_cross_out, grad_cross_query, grad_self_out = (
        jnp.sum(placed[:, n].astype(jnp.float32), axis=0) for n in range(3)
    )
    unit_grads = jnp.concatenate(add_second(unit_came, *unit_firsts), axis=1)
    grad_cross_kv = jnp.sum(later[:, :, :width].astype(jnp.float32), axis=0)
    kv_rows = part_rows // 2
    grad_qkv = (
        later[:, :, width:]
        .reshape(seq_size, part_rows, pairs, 3, LANES)
        .transpose(3, 1, 0, 2, 4)
        .reshape(3, part_rows, seq_size, pairs * LANES)[..., :head_width]
        .reshape(3, part_rows, width)
        .astype(jnp.float32)
    )
    return (
        output,
        grad_tokens,
        gains[0],
        gains[1],
        gains[2],
        grad_qkv[0],
        grad_qkv[1],
        grad_qkv[2],
        grad_self_out,
        grad_cross_query,
        grad_cross_kv[:kv_rows],
        grad_cross_kv[kv_rows:],
        grad_cross_out,
        unit_grads[0],
        unit_grads[1],
        unit_grads[2],
    )


def solution(mesh):
    placed = (
        P(("dp", "seq"), None),
        P("dp", None, None, None),
        P("dp", None),
        P(),
        P(),
        P(),
        P(("dp", "seq"), None),
        P(("dp", "seq"), None),
        P(("dp", "seq"), None),
        P(("dp", "seq"), None),
        P(("dp", "seq"), None),
        P(("dp", "seq"), None),
        P(("dp", "seq"), None),
        P(("dp", "seq"), None),
        P(("dp", "seq"), None),
        P(("dp", "seq"), None),
        P(("dp", "seq"), None),
        P(("dp", "seq"), None),
    )
    return jax.shard_map(
        local,
        mesh=mesh,
        in_specs=placed,
        out_specs=(
            P(("dp", "seq"), None),
            P(("dp", "seq"), None),
            P(("dp", "seq")),
            P(("dp", "seq")),
            P(("dp", "seq")),
            P(("dp", "seq"), None),
            P(("dp", "seq"), None),
            P(("dp", "seq"), None),
            P(("dp", "seq"), None),
            P(("dp", "seq"), None),
            P(("dp", "seq"), None),
            P(("dp", "seq"), None),
            P(("dp", "seq"), None),
            P(("dp", "seq"), None),
            P(("dp", "seq"), None),
            P(("dp", "seq"), None),
        ),
        check_vma=False,
    )
```
